1024 devices in a mesh: gx: 16 (over z_hi, x), gy: 16 (over z_lo, core), gz: 4 (over y).
Axes of the slice: x: 4, y: 4, z: 32 (z_hi: 4, z_lo: 8; z = z_hi * 8 + z_lo), core: 2. Of those that a mesh axis runs over, the one named last changes fastest.
Arguments:
- phase_label: int32 [128, 128, 1024], P('gx', 'gy', 'gz'), may hold values from 0 to 2
- concentration: float32 [128, 128, 1024], P('gx', 'gy', 'gz'), may hold values from 0.3 to 3
- phase_factor: float32 [3], replicated, may hold values from 0.05 to 1
- potential: float32 [3, 128, 128, 1024], P(None, 'gx', 'gy', 'gz'), may hold values from -6 to 6
- source: float32 [3, 128, 128, 1024], P(None, 'gx', 'gy', 'gz'), may hold values from -6 to 6
Outputs:
- level_correction: float32 [3, 64, 64, 512], P(None, 'gx', 'gy', 'gz')
- coarse_correction: float32 [3, 16, 16, 128], P(None, 'gx', 'gy')
The draws below stay inside these ranges and needn't reach their ends.
All inputs are finite; a program needn't handle non-finite values.
Results may differ from the reference program's by a relative error of at most 0.00002.
Values sent between devices are 32-bit elements; how exact they have to be, the bound alone decides.
A program may use at most 32 MiB of HBM per device.

```python
import math
import jax
import jax.numpy as jnp

FIELDS = 3
SWEEPS = 4
NX = 128
NY = 128
NZ = 1024


def place_ends(entries, rng, smallest, top_value):
    longest = entries.shape.index(max(entries.shape))
    spots = []
    for shift in (0, 1):
        where = [jax.random.randint(jax.random.fold_in(rng, axis), (), 0, length) for axis, length in enumerate(entries.shape)]
        where[longest] = (where[longest] + shift) % entries.shape[longest]
        spots.append(tuple(where))
    return entries.at[spots[0]].set(smallest).at[spots[1]].set(top_value)


def block_scale(rng, dims, pieces, least, high):
    factor_of = 1.0
    for dim, blocks in pieces:
        heights = jax.random.uniform(jax.random.fold_in(jax.random.fold_in(rng, 6), dim), (blocks,), jnp.float32, least / len(pieces), high / len(pieces))
        factor_of = factor_of * jnp.repeat(jnp.exp(heights), dims[dim] // blocks).reshape((-1,) + (1,) * (len(dims) - 1 - dim))
    return factor_of


def gaussian(key, shape, deviation, most, cuts=(), kind=jnp.bfloat16):
    factor_of = block_scale(key, shape, cuts, -0.22, 0.18) if cuts else 1.0
    drawn = jax.random.normal(key, shape, jnp.float32) * deviation * factor_of
    return jnp.minimum(jnp.maximum(drawn, -most), most).astype(kind)


def setup_inputs(seed: int = 0) -> dict:
    key_of = jax.random.split(jax.random.key(seed), 6)
    phase_label = place_ends(jax.random.randint(key_of[0], (NX, NY, NZ), 0, 3), jax.random.fold_in(key_of[0], 1), 0, 2).astype(jnp.int32)
    concentration = jnp.clip(jnp.exp(math.log(3.0) - 2.3025851 * jax.random.uniform(key_of[1], (NX, NY, NZ), jnp.float32) ** block_scale(key_of[1], (NX, NY, NZ), ((0, 16), (1, 16), (2, 4)), -0.2, 0.2)), 0.3, 3.0)
    phase_factor = jnp.clip(jnp.exp(jax.random.uniform(key_of[2], (3,), jnp.float32, math.log(0.05), math.log(1.0))), 0.05, 1.0)
    potential = gaussian(key_of[3], (FIELDS, NX, NY, NZ), 1.0, 6.0, ((1, 16), (2, 16), (3, 4)), jnp.float32)
    source = gaussian(key_of[4], (FIELDS, NX, NY, NZ), 1.0, 6.0, ((1, 16), (2, 16), (3, 4)), jnp.float32)
    return dict(phase_label=phase_label, concentration=concentration, phase_factor=phase_factor, potential=potential, source=source)


mass_term = 0.05
damping = 0.7
decay_rate = 0.3


def face_stencil(conduct):
    padded = jnp.pad(conduct, 1)
    center = padded[1:-1, 1:-1, 1:-1]

    def harmonic(other):
        return 2.0 * center * other / (center + other)

    parts = [jnp.full(center.shape, mass_term, jnp.float32),
             harmonic(padded[:-2, 1:-1, 1:-1]), harmonic(padded[2:, 1:-1, 1:-1]),
             harmonic(padded[1:-1, :-2, 1:-1]), harmonic(padded[1:-1, 2:, 1:-1]),
             harmonic(padded[1:-1, 1:-1, :-2]), harmonic(padded[1:-1, 1:-1, 2:])]
    return jnp.stack(parts)


def apply_stencil(stencil, values):
    padded = jnp.pad(values, ((0, 0), (1, 1), (1, 1), (1, 1)))
    total = stencil[0] * values
    total = total + stencil[1] * (values - padded[:, :-2, 1:-1, 1:-1])
    total = total + stencil[2] * (values - padded[:, 2:, 1:-1, 1:-1])
    total = total + stencil[3] * (values - padded[:, 1:-1, :-2, 1:-1])
    total = total + stencil[4] * (values - padded[:, 1:-1, 2:, 1:-1])
    total = total + stencil[5] * (values - padded[:, 1:-1, 1:-1, :-2])
    total = total + stencil[6] * (values - padded[:, 1:-1, 1:-1, 2:])
    return total


def blocks(values):
    lead, sx, sy, sz = values.shape
    return values.reshape(lead, sx // 2, 2, sy // 2, 2, sz // 2, 2)


def restrict(values):
    return jnp.sum(blocks(values), axis=(2, 4, 6))


def galerkin(stencil):
    split = blocks(stencil)
    parts = [jnp.sum(split[0], axis=(1, 3, 5)),
             jnp.sum(split[1][:, 0], axis=(2, 4)), jnp.sum(split[2][:, 1], axis=(2, 4)),
             jnp.sum(split[3][:, :, :, 0], axis=(1, 4)), jnp.sum(split[4][:, :, :, 1], axis=(1, 4)),
             jnp.sum(split[5][:, :, :, :, :, 0], axis=(1, 3)), jnp.sum(split[6][:, :, :, :, :, 1], axis=(1, 3))]
    return jnp.stack(parts)


def smooth(residual, stencil):
    diagonal = jnp.sum(stencil, axis=0)
    correction = damping * residual / diagonal
    correction = correction + damping * (residual - apply_stencil(stencil, correction)) / diagonal
    return correction, residual - apply_stencil(stencil, correction)


def reference(phase_label, concentration, phase_factor, potential, source):
    lookup = jnp.zeros(phase_label.shape, jnp.float32)
    for index in range(3):
        lookup = lookup + jnp.where(phase_label == index, phase_factor[index], 0.0)
    conduct = lookup * concentration * jnp.exp(-decay_rate * concentration)
    stencil0 = face_stencil(conduct)
    first = restrict(source - apply_stencil(stencil0, potential))
    stencil1 = galerkin(stencil0)
    level_correction, left1 = smooth(first, stencil1)
    stencil2 = galerkin(stencil1)
    second, left2 = smooth(restrict(left1), stencil2)
    stencil3 = galerkin(stencil2)
    third = restrict(left2)
    diagonal = jnp.sum(stencil3, axis=0)
    correction = damping * third / diagonal
    for sweep in range(SWEEPS - 1):
        correction = correction + damping * (third - apply_stencil(stencil3, correction)) / diagonal
    return level_correction, correction
```

```python
import functools

import jax
import jax.numpy as jnp
from jax import lax
from jax.experimental import pallas as pl
from jax.experimental.pallas import tpu as pltpu
from jax.sharding import PartitionSpec as P

MESH = pl.DeviceIdType.MESH
FIELDS = 3
MASS = 0.05
DAMPING = 0.7
DECAY = 0.3
XREACH = 4
YREACH = 3
WIDE = 256


def rs(x, k):
    k %= x.shape[-2]
    return pltpu.roll(x, k, x.ndim - 2) if k else x


def rl(x, k):
    k %= x.shape[-1]
    return pltpu.roll(x, k, x.ndim - 1) if k else x


def harmonic(a, b):
    return 2.0 * a * b / (a + b)


def safe(d):
    return jnp.where(d > 0.0, d, 1.0)


def kernel(names, sizes, phase, conc, pot, src, factor, lev_out, coarse_out, *scratch):
    (ph, co, po, so, in_sem, ys1, yr1, zs1, zr1, xs1, xr1, xs2, xr2, ys3, yr3, zs3, zr3, ys4, yr4, zs4, zr4,
     qb, ys6, yr6, zs6, zr6, ys7, yr7, zs7, zr7, gb, ssem, rsem) = scratch
    ax, ay, az = names
    nx, ny, nz = sizes
    gx, gy, gz = (lax.axis_index(a) for a in names)
    here = {ax: gx, ay: gy, az: gz}
    count = {ax: nx, ay: ny, az: nz}

    def has(axis, step):
        at = here[axis] + step
        return (at >= 0) & (at < count[axis])

    barrier = pltpu.get_barrier_semaphore()
    greet = [(ax, d) for d in range(-XREACH, XREACH + 1) if d] + [(ay, d) for d in range(-YREACH, YREACH + 1) if d]
    met = jnp.int32(nz - 1)
    for axis, d in greet:
        met = met + has(axis, d).astype(jnp.int32)

        @pl.when(has(axis, d))
        def _(axis=axis, d=d):
            pl.semaphore_signal(barrier, inc=1, device_id={axis: here[axis] + d}, device_id_type=MESH)

    for rel in range(1, nz):
        pl.semaphore_signal(barrier, inc=1, device_id={az: lax.rem(gz + rel, nz)}, device_id_type=MESH)

    loads = [pltpu.make_async_copy(a, b, in_sem.at[i]) for i, (a, b) in enumerate(((phase, ph), (conc, co), (pot, po), (src, so)))]
    for load in loads:
        load.start()

    for axis, bufs in ((ax, (xr1, xr2)), (ay, (yr1, yr3, yr4, yr6, yr7)), (az, (zr1, zr3, zr4, zr6, zr7))):
        for side, d in ((0, -1), (1, 1)):

            @pl.when(jnp.logical_not(has(axis, d)))
            def _(bufs=bufs, side=side):
                for buf in bufs:
                    buf[side] = jnp.zeros(buf.shape[1:], jnp.float32)

    for axis, buf, reach in ((ax, qb, XREACH), (ay, gb, YREACH)):
        for d in range(-reach, reach + 1):
            if d:

                @pl.when(jnp.logical_not(has(axis, d)))
                def _(buf=buf, slot=reach + d):
                    buf[slot] = jnp.zeros(buf.shape[1:], jnp.float32)

    pending = []
    used = [0]

    def copy(k, a, b, target):
        return pltpu.make_async_remote_copy(
            src_ref=a, dst_ref=b, send_sem=ssem.at[k], recv_sem=rsem.at[k], device_id=target, device_id_type=MESH
        )

    def push(k, a, b, axis, d):
        pending.append((k, a, b, axis, d))

        @pl.when(has(axis, d))
        def _():
            copy(k, a, b, {axis: here[axis] + d}).start()

    def take(k, b, axis, d):
        @pl.when(has(axis, d))
        def _():
            copy(k, b, b, {axis: here[axis] + d}).wait_recv()

    def exchange(axis, sent, got):
        k = used[0]
        used[0] += 2
        push(k, sent.at[0], got.at[1], axis, -1)
        push(k + 1, sent.at[1], got.at[0], axis, 1)

        def wait():
            take(k, got.at[1], axis, 1)
            take(k + 1, got.at[0], axis, -1)

        return wait

    sub = lax.broadcasted_iota(jnp.int32, (8, WIDE), 0)
    lane = lax.broadcasted_iota(jnp.int32, (8, WIDE), 1)
    lane1 = lax.broadcasted_iota(jnp.int32, (8, 128), 1)

    def zpack(sent, slabs, stride, unit):
        low = high = jnp.zeros((8, 128), jnp.float32)
        for k, s in enumerate(slabs):
            mine = (lane1 >= unit * k) & (lane1 < unit * (k + 1))
            low = jnp.where(mine, rl(s[:, :128], unit * k), low)
            high = jnp.where(mine, rl(s[:, 128:], unit * k - (128 - stride)), high)
        sent[0] = low
        sent[1] = high

    def zhalo(low, high, k, stride, unit):
        return jnp.concatenate([rl(low, -unit * k), rl(high, 128 - stride - unit * k)], axis=1)

    def ypack_rows(sent, slabs, stride):
        for g in range(sent.shape[1]):
            low = high = jnp.zeros((8, WIDE), jnp.float32)
            for j, s in enumerate(slabs[8 * g : 8 * g + 8]):
                low = jnp.where(sub == j, rs(s, j), low)
                high = jnp.where(sub == j, rs(s, j - (8 - stride)), high)
            sent[0, g] = low
            sent[1, g] = high

    def row(got, side, k):
        return jnp.broadcast_to(got[side, k // 8, k % 8 : k % 8 + 1, :], (8, WIDE))

    loads[0].wait()
    loads[1].wait()
    loads[2].wait()
    phase_v = ph[...]
    conc_v = co[...]
    lookup = jnp.zeros(phase_v.shape, jnp.float32)
    for i in range(3):
        lookup = lookup + jnp.where(phase_v == i, factor[i], 0.0)
    conduct = lookup * conc_v * jnp.exp(-DECAY * conc_v)
    fine = [jnp.stack([conduct[x]] + [po[f, x] for f in range(FIELDS)]) for x in range(8)]
    ypack_rows(ys1, [fine[x][a] for a in range(4) for x in range(8)], 1)
    zpack(zs1, [fine[x][a] for a in range(4) for x in range(8)], 1, 1)
    xs1[0] = fine[0]
    xs1[1] = fine[7]
    loads[3].wait()

    pl.semaphore_wait(barrier, met)

    wait_y1 = exchange(ay, ys1, yr1)
    wait_z1 = exchange(az, zs1, zr1)
    wait_x1 = exchange(ax, xs1, xr1)

    def rest(c):
        return c[0], c[1:]

    def flux(c, v, other):
        face = harmonic(c, other[0])
        return face, face * (v - other[1:])

    inner = []
    for i in range(3):
        a, b = fine[2 * i + 1], fine[2 * i + 2]
        inner.append(flux(a[0], a[1:], b))

    wait_y1()
    wait_z1()
    zlow, zhigh = zr1[0], zr1[1]
    part, ypart, zpart = [], [], []
    for x in range(8):
        c, v = rest(fine[x])
        near = jnp.where(sub % 2 == 0, rs(fine[x], 1), rs(fine[x], -1))
        edge = jnp.stack([jnp.where(sub == 0, row(yr1, 0, a * 8 + x), row(yr1, 1, a * 8 + x)) for a in range(4)])
        near = jnp.where((sub == 0) | (sub == 7), edge, near)
        sy, fy = flux(c, v, near)
        near = jnp.where(lane % 2 == 0, rl(fine[x], 1), rl(fine[x], -1))
        edge = jnp.stack([zhalo(zlow, zhigh, a * 8 + x, 1, 1) for a in range(4)])
        near = jnp.where((lane == 0) | (lane == WIDE - 1), edge, near)
        sz, fz = flux(c, v, near)
        source = jnp.stack([so[f, x] for f in range(FIELDS)])
        part.append(source - MASS * v - fy - fz)
        ypart.append(sy)
        zpart.append(sz)

    def fold(t, stride):
        t = t + rl(t, -stride)
        return t + rs(t, -stride)

    mass1 = MASS * 8.0
    r1, ylo, yhi, zlo, zhi, diag, sx = {}, {}, {}, {}, {}, {}, {}
    for i in range(3):
        sx[i] = fold(inner[i][0], 1)
    for i in range(4):
        t = part[2 * i] + part[2 * i + 1]
        if i < 3:
            t = t - inner[i][1]
        if i > 0:
            t = t + inner[i - 1][1]
        r1[i] = fold(t, 1)
        a = ypart[2 * i] + ypart[2 * i + 1]
        a = a + rl(a, -1)
        ylo[i], yhi[i] = a, rs(a, -1)
        b = zpart[2 * i] + zpart[2 * i + 1]
        b = b + rs(b, -1)
        zlo[i], zhi[i] = b, rl(b, -1)
        d = mass1 + ylo[i] + yhi[i] + zlo[i] + zhi[i]
        if i < 3:
            d = d + sx[i]
        if i > 0:
            d = d + sx[i - 1]
        diag[i] = d

    e0, weight = {}, {}
    for i in (1, 2):
        weight[i] = DAMPING / safe(diag[i])
        e0[i] = weight[i] * r1[i]

    q0 = sub % 2 == 0
    p0 = lane % 2 == 0

    def merge4(a, b, c, d):
        return jnp.where(q0, jnp.where(p0, a, rl(b, 1)), jnp.where(p0, rs(c, 1), rs(rl(d, 1), 1)))

    def split4(m):
        low = rs(m, -1)
        return m, rl(m, -1), low, rl(low, -1)

    for side, (edge, next_to, face) in enumerate(((0, 1, 0), (3, 2, 2))):
        xs2[side, 0] = merge4(e0[next_to][0], e0[next_to][1], e0[next_to][2], diag[edge])
        xs2[side, 1] = merge4(r1[edge][0], r1[edge][1], r1[edge][2], sx[face])
        xs2[side, 2] = merge4(ylo[edge], yhi[edge], zlo[edge], zhi[edge])
    wait_x2 = exchange(ax, xs2, xr2)

    wait_x1()
    border = {}
    for side, x in ((0, 0), (1, 7)):
        face, out = flux(fine[x][0], fine[x][1:], xr1[side])
        border[side] = (fold(face, 1), fold(out, 1))
    wait_x2()
    for side, edge, out, far, own_face, far_face in ((0, 0, -1, -2, -1, -2), (1, 3, 4, 5, 3, 4)):
        face, through = border[side]
        a = split4(xr2[side, 0])
        b = split4(xr2[side, 1])
        c = split4(xr2[side, 2])
        e0[far] = jnp.stack(a[:3])
        r1[out] = jnp.stack(b[:3]) + through
        r1[edge] = r1[edge] - through
        sx[far_face] = b[3]
        sx[own_face] = face
        ylo[out], yhi[out], zlo[out], zhi[out] = c
        diag[out] = a[3] + face
        diag[edge] = diag[edge] + face
        for i in (out, edge):
            weight[i] = DAMPING / safe(diag[i])
            e0[i] = weight[i] * r1[i]

    def halos(got_y, got_z, layers, low, high, i):
        base = layers.index(i) * FIELDS
        ylow = jnp.stack([row(got_y, 0, base + f) for f in range(FIELDS)])
        yhigh = jnp.stack([row(got_y, 1, base + f) for f in range(FIELDS)])
        zedge = jnp.stack([zhalo(low, high, base + f, 2, 1) for f in range(FIELDS)])
        return ylow, yhigh, zedge

    six = [-1, 0, 1, 2, 3, 4]
    slabs = [e0[i][f] for i in six for f in range(FIELDS)]
    ypack_rows(ys3, slabs, 2)
    wait_y = exchange(ay, ys3, yr3)
    zpack(zs3, slabs, 2, 1)
    wait_z = exchange(az, zs3, zr3)
    wait_y()
    wait_z()
    low, high = zr3[0], zr3[1]
    e1 = {}
    for i in six:
        e = e0[i]
        ylow, yhigh, zedge = halos(yr3, zr3, six, low, high, i)
        total = mass1 * e + sx[i - 1] * (e - e0[i - 1]) + sx[i] * (e - e0[i + 1])
        total = total + ylo[i] * (e - jnp.where(sub < 2, ylow, rs(e, 2)))
        total = total + yhi[i] * (e - jnp.where(sub >= 6, yhigh, rs(e, -2)))
        total = total + zlo[i] * (e - jnp.where(lane < 2, zedge, rl(e, 2)))
        total = total + zhi[i] * (e - jnp.where(lane >= WIDE - 2, zedge, rl(e, -2)))
        e1[i] = e + weight[i] * (r1[i] - total)

    four = [0, 1, 2, 3]
    slabs = [e1[i][f] for i in four for f in range(FIELDS)]
    ypack_rows(ys4, slabs, 2)
    wait_y = exchange(ay, ys4, yr4)
    zpack(zs4, slabs, 2, 1)
    wait_z = exchange(az, zs4, zr4)

    mass2 = mass1 * 8.0
    yfirst = sub % 4 < 2
    zfirst = lane % 4 < 2
    yout = {i: jnp.where(yfirst, ylo[i], yhi[i]) for i in four}
    zout = {i: jnp.where(zfirst, zlo[i], zhi[i]) for i in four}
    sx2 = {-1: fold(sx[-1], 2), 0: fold(sx[1], 2), 1: fold(sx[3], 2)}
    ylo2, yhi2, zlo2, zhi2, diag2 = {}, {}, {}, {}, {}
    for i in range(2):
        a = yout[2 * i] + yout[2 * i + 1]
        a = a + rl(a, -2)
        ylo2[i], yhi2[i] = a, rs(a, -2)
        b = zout[2 * i] + zout[2 * i + 1]
        b = b + rs(b, -2)
        zlo2[i], zhi2[i] = b, rl(b, -2)
        diag2[i] = mass2 + sx2[i - 1] + sx2[i] + ylo2[i] + yhi2[i] + zlo2[i] + zhi2[i]

    wait_y()
    wait_z()
    low, high = zr4[0], zr4[1]
    left = {}
    for i in four:
        e = e1[i]
        ylow, yhigh, zedge = halos(yr4, zr4, four, low, high, i)
        across = i - 1 if i % 2 == 0 else i + 1
        near_y = jnp.where(yfirst, jnp.where(sub < 2, ylow, rs(e, 2)), jnp.where(sub >= 6, yhigh, rs(e, -2)))
        near_z = jnp.where(zfirst, rl(e, 2), rl(e, -2))
        near_z = jnp.where((lane < 2) | (lane >= WIDE - 2), zedge, near_z)
        total = mass1 * e + sx[min(i, across)] * (e - e1[across])
        total = total + yout[i] * (e - near_y) + zout[i] * (e - near_z)
        left[i] = r1[i] - total
    r2 = {i: fold(left[2 * i] + left[2 * i + 1], 2) for i in range(2)}

    q4 = sub % 4
    p4 = lane % 4

    def by(which, a, b, c, d):
        return jnp.where(which < 2, jnp.where(which == 0, a, b), jnp.where(which == 2, c, d))

    def rows4(a, b, c, d):
        return by(q4, a, rs(b, 1), rs(c, 2), rs(d, 3))

    block = by(
        p4,
        rows4(r2[0][0], r2[0][1], r2[0][2], diag2[0]),
        rl(rows4(r2[1][0], r2[1][1], r2[1][2], diag2[1]), 1),
        rl(rows4(sx2[0], yhi2[0], zhi2[0], zlo2[0]), 2),
        rl(rows4(sx2[1], yhi2[1], zhi2[1], zlo2[1]), 3),
    )
    qb[XREACH] = block
    first = used[0]
    steps = [d for d in range(-XREACH, XREACH + 1) if d]
    used[0] += len(steps)
    for k, d in enumerate(steps):
        push(first + k, qb.at[XREACH], qb.at[XREACH - d], ax, d)

    packed = jnp.concatenate([merge4(*(e1[i][f] for i in four)) for f in range(FIELDS)], axis=0)
    r = lax.broadcasted_iota(jnp.int32, (WIDE, WIDE), 0)
    c = lax.broadcasted_iota(jnp.int32, (WIDE, WIDE), 1)
    order = jnp.where(c == (r % 2) * 128 + r // 2, 1.0, 0.0)
    dense = jnp.dot(packed, order, precision=lax.Precision.HIGHEST, preferred_element_type=jnp.float32)
    for f in range(FIELDS):
        for y in range(4):
            for q in range(2):
                for p in range(2):
                    k = f * 8 + 2 * y + q
                    lev_out[f, 2 * q + p, y : y + 1, :] = dense[k : k + 1, 128 * p : 128 * p + 128]

    for k, d in enumerate(steps):
        take(first + k, qb.at[XREACH - d], ax, -d)

    n2 = 2 * XREACH + 1
    q = qb[...]

    def spread(x, item):
        return jnp.where(q4 == 0, rs(x, -item), jnp.where(q4 == 1, rs(x, 1 - item), rs(x, 2 - item)))

    layer0 = p4 == 0
    weight2 = DAMPING / safe(spread(q, 3))
    coef = rl(q, -2)
    xhi, yhi_, zhi_, zlo_ = (spread(coef, item) for item in range(4))
    e = weight2 * q

    def below(x):
        return jnp.concatenate([x[:1], x[:-1]], axis=0)

    def above(x):
        return jnp.concatenate([x[1:], x[-1:]], axis=0)

    def next_x(x):
        return jnp.where(layer0, rl(x, -1), above(rl(x, 1)))

    def last_x(x):
        return jnp.where(layer0, below(rl(x, -1)), rl(x, 1))

    def ypack_halves(sent, x):
        for g in range(sent.shape[1]):
            a, b = x[2 * g], x[min(2 * g + 1, x.shape[0] - 1)]
            sent[0, g] = jnp.where(sub < 4, a, rs(b, 4))
            sent[1, g] = jnp.where(sub < 4, rs(a, 4), b)

    def yedges(got, n):
        out = []
        for d in range(n):
            low, high = got[0, d // 2], got[1, d // 2]
            if d % 2 == 0:
                out.append(jnp.where(sub < 4, low, rs(high, 4)))
            else:
                out.append(jnp.where(sub < 4, rs(low, 4), high))
        return jnp.stack(out)

    def zedges(got, n):
        low, high = got[0], got[1]
        return jnp.stack([zhalo(low, high, d, 4, 4) for d in range(n)])

    ypack_halves(ys6, jnp.where(q4 == 3, rs(coef, 2), e))
    wait_y = exchange(ay, ys6, yr6)
    zpack(zs6, [e[d] for d in range(n2)], 4, 4)
    wait_z = exchange(az, zs6, zr6)
    xlo = last_x(xhi)
    near = xlo * (e - last_x(e)) + xhi * (e - next_x(e)) + mass2 * e
    wait_y()
    wait_z()
    edge = yedges(yr6, n2)
    zedge = zedges(zr6, n2)
    ylo_ = jnp.where(sub < 4, spread(edge, 3), rs(yhi_, 4))
    other = rs(e, 4)
    total = near + ylo_ * (e - jnp.where(sub < 4, edge, other)) + yhi_ * (e - jnp.where(sub < 4, other, edge))
    total = total + zlo_ * (e - jnp.where(lane < 4, zedge, rl(e, 4)))
    total = total + zhi_ * (e - jnp.where(lane >= WIDE - 4, zedge, rl(e, -4)))
    e = e + weight2 * (q - total)

    n3 = n2 - 2
    ypack_halves(ys7, e[1:-1])
    wait_y = exchange(ay, ys7, yr7)
    zpack(zs7, [e[d] for d in range(1, n2 - 1)], 4, 4)
    wait_z = exchange(az, zs7, zr7)

    mass3 = mass2 * 8.0
    zfirst = lane % 8 < 4
    xout = jnp.where(layer0, xlo, xhi)[1:-1]
    yout = jnp.where(sub < 4, ylo_, yhi_)[1:-1]
    zout = jnp.where(zfirst, zlo_, zhi_)[1:-1]
    a = xout + rs(xout, 4)
    a = a + rl(a, -4)
    xlo3, xhi3 = a, rl(a, -1)
    a = yout + rl(yout, -1)
    a = a + rl(a, -4)
    ylo3, yhi3 = a, rs(a, 4)
    a = zout + rl(zout, -1)
    a = a + rs(a, 4)
    zlo3, zhi3 = a, rl(a, -4)
    diag3 = mass3 + xlo3 + xhi3 + ylo3 + yhi3 + zlo3 + zhi3
    near_x = jnp.where(layer0, last_x(e), next_x(e))[1:-1]
    e = e[1:-1]
    near_z = jnp.where(zfirst, rl(e, 4), rl(e, -4))
    partial = q[1:-1] - mass2 * e - xout * (e - near_x)
    coefs = jnp.where(sub == 3, rs(diag3, 3), jnp.where(sub == 4, rs(xhi3, 4), jnp.where(sub == 5, rs(yhi3, 5), rs(zhi3, 6))))
    wait_y()
    wait_z()
    edge = yedges(yr7, n3)
    zedge = zedges(zr7, n3)
    near_z = jnp.where((lane < 4) | (lane >= WIDE - 4), zedge, near_z)
    t = partial - yout * (e - edge) - zout * (e - near_z)
    t = t + rl(t, -1)
    t = t + rs(t, 4)
    t = t + rl(t, -4)
    t = jnp.where(sub < 3, t, coefs)
    block = jnp.zeros((8, WIDE), jnp.float32)
    for l in range(n3):
        block = jnp.where((lane % 8 == l) & (sub < 7), rl(t[l], l), block)

    def column(at):
        return gb.at[YREACH, :, pl.ds(pl.multiple_of(at * WIDE, WIDE), WIDE)]

    gb[YREACH, :, pl.ds(pl.multiple_of(gz * WIDE, WIDE), WIDE)] = block
    first = used[0]
    used[0] += nz - 1
    along = []
    for rel in range(1, nz):
        c = copy(first + rel - 1, column(gz), column(gz), {az: lax.rem(gz + rel, nz)})
        c.start()
        along.append(c)
    for rel in range(1, nz):
        back = lax.rem(gz + nz - rel, nz)
        copy(first + rel - 1, column(back), column(back), {az: back}).wait_recv()
    first = used[0]
    steps = [d for d in range(-YREACH, YREACH + 1) if d]
    used[0] += len(steps)
    for k, d in enumerate(steps):
        push(first + k, gb.at[YREACH], gb.at[YREACH - d], ay, d)
    for k, d in enumerate(steps):
        take(first + k, gb.at[YREACH - d], ay, -d)

    full = (8, WIDE * nz)
    n = 2 * YREACH + 1

    def coefficient(j, item):
        return jnp.broadcast_to(gb[j, item : item + 1, :], full)

    r3 = [gb[j] for j in range(n)]
    w3 = [DAMPING / safe(coefficient(j, 3)) for j in range(n)]
    e = {j: w3[j] * r3[j] for j in range(n)}
    xhi = {j: coefficient(j, 4) for j in range(1, n - 1)}
    yhi = {j: coefficient(j, 5) for j in range(n - 1)}
    zhi = {j: coefficient(j, 6) for j in range(1, n - 1)}
    xlo = {j: rl(xhi[j], 1) for j in xhi}
    zlo = {j: rl(zhi[j], 8) for j in zhi}
    for sweep in range(1, YREACH + 1):
        new = {}
        for j in range(sweep, n - sweep):
            v = e[j]
            total = mass3 * v + xlo[j] * (v - rl(v, 1)) + xhi[j] * (v - rl(v, -1))
            total = total + yhi[j - 1] * (v - e[j - 1]) + yhi[j] * (v - e[j + 1])
            total = total + zlo[j] * (v - rl(v, 8)) + zhi[j] * (v - rl(v, -8))
            new[j] = v + w3[j] * (r3[j] - total)
        e = new
    own = e[YREACH]
    tile = jnp.zeros((8, 128), jnp.float32)
    for t in range(2 * nz):
        tile = jnp.where(lane1 % 8 == t, rl(own[:, 128 * t : 128 * t + 128], t - XREACH + 1), tile)
    r = lax.broadcasted_iota(jnp.int32, (128, 32 * nz), 0)
    c = lax.broadcasted_iota(jnp.int32, (128, 32 * nz), 1)
    order = jnp.where(c == (r % 8) * 16 + r // 8, 1.0, 0.0)
    dense = jnp.dot(tile, order, precision=lax.Precision.HIGHEST, preferred_element_type=jnp.float32)
    for f in range(FIELDS):
        coarse_out[f, 0, :, :] = dense[f : f + 1, :]

    for k, a, b, axis, d in pending:

        @pl.when(has(axis, d))
        def _(k=k, a=a, b=b, axis=axis, d=d):
            copy(k, a, b, {axis: here[axis] + d}).wait_send()

    for c in along:
        c.wait_send()


def solution(mesh):
    names = mesh.axis_names
    sizes = tuple(mesh.shape[a] for a in names)
    nz = sizes[2]
    f32 = jnp.float32

    def both(*shape):
        return [pltpu.VMEM((2, *shape), f32)] * 2

    scratch = [
        pltpu.VMEM((8, 8, WIDE), jnp.int32),
        pltpu.VMEM((8, 8, WIDE), f32),
        pltpu.VMEM((FIELDS, 8, 8, WIDE), f32),
        pltpu.VMEM((FIELDS, 8, 8, WIDE), f32),
        pltpu.SemaphoreType.DMA((4,)),
        *both(4, 8, WIDE), *both(8, 128), *both(4, 8, WIDE), *both(3, 8, WIDE),
        *both(3, 8, WIDE), *both(8, 128),
        *both(2, 8, WIDE), *both(8, 128),
        pltpu.VMEM((2 * XREACH + 1, 8, WIDE), f32),
        *both(5, 8, WIDE), *both(8, 128),
        *both(4, 8, WIDE), *both(8, 128),
        pltpu.VMEM((2 * YREACH + 1, 8, WIDE * nz), f32),
    ]
    sems = 2 * 4 + 4 + 4 + 2 * XREACH + 4 + 4 + (nz - 1) + 2 * YREACH
    scratch += [pltpu.SemaphoreType.DMA((sems,)), pltpu.SemaphoreType.DMA((sems,))]

    def local(phase_label, concentration, phase_factor, potential, source):
        return pl.pallas_call(
            functools.partial(kernel, names, sizes),
            out_shape=(
                jax.ShapeDtypeStruct((FIELDS, 4, 4, 128), f32),
                jax.ShapeDtypeStruct((FIELDS, 1, 1, 32 * nz), f32),
            ),
            in_specs=[pl.BlockSpec(memory_space=pl.ANY)] * 4 + [pl.BlockSpec(memory_space=pltpu.SMEM)],
            out_specs=(pl.BlockSpec(memory_space=pltpu.VMEM), pl.BlockSpec(memory_space=pltpu.VMEM)),
            scratch_shapes=scratch,
            compiler_params=pltpu.CompilerParams(collective_id=0, has_side_effects=True, vmem_limit_bytes=32 << 20),
        )(phase_label, concentration, potential, source, phase_factor)

    return jax.shard_map(
        local,
        mesh=mesh,
        in_specs=(P(*names), P(*names), P(), P(None, *names), P(None, *names)),
        out_specs=(P(None, *names), P(None, names[0], names[1], None)),
        check_vma=False,
    )
```

```python
import functools

import jax
import jax.numpy as jnp
from jax import lax
from jax.experimental import pallas as pl
from jax.experimental.pallas import tpu as pltpu
from jax.sharding import PartitionSpec as P

MESH = pl.DeviceIdType.MESH
FIELDS = 3
MASS = 0.05
DAMPING = 0.7
DECAY = 0.3
XREACH = 4
YREACH = 3
WIDE = 256
XROW = 4


def rs(x, k):
    k %= x.shape[-2]
    return pltpu.roll(x, k, x.ndim - 2) if k else x


def rl(x, k):
    k %= x.shape[-1]
    return pltpu.roll(x, k, x.ndim - 1) if k else x


def harmonic(a, b):
    return 2.0 * a * b / (a + b)


def safe(d):
    return jnp.where(d > 0.0, d, 1.0)


def kernel(names, sizes, phase, conc, pot, src, factors, lev_out, coarse_out, *scratch):
    (ph, co, po, so, in_sem, ys1, yr1, zs1, zr1, xs1, xr1, xk1, xs2, xr2, xk2, ys3, yr3, zs3, zr3, ys4, yr4, zs4, zr4,
     qb, ys6, yr6, zs6, zr6, ys7, yr7, zs7, zr7, gb, factor, ssem, rsem) = scratch
    ax, ay, az = names
    nx, ny, nz = sizes
    gx, gy, gz = (lax.axis_index(a) for a in names)
    here = {ax: gx, ay: gy, az: gz}
    count = {ax: nx, ay: ny, az: nz}

    def has(axis, step):
        at = here[axis] + step
        return (at >= 0) & (at < count[axis])

    barrier = pltpu.get_barrier_semaphore()
    met = jnp.int32(nz - 1)
    for d in range(-XREACH, XREACH + 1):
        if d:
            met = met + has(ax, d).astype(jnp.int32)

            @pl.when(has(ax, d))
            def _(d=d):
                pl.semaphore_signal(barrier, inc=1, device_id={ax: gx + d}, device_id_type=MESH)

    for d in range(-YREACH, YREACH + 1):
        if d:
            met = met + nz * has(ay, d).astype(jnp.int32)

            @pl.when(has(ay, d))
            def _(d=d):
                for rel in range(nz):
                    to = {ay: gy + d, az: lax.rem(gz + rel, nz)}
                    pl.semaphore_signal(barrier, inc=1, device_id=to, device_id_type=MESH)

    for rel in range(1, nz):
        pl.semaphore_signal(barrier, inc=1, device_id={az: lax.rem(gz + rel, nz)}, device_id_type=MESH)

    loads = [pltpu.make_async_copy(a, b, in_sem.at[i]) for i, (a, b) in enumerate(((phase, ph), (conc, co), (factors, factor), (pot, po), (src, so)))]
    for load in loads:
        load.start()

    for axis, bufs in ((ax, (xr1, xr2)), (ay, (yr1, yr3, yr4, yr6, yr7)), (az, (zr1, zr3, zr4, zr6, zr7))):
        for side, d in ((0, -1), (1, 1)):

            @pl.when(jnp.logical_not(has(axis, d)))
            def _(bufs=bufs, side=side):
                for buf in bufs:
                    buf[side] = jnp.zeros(buf.shape[1:], jnp.float32)

    for axis, buf, reach in ((ax, qb, XREACH), (ay, gb, YREACH)):
        for d in range(-reach, reach + 1):
            if d:

                @pl.when(jnp.logical_not(has(axis, d)))
                def _(buf=buf, slot=reach + d):
                    buf[slot] = jnp.zeros(buf.shape[1:], jnp.float32)

    pending = []
    used = [0]

    def fresh(n=1):
        used[0] += n
        return used[0] - n

    def copy(k, a, b, target):
        return pltpu.make_async_remote_copy(
            src_ref=a, dst_ref=b, send_sem=ssem.at[k], recv_sem=rsem.at[k], device_id=target, device_id_type=MESH
        )

    def start(k, a, b, target, when):
        pending.append((k, a, b, target, when))

        @pl.when(when)
        def _():
            copy(k, a, b, target).start()

    def arrived(k, b, when):
        @pl.when(when)
        def _():
            copy(k, b, b, {}).wait_recv()

    def push(k, a, b, axis, d):
        start(k, a, b, {axis: here[axis] + d}, has(axis, d))

    def take(k, b, axis, d):
        arrived(k, b, has(axis, d))

    def exchange(axis, sent, got):
        k = fresh(2)
        push(k, sent.at[0], got.at[1], axis, -1)
        push(k + 1, sent.at[1], got.at[0], axis, 1)

        def wait():
            take(k, got.at[1], axis, 1)
            take(k + 1, got.at[0], axis, -1)

        return wait

    place = lax.rem(gx, XROW)

    class Crossing:
        def __init__(self, sent, got, kept, pieces, lines):
            self.sent, self.got, self.kept, self.pieces, self.lines = sent, got, kept, pieces, lines
            self.whole = fresh(2)
            self.part = fresh(2 * len(pieces))
            self.hop = fresh(2 * len(pieces))
            for side, d in ((0, -1), (1, 1)):
                edge = 0 if side == 0 else XROW - 1
                inside = has(ax, d) & (place != edge)
                leaves = has(ax, d) & (place == edge)
                start(self.whole + side, sent.at[side], got.at[1 - side], {ax: gx + d}, inside)
                for i, piece in enumerate(pieces):
                    line = lines[side][i]
                    if line == edge:
                        start(self.sem(side, i), sent.at[side, piece], got.at[1 - side, piece], {ax: gx + d}, leaves)
                    else:
                        peer = {ax: gx + line - edge}
                        k = self.hop + side * len(pieces) + i
                        start(k, sent.at[side, piece], kept.at[side], peer, leaves)

        def sem(self, side, i):
            return self.part + side * len(self.pieces) + i

        def forward(self):
            for side, d in ((0, -1), (1, 1)):
                edge = 0 if side == 0 else XROW - 1
                to = gx - place + edge + d
                exists = (to >= 0) & (to < nx)
                for i, piece in enumerate(self.pieces):
                    line = self.lines[side][i]
                    if line != edge:
                        mine = exists & (place == line)
                        arrived(self.hop + side * len(self.pieces) + i, self.kept.at[side], mine)
                        start(self.sem(side, i), self.kept.at[side], self.got.at[1 - side, piece], {ax: to}, mine)

        def finish(self):
            for side, d in ((0, -1), (1, 1)):
                edge = 0 if side == 0 else XROW - 1
                arrived(self.whole + 1 - side, self.got.at[side], has(ax, d) & (place != edge))
                for i, piece in enumerate(self.pieces):
                    arrived(self.sem(1 - side, i), self.got.at[side, piece], has(ax, d) & (place == edge))

    sub = lax.broadcasted_iota(jnp.int32, (8, WIDE), 0)
    lane = lax.broadcasted_iota(jnp.int32, (8, WIDE), 1)
    lane1 = lax.broadcasted_iota(jnp.int32, (8, 128), 1)

    def zpack(sent, slabs, stride, unit):
        low = high = jnp.zeros((8, 128), jnp.float32)
        for k, s in enumerate(slabs):
            mine = (lane1 >= unit * k) & (lane1 < unit * (k + 1))
            low = jnp.where(mine, rl(s[:, :128], unit * k), low)
            high = jnp.where(mine, rl(s[:, 128:], unit * k - (128 - stride)), high)
        sent[0] = low
        sent[1] = high

    def zhalo(low, high, k, stride, unit):
        return jnp.concatenate([rl(low, -unit * k), rl(high, 128 - stride - unit * k)], axis=1)

    def ypack_rows(sent, slabs, stride):
        for g in range(sent.shape[1]):
            low = high = jnp.zeros((8, WIDE), jnp.float32)
            for j, s in enumerate(slabs[8 * g : 8 * g + 8]):
                low = jnp.where(sub == j, rs(s, j), low)
                high = jnp.where(sub == j, rs(s, j - (8 - stride)), high)
            sent[0, g] = low
            sent[1, g] = high

    def row(got, side, k):
        return jnp.broadcast_to(got[side, k // 8, k % 8 : k % 8 + 1, :], (8, WIDE))

    loads[0].wait()
    loads[1].wait()
    loads[2].wait()
    loads[3].wait()
    phase_v = ph[...]
    conc_v = co[...]
    lookup = jnp.zeros(phase_v.shape, jnp.float32)
    for i in range(3):
        lookup = lookup + jnp.where(phase_v == i, factor[i], 0.0)
    conduct = lookup * conc_v * jnp.exp(-DECAY * conc_v)
    fine = [jnp.stack([conduct[x]] + [po[f, x] for f in range(FIELDS)]) for x in range(8)]
    ypack_rows(ys1, [fine[x][a] for a in range(4) for x in range(8)], 1)
    zpack(zs1, [fine[x][a] for a in range(4) for x in range(8)], 1, 1)
    xs1[0] = fine[0]
    xs1[1] = fine[7]
    loads[4].wait()

    pl.semaphore_wait(barrier, met)

    wait_y1 = exchange(ay, ys1, yr1)
    wait_z1 = exchange(az, zs1, zr1)
    slabs = [pl.ds(i, 1) for i in range(4)]
    early = Crossing(xs1, xr1, xk1, slabs, ([0, 1, 2, 3], [0, 1, 2, 3]))

    def rest(c):
        return c[0], c[1:]

    def flux(c, v, other):
        face = harmonic(c, other[0])
        return face, face * (v - other[1:])

    inner = []
    for i in range(3):
        a, b = fine[2 * i + 1], fine[2 * i + 2]
        inner.append(flux(a[0], a[1:], b))

    wait_y1()
    wait_z1()
    zlow, zhigh = zr1[0], zr1[1]
    part, ypart, zpart = [], [], []
    for x in range(8):
        c, v = rest(fine[x])
        near = jnp.where(sub % 2 == 0, rs(fine[x], 1), rs(fine[x], -1))
        edge = jnp.stack([jnp.where(sub == 0, row(yr1, 0, a * 8 + x), row(yr1, 1, a * 8 + x)) for a in range(4)])
        near = jnp.where((sub == 0) | (sub == 7), edge, near)
        sy, fy = flux(c, v, near)
        near = jnp.where(lane % 2 == 0, rl(fine[x], 1), rl(fine[x], -1))
        edge = jnp.stack([zhalo(zlow, zhigh, a * 8 + x, 1, 1) for a in range(4)])
        near = jnp.where((lane == 0) | (lane == WIDE - 1), edge, near)
        sz, fz = flux(c, v, near)
        source = jnp.stack([so[f, x] for f in range(FIELDS)])
        part.append(source - MASS * v - fy - fz)
        ypart.append(sy)
        zpart.append(sz)

    def fold(t, stride):
        t = t + rl(t, -stride)
        return t + rs(t, -stride)

    mass1 = MASS * 8.0
    r1, ylo, yhi, zlo, zhi, diag, sx = {}, {}, {}, {}, {}, {}, {}
    for i in range(3):
        sx[i] = fold(inner[i][0], 1)
    for i in range(4):
        t = part[2 * i] + part[2 * i + 1]
        if i < 3:
            t = t - inner[i][1]
        if i > 0:
            t = t + inner[i - 1][1]
        r1[i] = fold(t, 1)
        a = ypart[2 * i] + ypart[2 * i + 1]
        a = a + rl(a, -1)
        ylo[i], yhi[i] = a, rs(a, -1)
        b = zpart[2 * i] + zpart[2 * i + 1]
        b = b + rs(b, -1)
        zlo[i], zhi[i] = b, rl(b, -1)
        d = mass1 + ylo[i] + yhi[i] + zlo[i] + zhi[i]
        if i < 3:
            d = d + sx[i]
        if i > 0:
            d = d + sx[i - 1]
        diag[i] = d

    e0, weight = {}, {}
    for i in (1, 2):
        weight[i] = DAMPING / safe(diag[i])
        e0[i] = weight[i] * r1[i]

    q0 = sub % 2 == 0
    p0 = lane % 2 == 0

    def merge4(a, b, c, d):
        return jnp.where(q0, jnp.where(p0, a, rl(b, 1)), jnp.where(p0, rs(c, 1), rs(rl(d, 1), 1)))

    def split4(m):
        low = rs(m, -1)
        return m, rl(m, -1), low, rl(low, -1)

    for side, (edge, next_to, face) in enumerate(((0, 1, 0), (3, 2, 2))):
        xs2[side, 0] = merge4(e0[next_to][0], e0[next_to][1], e0[next_to][2], diag[edge])
        xs2[side, 1] = merge4(r1[edge][0], r1[edge][1], r1[edge][2], sx[face])
        xs2[side, 2] = merge4(ylo[edge], yhi[edge], zlo[edge], zhi[edge])
    late = Crossing(xs2, xr2, xk2, [pl.ds(0, 2), pl.ds(2, 1)], ([0, 1], [XROW - 1, XROW - 2]))
    early.forward()
    late.forward()
    early.finish()
    border = {}
    for side, x in ((0, 0), (1, 7)):
        face, out = flux(fine[x][0], fine[x][1:], xr1[side])
        border[side] = (fold(face, 1), fold(out, 1))
    late.finish()
    for side, edge, out, far, own_face, far_face in ((0, 0, -1, -2, -1, -2), (1, 3, 4, 5, 3, 4)):
        face, through = border[side]
        a = split4(xr2[side, 0])
        b = split4(xr2[side, 1])
        c = split4(xr2[side, 2])
        e0[far] = jnp.stack(a[:3])
        r1[out] = jnp.stack(b[:3]) + through
        r1[edge] = r1[edge] - through
        sx[far_face] = b[3]
        sx[own_face] = face
        ylo[out], yhi[out], zlo[out], zhi[out] = c
        diag[out] = a[3] + face
        diag[edge] = diag[edge] + face
        for i in (out, edge):
            weight[i] = DAMPING / safe(diag[i])
            e0[i] = weight[i] * r1[i]

    def halos(got_y, got_z, layers, low, high, i):
        base = layers.index(i) * FIELDS
        ylow = jnp.stack([row(got_y, 0, base + f) for f in range(FIELDS)])
        yhigh = jnp.stack([row(got_y, 1, base + f) for f in range(FIELDS)])
        zedge = jnp.stack([zhalo(low, high, base + f, 2, 1) for f in range(FIELDS)])
        return ylow, yhigh, zedge

    six = [-1, 0, 1, 2, 3, 4]
    slabs = [e0[i][f] for i in six for f in range(FIELDS)]
    ypack_rows(ys3, slabs, 2)
    wait_y = exchange(ay, ys3, yr3)
    zpack(zs3, slabs, 2, 1)
    wait_z = exchange(az, zs3, zr3)
    wait_y()
    wait_z()
    low, high = zr3[0], zr3[1]
    e1 = {}
    for i in six:
        e = e0[i]
        ylow, yhigh, zedge = halos(yr3, zr3, six, low, high, i)
        total = mass1 * e + sx[i - 1] * (e - e0[i - 1]) + sx[i] * (e - e0[i + 1])
        total = total + ylo[i] * (e - jnp.where(sub < 2, ylow, rs(e, 2)))
        total = total + yhi[i] * (e - jnp.where(sub >= 6, yhigh, rs(e, -2)))
        total = total + zlo[i] * (e - jnp.where(lane < 2, zedge, rl(e, 2)))
        total = total + zhi[i] * (e - jnp.where(lane >= WIDE - 2, zedge, rl(e, -2)))
        e1[i] = e + weight[i] * (r1[i] - total)

    four = [0, 1, 2, 3]
    slabs = [e1[i][f] for i in four for f in range(FIELDS)]
    ypack_rows(ys4, slabs, 2)
    wait_y = exchange(ay, ys4, yr4)
    zpack(zs4, slabs, 2, 1)
    wait_z = exchange(az, zs4, zr4)

    mass2 = mass1 * 8.0
    yfirst = sub % 4 < 2
    zfirst = lane % 4 < 2
    yout = {i: jnp.where(yfirst, ylo[i], yhi[i]) for i in four}
    zout = {i: jnp.where(zfirst, zlo[i], zhi[i]) for i in four}
    sx2 = {-1: fold(sx[-1], 2), 0: fold(sx[1], 2), 1: fold(sx[3], 2)}
    ylo2, yhi2, zlo2, zhi2, diag2 = {}, {}, {}, {}, {}
    for i in range(2):
        a = yout[2 * i] + yout[2 * i + 1]
        a = a + rl(a, -2)
        ylo2[i], yhi2[i] = a, rs(a, -2)
        b = zout[2 * i] + zout[2 * i + 1]
        b = b + rs(b, -2)
        zlo2[i], zhi2[i] = b, rl(b, -2)
        diag2[i] = mass2 + sx2[i - 1] + sx2[i] + ylo2[i] + yhi2[i] + zlo2[i] + zhi2[i]

    wait_y()
    wait_z()
    low, high = zr4[0], zr4[1]
    left = {}
    for i in four:
        e = e1[i]
        ylow, yhigh, zedge = halos(yr4, zr4, four, low, high, i)
        across = i - 1 if i % 2 == 0 else i + 1
        near_y = jnp.where(yfirst, jnp.where(sub < 2, ylow, rs(e, 2)), jnp.where(sub >= 6, yhigh, rs(e, -2)))
        near_z = jnp.where(zfirst, rl(e, 2), rl(e, -2))
        near_z = jnp.where((lane < 2) | (lane >= WIDE - 2), zedge, near_z)
        total = mass1 * e + sx[min(i, across)] * (e - e1[across])
        total = total + yout[i] * (e - near_y) + zout[i] * (e - near_z)
        left[i] = r1[i] - total
    r2 = {i: fold(left[2 * i] + left[2 * i + 1], 2) for i in range(2)}

    q4 = sub % 4
    p4 = lane % 4

    def by(which, a, b, c, d):
        return jnp.where(which < 2, jnp.where(which == 0, a, b), jnp.where(which == 2, c, d))

    def rows4(a, b, c, d):
        return by(q4, a, rs(b, 1), rs(c, 2), rs(d, 3))

    block = by(
        p4,
        rows4(r2[0][0], r2[0][1], r2[0][2], diag2[0]),
        rl(rows4(r2[1][0], r2[1][1], r2[1][2], diag2[1]), 1),
        rl(rows4(sx2[0], yhi2[0], zhi2[0], zlo2[0]), 2),
        rl(rows4(sx2[1], yhi2[1], zhi2[1], zlo2[1]), 3),
    )
    qb[XREACH] = block
    direct = fresh(2 * XREACH + 1)
    for d in (-XREACH, XREACH, 1, -1, 2, -2, 3, -3):
        inside = has(ax, d) if abs(d) == XREACH else has(ax, d) & (place + d >= 0) & (place + d < XROW)
        start(direct + XREACH - d, qb.at[XREACH], qb.at[XREACH - d], {ax: gx + d}, inside)

    packed = jnp.concatenate([merge4(*(e1[i][f] for i in four)) for f in range(FIELDS)], axis=0)
    r = lax.broadcasted_iota(jnp.int32, (WIDE, WIDE), 0)
    c = lax.broadcasted_iota(jnp.int32, (WIDE, WIDE), 1)
    order = jnp.where(c == (r % 2) * 128 + r // 2, 1.0, 0.0)
    dense = jnp.dot(packed, order, precision=lax.Precision.HIGHEST, preferred_element_type=jnp.float32)
    for f in range(FIELDS):
        for y in range(4):
            for q in range(2):
                for p in range(2):
                    k = f * 8 + 2 * y + q
                    lev_out[f, 2 * q + p, y : y + 1, :] = dense[k : k + 1, 128 * p : 128 * p + 128]

    handed = fresh(2 * XREACH + 1)
    for side in (-1, 1):
        far = XREACH + side * XREACH
        take(direct + far, qb.at[far], ax, side * XREACH)
        for step in range(1, XROW):
            slot = far - side * step
            inside = has(ax, side * XREACH) & (place + side * step >= 0) & (place + side * step < XROW)
            start(handed + slot, qb.at[far], qb.at[slot], {ax: gx + side * step}, inside)
    for side in (-1, 1):
        for step in range(1, XROW):
            slot = XREACH + side * step
            inside = (place + side * step >= 0) & (place + side * step < XROW)
            arrived(direct + slot, qb.at[slot], has(ax, side * step) & inside)
            arrived(handed + slot, qb.at[slot], has(ax, side * step) & jnp.logical_not(inside))

    n2 = 2 * XREACH + 1
    q = qb[...]

    def spread(x, item):
        return jnp.where(q4 == 0, rs(x, -item), jnp.where(q4 == 1, rs(x, 1 - item), rs(x, 2 - item)))

    layer0 = p4 == 0
    weight2 = DAMPING / safe(spread(q, 3))
    coef = rl(q, -2)
    xhi, yhi_, zhi_, zlo_ = (spread(coef, item) for item in range(4))
    e = weight2 * q

    def below(x):
        return jnp.concatenate([x[:1], x[:-1]], axis=0)

    def above(x):
        return jnp.concatenate([x[1:], x[-1:]], axis=0)

    def next_x(x):
        return jnp.where(layer0, rl(x, -1), above(rl(x, 1)))

    def last_x(x):
        return jnp.where(layer0, below(rl(x, -1)), rl(x, 1))

    def ypack_halves(sent, x):
        for g in range(sent.shape[1]):
            a, b = x[2 * g], x[min(2 * g + 1, x.shape[0] - 1)]
            sent[0, g] = jnp.where(sub < 4, a, rs(b, 4))
            sent[1, g] = jnp.where(sub < 4, rs(a, 4), b)

    def yedges(got, n):
        out = []
        for d in range(n):
            low, high = got[0, d // 2], got[1, d // 2]
            if d % 2 == 0:
                out.append(jnp.where(sub < 4, low, rs(high, 4)))
            else:
                out.append(jnp.where(sub < 4, rs(low, 4), high))
        return jnp.stack(out)

    def zedges(got, n):
        low, high = got[0], got[1]
        return jnp.stack([zhalo(low, high, d, 4, 4) for d in range(n)])

    ypack_halves(ys6, jnp.where(q4 == 3, rs(coef, 2), e))
    wait_y = exchange(ay, ys6, yr6)
    zpack(zs6, [e[d] for d in range(n2)], 4, 4)
    wait_z = exchange(az, zs6, zr6)
    xlo = last_x(xhi)
    near = xlo * (e - last_x(e)) + xhi * (e - next_x(e)) + mass2 * e
    wait_y()
    wait_z()
    edge = yedges(yr6, n2)
    zedge = zedges(zr6, n2)
    ylo_ = jnp.where(sub < 4, spread(edge, 3), rs(yhi_, 4))
    other = rs(e, 4)
    total = near + ylo_ * (e - jnp.where(sub < 4, edge, other)) + yhi_ * (e - jnp.where(sub < 4, other, edge))
    total = total + zlo_ * (e - jnp.where(lane < 4, zedge, rl(e, 4)))
    total = total + zhi_ * (e - jnp.where(lane >= WIDE - 4, zedge, rl(e, -4)))
    e = e + weight2 * (q - total)

    n3 = n2 - 2
    ypack_halves(ys7, e[1:-1])
    wait_y = exchange(ay, ys7, yr7)
    zpack(zs7, [e[d] for d in range(1, n2 - 1)], 4, 4)
    wait_z = exchange(az, zs7, zr7)

    mass3 = mass2 * 8.0
    zfirst = lane % 8 < 4
    xout = jnp.where(layer0, xlo, xhi)[1:-1]
    yout = jnp.where(sub < 4, ylo_, yhi_)[1:-1]
    zout = jnp.where(zfirst, zlo_, zhi_)[1:-1]
    a = xout + rs(xout, 4)
    a = a + rl(a, -4)
    xlo3, xhi3 = a, rl(a, -1)
    a = yout + rl(yout, -1)
    a = a + rl(a, -4)
    ylo3, yhi3 = a, rs(a, 4)
    a = zout + rl(zout, -1)
    a = a + rs(a, 4)
    zlo3, zhi3 = a, rl(a, -4)
    diag3 = mass3 + xlo3 + xhi3 + ylo3 + yhi3 + zlo3 + zhi3
    near_x = jnp.where(layer0, last_x(e), next_x(e))[1:-1]
    e = e[1:-1]
    near_z = jnp.where(zfirst, rl(e, 4), rl(e, -4))
    partial = q[1:-1] - mass2 * e - xout * (e - near_x)
    coefs = jnp.where(sub == 3, rs(diag3, 3), jnp.where(sub == 4, rs(xhi3, 4), jnp.where(sub == 5, rs(yhi3, 5), rs(zhi3, 6))))
    wait_y()
    wait_z()
    edge = yedges(yr7, n3)
    zedge = zedges(zr7, n3)
    near_z = jnp.where((lane < 4) | (lane >= WIDE - 4), zedge, near_z)
    t = partial - yout * (e - edge) - zout * (e - near_z)
    t = t + rl(t, -1)
    t = t + rs(t, 4)
    t = t + rl(t, -4)
    t = jnp.where(sub < 3, t, coefs)
    block = jnp.zeros((8, WIDE), jnp.float32)
    for l in range(n3):
        block = jnp.where((lane % 8 == l) & (sub < 7), rl(t[l], l), block)

    def column(slot, at):
        return gb.at[slot, :, pl.ds(pl.multiple_of(at * WIDE, WIDE), WIDE)]

    gb[YREACH, :, pl.ds(pl.multiple_of(gz * WIDE, WIDE), WIDE)] = block
    first = fresh((2 * YREACH + 1) * nz)
    others = [(d, rel) for d in sorted(range(-YREACH, YREACH + 1), key=abs) for rel in range(nz) if d or rel]
    for d, rel in others:
        k = first + (YREACH - d) * nz + rel
        to = {ay: gy + d, az: lax.rem(gz + rel, nz)}
        start(k, column(YREACH, gz), column(YREACH - d, gz), to, has(ay, d))
    for d, rel in others:
        k = first + (YREACH - d) * nz + rel
        arrived(k, column(YREACH - d, lax.rem(gz + nz - rel, nz)), has(ay, -d))

    full = (8, WIDE * nz)
    n = 2 * YREACH + 1

    def coefficient(j, item):
        return jnp.broadcast_to(gb[j, item : item + 1, :], full)

    r3 = [gb[j] for j in range(n)]
    w3 = [DAMPING / safe(coefficient(j, 3)) for j in range(n)]
    e = {j: w3[j] * r3[j] for j in range(n)}
    xhi = {j: coefficient(j, 4) for j in range(1, n - 1)}
    yhi = {j: coefficient(j, 5) for j in range(n - 1)}
    zhi = {j: coefficient(j, 6) for j in range(1, n - 1)}
    xlo = {j: rl(xhi[j], 1) for j in xhi}
    zlo = {j: rl(zhi[j], 8) for j in zhi}
    for sweep in range(1, YREACH + 1):
        new = {}
        for j in range(sweep, n - sweep):
            v = e[j]
            total = mass3 * v + xlo[j] * (v - rl(v, 1)) + xhi[j] * (v - rl(v, -1))
            total = total + yhi[j - 1] * (v - e[j - 1]) + yhi[j] * (v - e[j + 1])
            total = total + zlo[j] * (v - rl(v, 8)) + zhi[j] * (v - rl(v, -8))
            new[j] = v + w3[j] * (r3[j] - total)
        e = new
    own = e[YREACH]
    tile = jnp.zeros((8, 128), jnp.float32)
    for t in range(2 * nz):
        tile = jnp.where(lane1 % 8 == t, rl(own[:, 128 * t : 128 * t + 128], t - XREACH + 1), tile)
    r = lax.broadcasted_iota(jnp.int32, (128, 32 * nz), 0)
    c = lax.broadcasted_iota(jnp.int32, (128, 32 * nz), 1)
    order = jnp.where(c == (r % 8) * 16 + r // 8, 1.0, 0.0)
    dense = jnp.dot(tile, order, precision=lax.Precision.HIGHEST, preferred_element_type=jnp.float32)
    for f in range(FIELDS):
        coarse_out[f, 0, :, :] = dense[f : f + 1, :]

    for k, a, b, target, when in pending:

        @pl.when(when)
        def _(k=k, a=a, b=b, target=target):
            copy(k, a, b, target).wait_send()


def solution(mesh):
    names = mesh.axis_names
    sizes = tuple(mesh.shape[a] for a in names)
    nz = sizes[2]
    f32 = jnp.float32

    def both(*shape):
        return [pltpu.VMEM((2, *shape), f32)] * 2

    scratch = [
        pltpu.VMEM((8, 8, WIDE), jnp.int32),
        pltpu.VMEM((8, 8, WIDE), f32),
        pltpu.VMEM((FIELDS, 8, 8, WIDE), f32),
        pltpu.VMEM((FIELDS, 8, 8, WIDE), f32),
        pltpu.SemaphoreType.DMA((5,)),
        *both(4, 8, WIDE), *both(8, 128),
        *both(4, 8, WIDE), pltpu.VMEM((2, 1, 8, WIDE), f32), *both(3, 8, WIDE), pltpu.VMEM((2, 1, 8, WIDE), f32),
        *both(3, 8, WIDE), *both(8, 128),
        *both(2, 8, WIDE), *both(8, 128),
        pltpu.VMEM((2 * XREACH + 1, 8, WIDE), f32),
        *both(5, 8, WIDE), *both(8, 128),
        *both(4, 8, WIDE), *both(8, 128),
        pltpu.VMEM((2 * YREACH + 1, 8, WIDE * nz), f32),
        pltpu.SMEM((3,), f32),
    ]
    sems = 2 * 2 * 5 + (2 + 16) + (2 + 8) + 2 * (2 * XREACH + 1) + (2 * YREACH + 1) * nz
    scratch += [pltpu.SemaphoreType.DMA((sems,)), pltpu.SemaphoreType.DMA((sems,))]

    def local(phase_label, concentration, phase_factor, potential, source):
        return pl.pallas_call(
            functools.partial(kernel, names, sizes),
            out_shape=(
                jax.ShapeDtypeStruct((FIELDS, 4, 4, 128), f32),
                jax.ShapeDtypeStruct((FIELDS, 1, 1, 32 * nz), f32),
            ),
            in_specs=[pl.BlockSpec(memory_space=pltpu.HBM)] * 5,
            out_specs=(pl.BlockSpec(memory_space=pltpu.VMEM), pl.BlockSpec(memory_space=pltpu.VMEM)),
            scratch_shapes=scratch,
            compiler_params=pltpu.CompilerParams(collective_id=0, has_side_effects=True, vmem_limit_bytes=55168 << 10),
        )(phase_label, concentration, potential, source, phase_factor)

    return jax.shard_map(
        local,
        mesh=mesh,
        in_specs=(P(*names), P(*names), P(), P(None, *names), P(None, *names)),
        out_specs=(P(None, *names), P(None, names[0], names[1], None)),
        check_vma=False,
    )
```

```python
import functools

import jax
import jax.numpy as jnp
from jax import lax
from jax.experimental import pallas as pl
from jax.experimental.pallas import tpu as pltpu
from jax.sharding import PartitionSpec as P

MESH = pl.DeviceIdType.MESH
FIELDS = 3
MASS = 0.05
DAMPING = 0.7
DECAY = 0.3
XREACH = 4
YREACH = 3
WIDE = 256
XROW = 4


def rs(x, k):
    k %= x.shape[-2]
    return pltpu.roll(x, k, x.ndim - 2) if k else x


def rl(x, k):
    k %= x.shape[-1]
    return pltpu.roll(x, k, x.ndim - 1) if k else x


def harmonic(a, b):
    return 2.0 * a * b / (a + b)


def safe(d):
    return jnp.where(d > 0.0, d, 1.0)


def kernel(names, sizes, phase, conc, pot, src, factors, lev_out, coarse_out, *scratch):
    (ph, co, po, so, in_sem, ys1, yr1, zs1, zr1, xs1, xr1, xk1, xs2, xr2, xk2, ys3, yr3, zs3, zr3, ys4, yr4, zs4, zr4,
     qb, ys6, yr6, zs6, zr6, ys7, yr7, zs7, zr7, gb, factor, row_sem, ssem, rsem) = scratch
    ax, ay, az = names
    nx, ny, nz = sizes
    gx, gy, gz = (lax.axis_index(a) for a in names)
    here = {ax: gx, ay: gy, az: gz}
    count = {ax: nx, ay: ny, az: nz}

    def has(axis, step):
        at = here[axis] + step
        return (at >= 0) & (at < count[axis])

    barrier = pltpu.get_barrier_semaphore()
    place = lax.rem(gx, XROW)
    met = jnp.int32(nz - 1)
    for d in (1, -1, 2, -2, 3, -3):
        known = has(ax, d) & (place + d >= 0) & (place + d < XROW)
        if abs(d) == 1:
            known = has(ax, d)
        met = met + known.astype(jnp.int32)

        @pl.when(known)
        def _(d=d):
            pl.semaphore_signal(barrier, inc=1, device_id={ax: gx + d}, device_id_type=MESH)

    for d in range(-YREACH, YREACH + 1):
        if d:
            met = met + nz * has(ay, d).astype(jnp.int32)

            @pl.when(has(ay, d))
            def _(d=d):
                for rel in range(nz):
                    to = {ay: gy + d, az: lax.rem(gz + rel, nz)}
                    pl.semaphore_signal(barrier, inc=1, device_id=to, device_id_type=MESH)

    for rel in range(1, nz):
        pl.semaphore_signal(barrier, inc=1, device_id={az: lax.rem(gz + rel, nz)}, device_id_type=MESH)

    loads = [pltpu.make_async_copy(a, b, in_sem.at[i]) for i, (a, b) in enumerate(((phase, ph), (conc, co), (factors, factor), (pot, po), (src, so)))]
    for load in loads:
        load.start()

    for axis, bufs in ((ax, (xr1, xr2)), (ay, (yr1, yr3, yr4, yr6, yr7)), (az, (zr1, zr3, zr4, zr6, zr7))):
        for side, d in ((0, -1), (1, 1)):

            @pl.when(jnp.logical_not(has(axis, d)))
            def _(bufs=bufs, side=side):
                for buf in bufs:
                    buf[side] = jnp.zeros(buf.shape[1:], jnp.float32)

    for axis, buf, reach in ((ax, qb, XREACH), (ay, gb, YREACH)):
        for d in range(-reach, reach + 1):
            if d:

                @pl.when(jnp.logical_not(has(axis, d)))
                def _(buf=buf, slot=reach + d):
                    buf[slot] = jnp.zeros(buf.shape[1:], jnp.float32)

    pending = []
    used = [0]

    def fresh(n=1):
        used[0] += n
        return used[0] - n

    def copy(k, a, b, target):
        return pltpu.make_async_remote_copy(
            src_ref=a, dst_ref=b, send_sem=ssem.at[k], recv_sem=rsem.at[k], device_id=target, device_id_type=MESH
        )

    def start(k, a, b, target, when):
        pending.append((k, a, b, target, when))

        @pl.when(when)
        def _():
            copy(k, a, b, target).start()

    def arrived(k, b, when):
        @pl.when(when)
        def _():
            copy(k, b, b, {}).wait_recv()

    def drain(n):
        for k, a, b, target, when in pending[:n]:

            @pl.when(when)
            def _(k=k, a=a, b=b, target=target):
                copy(k, a, b, target).wait_send()

        del pending[:n]

    def push(k, a, b, axis, d):
        start(k, a, b, {axis: here[axis] + d}, has(axis, d))

    def take(k, b, axis, d):
        arrived(k, b, has(axis, d))

    def exchange(axis, sent, got):
        k = fresh(2)
        push(k, sent.at[0], got.at[1], axis, -1)
        push(k + 1, sent.at[1], got.at[0], axis, 1)

        def wait():
            take(k, got.at[1], axis, 1)
            take(k + 1, got.at[0], axis, -1)

        return wait

    class Crossing:
        def __init__(self, sent, got, kept, pieces, lines):
            self.sent, self.got, self.kept, self.pieces, self.lines = sent, got, kept, pieces, lines
            self.whole = fresh(2)
            self.part = fresh(2 * len(pieces))
            self.hop = fresh(2 * len(pieces))
            for side, d in ((0, -1), (1, 1)):
                edge = 0 if side == 0 else XROW - 1
                inside = has(ax, d) & (place != edge)
                leaves = has(ax, d) & (place == edge)
                start(self.whole + side, sent.at[side], got.at[1 - side], {ax: gx + d}, inside)
                for i, piece in enumerate(pieces):
                    line = lines[side][i]
                    if line == edge:
                        start(self.sem(side, i), sent.at[side, piece], got.at[1 - side, piece], {ax: gx + d}, leaves)
                    else:
                        peer = {ax: gx + line - edge}
                        k = self.hop + side * len(pieces) + i
                        start(k, sent.at[side, piece], kept.at[side], peer, leaves)

        def sem(self, side, i):
            return self.part + side * len(self.pieces) + i

        def forward(self):
            for side, d in ((0, -1), (1, 1)):
                edge = 0 if side == 0 else XROW - 1
                to = gx - place + edge + d
                exists = (to >= 0) & (to < nx)
                for i, piece in enumerate(self.pieces):
                    line = self.lines[side][i]
                    if line != edge:
                        mine = exists & (place == line)
                        arrived(self.hop + side * len(self.pieces) + i, self.kept.at[side], mine)
                        start(self.sem(side, i), self.kept.at[side], self.got.at[1 - side, piece], {ax: to}, mine)

        def finish(self):
            for side, d in ((0, -1), (1, 1)):
                edge = 0 if side == 0 else XROW - 1
                arrived(self.whole + 1 - side, self.got.at[side], has(ax, d) & (place != edge))
                for i, piece in enumerate(self.pieces):
                    arrived(self.sem(1 - side, i), self.got.at[side, piece], has(ax, d) & (place == edge))

    sub = lax.broadcasted_iota(jnp.int32, (8, WIDE), 0)
    lane = lax.broadcasted_iota(jnp.int32, (8, WIDE), 1)
    lane1 = lax.broadcasted_iota(jnp.int32, (8, 128), 1)

    def zpack(sent, slabs, stride, unit):
        low = high = jnp.zeros((8, 128), jnp.float32)
        for k, s in enumerate(slabs):
            mine = (lane1 >= unit * k) & (lane1 < unit * (k + 1))
            low = jnp.where(mine, rl(s[:, :128], unit * k), low)
            high = jnp.where(mine, rl(s[:, 128:], unit * k - (128 - stride)), high)
        sent[0] = low
        sent[1] = high

    def zhalo(low, high, k, stride, unit):
        return jnp.concatenate([rl(low, -unit * k), rl(high, 128 - stride - unit * k)], axis=1)

    def ypack_rows(sent, slabs, stride):
        for g in range(sent.shape[1]):
            low = high = jnp.zeros((8, WIDE), jnp.float32)
            for j, s in enumerate(slabs[8 * g : 8 * g + 8]):
                low = jnp.where(sub == j, rs(s, j), low)
                high = jnp.where(sub == j, rs(s, j - (8 - stride)), high)
            sent[0, g] = low
            sent[1, g] = high

    def row(got, side, k):
        return jnp.broadcast_to(got[side, k // 8, k % 8 : k % 8 + 1, :], (8, WIDE))

    loads[0].wait()
    loads[1].wait()
    loads[2].wait()
    loads[3].wait()
    phase_v = ph[...]
    conc_v = co[...]
    lookup = jnp.zeros(phase_v.shape, jnp.float32)
    for i in range(3):
        lookup = lookup + jnp.where(phase_v == i, factor[i], 0.0)
    conduct = lookup * conc_v * jnp.exp(-DECAY * conc_v)
    fine = [jnp.stack([conduct[x]] + [po[f, x] for f in range(FIELDS)]) for x in range(8)]
    ypack_rows(ys1, [fine[x][a] for a in range(4) for x in range(8)], 1)
    zpack(zs1, [fine[x][a] for a in range(4) for x in range(8)], 1, 1)
    xs1[0] = fine[0]
    xs1[1] = fine[7]
    loads[4].wait()

    pl.semaphore_wait(barrier, met)

    wait_y1 = exchange(ay, ys1, yr1)
    wait_z1 = exchange(az, zs1, zr1)
    slabs = [pl.ds(i, 1) for i in range(4)]
    early = Crossing(xs1, xr1, xk1, slabs, ([0, 1, 2, 3], [0, 1, 2, 3]))

    def rest(c):
        return c[0], c[1:]

    def flux(c, v, other):
        face = harmonic(c, other[0])
        return face, face * (v - other[1:])

    inner = []
    for i in range(3):
        a, b = fine[2 * i + 1], fine[2 * i + 2]
        inner.append(flux(a[0], a[1:], b))

    wait_y1()
    wait_z1()
    zlow, zhigh = zr1[0], zr1[1]
    part, ypart, zpart = [], [], []
    for x in range(8):
        c, v = rest(fine[x])
        near = jnp.where(sub % 2 == 0, rs(fine[x], 1), rs(fine[x], -1))
        edge = jnp.stack([jnp.where(sub == 0, row(yr1, 0, a * 8 + x), row(yr1, 1, a * 8 + x)) for a in range(4)])
        near = jnp.where((sub == 0) | (sub == 7), edge, near)
        sy, fy = flux(c, v, near)
        near = jnp.where(lane % 2 == 0, rl(fine[x], 1), rl(fine[x], -1))
        edge = jnp.stack([zhalo(zlow, zhigh, a * 8 + x, 1, 1) for a in range(4)])
        near = jnp.where((lane == 0) | (lane == WIDE - 1), edge, near)
        sz, fz = flux(c, v, near)
        source = jnp.stack([so[f, x] for f in range(FIELDS)])
        part.append(source - MASS * v - fy - fz)
        ypart.append(sy)
        zpart.append(sz)

    def fold(t, stride):
        t = t + rl(t, -stride)
        return t + rs(t, -stride)

    mass1 = MASS * 8.0
    r1, ylo, yhi, zlo, zhi, diag, sx = {}, {}, {}, {}, {}, {}, {}
    for i in range(3):
        sx[i] = fold(inner[i][0], 1)
    for i in range(4):
        t = part[2 * i] + part[2 * i + 1]
        if i < 3:
            t = t - inner[i][1]
        if i > 0:
            t = t + inner[i - 1][1]
        r1[i] = fold(t, 1)
        a = ypart[2 * i] + ypart[2 * i + 1]
        a = a + rl(a, -1)
        ylo[i], yhi[i] = a, rs(a, -1)
        b = zpart[2 * i] + zpart[2 * i + 1]
        b = b + rs(b, -1)
        zlo[i], zhi[i] = b, rl(b, -1)
        d = mass1 + ylo[i] + yhi[i] + zlo[i] + zhi[i]
        if i < 3:
            d = d + sx[i]
        if i > 0:
            d = d + sx[i - 1]
        diag[i] = d

    e0, weight = {}, {}
    for i in (1, 2):
        weight[i] = DAMPING / safe(diag[i])
        e0[i] = weight[i] * r1[i]

    q0 = sub % 2 == 0
    p0 = lane % 2 == 0

    def merge4(a, b, c, d):
        return jnp.where(q0, jnp.where(p0, a, rl(b, 1)), jnp.where(p0, rs(c, 1), rs(rl(d, 1), 1)))

    def split4(m):
        low = rs(m, -1)
        return m, rl(m, -1), low, rl(low, -1)

    for side, (edge, next_to, face) in enumerate(((0, 1, 0), (3, 2, 2))):
        xs2[side, 0] = merge4(e0[next_to][0], e0[next_to][1], e0[next_to][2], diag[edge])
        xs2[side, 1] = merge4(r1[edge][0], r1[edge][1], r1[edge][2], sx[face])
        xs2[side, 2] = merge4(ylo[edge], yhi[edge], zlo[edge], zhi[edge])
    late = Crossing(xs2, xr2, xk2, [pl.ds(0, 2), pl.ds(2, 1)], ([0, 1], [XROW - 1, XROW - 2]))
    early.forward()
    late.forward()
    early.finish()
    for side, edge in ((0, 0), (1, XROW - 1)):
        step = 1 if side == 0 else -1

        @pl.when((place == edge) & has(ax, -step))
        def _(side=side, step=step):
            for i in range(1, XROW):
                pl.semaphore_signal(row_sem.at[side], inc=1, device_id={ax: gx + step * i}, device_id_type=MESH)

    border = {}
    for side, x in ((0, 0), (1, 7)):
        face, out = flux(fine[x][0], fine[x][1:], xr1[side])
        border[side] = (fold(face, 1), fold(out, 1))
    late.finish()
    for side, edge, out, far, own_face, far_face in ((0, 0, -1, -2, -1, -2), (1, 3, 4, 5, 3, 4)):
        face, through = border[side]
        a = split4(xr2[side, 0])
        b = split4(xr2[side, 1])
        c = split4(xr2[side, 2])
        e0[far] = jnp.stack(a[:3])
        r1[out] = jnp.stack(b[:3]) + through
        r1[edge] = r1[edge] - through
        sx[far_face] = b[3]
        sx[own_face] = face
        ylo[out], yhi[out], zlo[out], zhi[out] = c
        diag[out] = a[3] + face
        diag[edge] = diag[edge] + face
        for i in (out, edge):
            weight[i] = DAMPING / safe(diag[i])
            e0[i] = weight[i] * r1[i]

    def halos(got_y, got_z, layers, low, high, i):
        base = layers.index(i) * FIELDS
        ylow = jnp.stack([row(got_y, 0, base + f) for f in range(FIELDS)])
        yhigh = jnp.stack([row(got_y, 1, base + f) for f in range(FIELDS)])
        zedge = jnp.stack([zhalo(low, high, base + f, 2, 1) for f in range(FIELDS)])
        return ylow, yhigh, zedge

    six = [-1, 0, 1, 2, 3, 4]
    slabs = [e0[i][f] for i in six for f in range(FIELDS)]
    ypack_rows(ys3, slabs, 2)
    wait_y = exchange(ay, ys3, yr3)
    zpack(zs3, slabs, 2, 1)
    wait_z = exchange(az, zs3, zr3)
    wait_y()
    wait_z()
    low, high = zr3[0], zr3[1]
    e1 = {}
    for i in six:
        e = e0[i]
        ylow, yhigh, zedge = halos(yr3, zr3, six, low, high, i)
        total = mass1 * e + sx[i - 1] * (e - e0[i - 1]) + sx[i] * (e - e0[i + 1])
        total = total + ylo[i] * (e - jnp.where(sub < 2, ylow, rs(e, 2)))
        total = total + yhi[i] * (e - jnp.where(sub >= 6, yhigh, rs(e, -2)))
        total = total + zlo[i] * (e - jnp.where(lane < 2, zedge, rl(e, 2)))
        total = total + zhi[i] * (e - jnp.where(lane >= WIDE - 2, zedge, rl(e, -2)))
        e1[i] = e + weight[i] * (r1[i] - total)

    four = [0, 1, 2, 3]
    slabs = [e1[i][f] for i in four for f in range(FIELDS)]
    ypack_rows(ys4, slabs, 2)
    wait_y = exchange(ay, ys4, yr4)
    zpack(zs4, slabs, 2, 1)
    wait_z = exchange(az, zs4, zr4)

    mass2 = mass1 * 8.0
    yfirst = sub % 4 < 2
    zfirst = lane % 4 < 2
    yout = {i: jnp.where(yfirst, ylo[i], yhi[i]) for i in four}
    zout = {i: jnp.where(zfirst, zlo[i], zhi[i]) for i in four}
    sx2 = {-1: fold(sx[-1], 2), 0: fold(sx[1], 2), 1: fold(sx[3], 2)}
    ylo2, yhi2, zlo2, zhi2, diag2 = {}, {}, {}, {}, {}
    for i in range(2):
        a = yout[2 * i] + yout[2 * i + 1]
        a = a + rl(a, -2)
        ylo2[i], yhi2[i] = a, rs(a, -2)
        b = zout[2 * i] + zout[2 * i + 1]
        b = b + rs(b, -2)
        zlo2[i], zhi2[i] = b, rl(b, -2)
        diag2[i] = mass2 + sx2[i - 1] + sx2[i] + ylo2[i] + yhi2[i] + zlo2[i] + zhi2[i]

    wait_y()
    wait_z()
    low, high = zr4[0], zr4[1]
    left = {}
    for i in four:
        e = e1[i]
        ylow, yhigh, zedge = halos(yr4, zr4, four, low, high, i)
        across = i - 1 if i % 2 == 0 else i + 1
        near_y = jnp.where(yfirst, jnp.where(sub < 2, ylow, rs(e, 2)), jnp.where(sub >= 6, yhigh, rs(e, -2)))
        near_z = jnp.where(zfirst, rl(e, 2), rl(e, -2))
        near_z = jnp.where((lane < 2) | (lane >= WIDE - 2), zedge, near_z)
        total = mass1 * e + sx[min(i, across)] * (e - e1[across])
        total = total + yout[i] * (e - near_y) + zout[i] * (e - near_z)
        left[i] = r1[i] - total
    r2 = {i: fold(left[2 * i] + left[2 * i + 1], 2) for i in range(2)}

    q4 = sub % 4
    p4 = lane % 4

    def by(which, a, b, c, d):
        return jnp.where(which < 2, jnp.where(which == 0, a, b), jnp.where(which == 2, c, d))

    def rows4(a, b, c, d):
        return by(q4, a, rs(b, 1), rs(c, 2), rs(d, 3))

    block = by(
        p4,
        rows4(r2[0][0], r2[0][1], r2[0][2], diag2[0]),
        rl(rows4(r2[1][0], r2[1][1], r2[1][2], diag2[1]), 1),
        rl(rows4(sx2[0], yhi2[0], zhi2[0], zlo2[0]), 2),
        rl(rows4(sx2[1], yhi2[1], zhi2[1], zlo2[1]), 3),
    )
    qb[XREACH] = block
    old = len(pending)
    direct = fresh(2 * XREACH + 1)
    for side, edge in ((0, 0), (1, XROW - 1)):

        @pl.when((place != edge) & has(ax, XREACH * (2 * side - 1)))
        def _(side=side):
            pl.semaphore_wait(row_sem.at[side], 1)

    for d in (-XREACH, XREACH, 1, -1, 2, -2, 3, -3):
        inside = has(ax, d) if abs(d) == XREACH else has(ax, d) & (place + d >= 0) & (place + d < XROW)
        start(direct + XREACH - d, qb.at[XREACH], qb.at[XREACH - d], {ax: gx + d}, inside)

    drain(old)
    packed = jnp.concatenate([merge4(*(e1[i][f] for i in four)) for f in range(FIELDS)], axis=0)
    r = lax.broadcasted_iota(jnp.int32, (WIDE, WIDE), 0)
    c = lax.broadcasted_iota(jnp.int32, (WIDE, WIDE), 1)
    order = jnp.where(c == (r % 2) * 128 + r // 2, 1.0, 0.0)
    dense = jnp.dot(packed, order, precision=lax.Precision.HIGHEST, preferred_element_type=jnp.float32)
    for f in range(FIELDS):
        for y in range(4):
            for q in range(2):
                for p in range(2):
                    k = f * 8 + 2 * y + q
                    lev_out[f, 2 * q + p, y : y + 1, :] = dense[k : k + 1, 128 * p : 128 * p + 128]

    handed = fresh(2 * XREACH + 1)
    for side in (-1, 1):
        far = XREACH + side * XREACH
        take(direct + far, qb.at[far], ax, side * XREACH)
        for step in range(1, XROW):
            slot = far - side * step
            inside = has(ax, side * XREACH) & (place + side * step >= 0) & (place + side * step < XROW)
            start(handed + slot, qb.at[far], qb.at[slot], {ax: gx + side * step}, inside)
    for side in (-1, 1):
        for step in range(1, XROW):
            slot = XREACH + side * step
            inside = (place + side * step >= 0) & (place + side * step < XROW)
            arrived(direct + slot, qb.at[slot], has(ax, side * step) & inside)
            arrived(handed + slot, qb.at[slot], has(ax, side * step) & jnp.logical_not(inside))

    n2 = 2 * XREACH + 1
    q = qb[...]

    def spread(x, item):
        return jnp.where(q4 == 0, rs(x, -item), jnp.where(q4 == 1, rs(x, 1 - item), rs(x, 2 - item)))

    layer0 = p4 == 0
    weight2 = DAMPING / safe(spread(q, 3))
    coef = rl(q, -2)
    xhi, yhi_, zhi_, zlo_ = (spread(coef, item) for item in range(4))
    e = weight2 * q

    def below(x):
        return jnp.concatenate([x[:1], x[:-1]], axis=0)

    def above(x):
        return jnp.concatenate([x[1:], x[-1:]], axis=0)

    def next_x(x):
        return jnp.where(layer0, rl(x, -1), above(rl(x, 1)))

    def last_x(x):
        return jnp.where(layer0, below(rl(x, -1)), rl(x, 1))

    def ypack_halves(sent, x):
        for g in range(sent.shape[1]):
            a, b = x[2 * g], x[min(2 * g + 1, x.shape[0] - 1)]
            sent[0, g] = jnp.where(sub < 4, a, rs(b, 4))
            sent[1, g] = jnp.where(sub < 4, rs(a, 4), b)

    def yedges(got, n):
        out = []
        for d in range(n):
            low, high = got[0, d // 2], got[1, d // 2]
            if d % 2 == 0:
                out.append(jnp.where(sub < 4, low, rs(high, 4)))
            else:
                out.append(jnp.where(sub < 4, rs(low, 4), high))
        return jnp.stack(out)

    def zedges(got, n):
        low, high = got[0], got[1]
        return jnp.stack([zhalo(low, high, d, 4, 4) for d in range(n)])

    ypack_halves(ys6, jnp.where(q4 == 3, rs(coef, 2), e))
    wait_y = exchange(ay, ys6, yr6)
    zpack(zs6, [e[d] for d in range(n2)], 4, 4)
    wait_z = exchange(az, zs6, zr6)
    xlo = last_x(xhi)
    near = xlo * (e - last_x(e)) + xhi * (e - next_x(e)) + mass2 * e
    wait_y()
    wait_z()
    edge = yedges(yr6, n2)
    zedge = zedges(zr6, n2)
    ylo_ = jnp.where(sub < 4, spread(edge, 3), rs(yhi_, 4))
    other = rs(e, 4)
    total = near + ylo_ * (e - jnp.where(sub < 4, edge, other)) + yhi_ * (e - jnp.where(sub < 4, other, edge))
    total = total + zlo_ * (e - jnp.where(lane < 4, zedge, rl(e, 4)))
    total = total + zhi_ * (e - jnp.where(lane >= WIDE - 4, zedge, rl(e, -4)))
    e = e + weight2 * (q - total)

    n3 = n2 - 2
    ypack_halves(ys7, e[1:-1])
    wait_y = exchange(ay, ys7, yr7)
    zpack(zs7, [e[d] for d in range(1, n2 - 1)], 4, 4)
    wait_z = exchange(az, zs7, zr7)

    mass3 = mass2 * 8.0
    zfirst = lane % 8 < 4
    xout = jnp.where(layer0, xlo, xhi)[1:-1]
    yout = jnp.where(sub < 4, ylo_, yhi_)[1:-1]
    zout = jnp.where(zfirst, zlo_, zhi_)[1:-1]
    a = xout + rs(xout, 4)
    a = a + rl(a, -4)
    xlo3, xhi3 = a, rl(a, -1)
    a = yout + rl(yout, -1)
    a = a + rl(a, -4)
    ylo3, yhi3 = a, rs(a, 4)
    a = zout + rl(zout, -1)
    a = a + rs(a, 4)
    zlo3, zhi3 = a, rl(a, -4)
    diag3 = mass3 + xlo3 + xhi3 + ylo3 + yhi3 + zlo3 + zhi3
    near_x = jnp.where(layer0, last_x(e), next_x(e))[1:-1]
    e = e[1:-1]
    near_z = jnp.where(zfirst, rl(e, 4), rl(e, -4))
    partial = q[1:-1] - mass2 * e - xout * (e - near_x)
    coefs = jnp.where(sub == 3, rs(diag3, 3), jnp.where(sub == 4, rs(xhi3, 4), jnp.where(sub == 5, rs(yhi3, 5), rs(zhi3, 6))))
    wait_y()
    wait_z()
    edge = yedges(yr7, n3)
    zedge = zedges(zr7, n3)
    near_z = jnp.where((lane < 4) | (lane >= WIDE - 4), zedge, near_z)
    t = partial - yout * (e - edge) - zout * (e - near_z)
    t = t + rl(t, -1)
    t = t + rs(t, 4)
    t = t + rl(t, -4)
    t = jnp.where(sub < 3, t, coefs)
    block = jnp.zeros((8, WIDE), jnp.float32)
    for l in range(n3):
        block = jnp.where((lane % 8 == l) & (sub < 7), rl(t[l], l), block)

    def column(slot, at):
        return gb.at[slot, :, pl.ds(pl.multiple_of(at * WIDE, WIDE), WIDE)]

    gb[YREACH, :, pl.ds(pl.multiple_of(gz * WIDE, WIDE), WIDE)] = block
    first = fresh((2 * YREACH + 1) * nz)
    old = len(pending)
    others = [(d, rel) for d in sorted(range(-YREACH, YREACH + 1), key=abs) for rel in range(nz) if d or rel]
    for d, rel in others:
        k = first + (YREACH - d) * nz + rel
        to = {ay: gy + d, az: lax.rem(gz + rel, nz)}
        start(k, column(YREACH, gz), column(YREACH - d, gz), to, has(ay, d))
    drain(old)
    for d, rel in others:
        k = first + (YREACH - d) * nz + rel
        arrived(k, column(YREACH - d, lax.rem(gz + nz - rel, nz)), has(ay, -d))

    full = (8, WIDE * nz)
    n = 2 * YREACH + 1

    def coefficient(j, item):
        return jnp.broadcast_to(gb[j, item : item + 1, :], full)

    r3 = [gb[j] for j in range(n)]
    w3 = [DAMPING / safe(coefficient(j, 3)) for j in range(n)]
    e = {j: w3[j] * r3[j] for j in range(n)}
    xhi = {j: coefficient(j, 4) for j in range(1, n - 1)}
    yhi = {j: coefficient(j, 5) for j in range(n - 1)}
    zhi = {j: coefficient(j, 6) for j in range(1, n - 1)}
    xlo = {j: rl(xhi[j], 1) for j in xhi}
    zlo = {j: rl(zhi[j], 8) for j in zhi}
    for sweep in range(1, YREACH + 1):
        new = {}
        for j in range(sweep, n - sweep):
            v = e[j]
            total = mass3 * v + xlo[j] * (v - rl(v, 1)) + xhi[j] * (v - rl(v, -1))
            total = total + yhi[j - 1] * (v - e[j - 1]) + yhi[j] * (v - e[j + 1])
            total = total + zlo[j] * (v - rl(v, 8)) + zhi[j] * (v - rl(v, -8))
            new[j] = v + w3[j] * (r3[j] - total)
        e = new
    own = e[YREACH]
    tile = jnp.zeros((8, 128), jnp.float32)
    for t in range(2 * nz):
        tile = jnp.where(lane1 % 8 == t, rl(own[:, 128 * t : 128 * t + 128], t - XREACH + 1), tile)
    r = lax.broadcasted_iota(jnp.int32, (128, 32 * nz), 0)
    c = lax.broadcasted_iota(jnp.int32, (128, 32 * nz), 1)
    order = jnp.where(c == (r % 8) * 16 + r // 8, 1.0, 0.0)
    dense = jnp.dot(tile, order, precision=lax.Precision.HIGHEST, preferred_element_type=jnp.float32)
    for f in range(FIELDS):
        coarse_out[f, 0, :, :] = dense[f : f + 1, :]

    drain(len(pending))


def solution(mesh):
    names = mesh.axis_names
    sizes = tuple(mesh.shape[a] for a in names)
    nz = sizes[2]
    f32 = jnp.float32

    def both(*shape):
        return [pltpu.VMEM((2, *shape), f32)] * 2

    scratch = [
        pltpu.VMEM((8, 8, WIDE), jnp.int32),
        pltpu.VMEM((8, 8, WIDE), f32),
        pltpu.VMEM((FIELDS, 8, 8, WIDE), f32),
        pltpu.VMEM((FIELDS, 8, 8, WIDE), f32),
        pltpu.SemaphoreType.DMA((5,)),
        *both(4, 8, WIDE), *both(8, 128),
        *both(4, 8, WIDE), pltpu.VMEM((2, 1, 8, WIDE), f32), *both(3, 8, WIDE), pltpu.VMEM((2, 1, 8, WIDE), f32),
        *both(3, 8, WIDE), *both(8, 128),
        *both(2, 8, WIDE), *both(8, 128),
        pltpu.VMEM((2 * XREACH + 1, 8, WIDE), f32),
        *both(5, 8, WIDE), *both(8, 128),
        *both(4, 8, WIDE), *both(8, 128),
        pltpu.VMEM((2 * YREACH + 1, 8, WIDE * nz), f32),
        pltpu.SMEM((3,), f32),
    ]
    sems = 2 * 2 * 5 + (2 + 16) + (2 + 8) + 2 * (2 * XREACH + 1) + (2 * YREACH + 1) * nz
    scratch += [pltpu.SemaphoreType.REGULAR((2,)), pltpu.SemaphoreType.DMA((sems,)), pltpu.SemaphoreType.DMA((sems,))]

    def local(phase_label, concentration, phase_factor, potential, source):
        return pl.pallas_call(
            functools.partial(kernel, names, sizes),
            out_shape=(
                jax.ShapeDtypeStruct((FIELDS, 4, 4, 128), f32),
                jax.ShapeDtypeStruct((FIELDS, 1, 1, 32 * nz), f32),
            ),
            in_specs=[pl.BlockSpec(memory_space=pltpu.HBM)] * 5,
            out_specs=(pl.BlockSpec(memory_space=pltpu.VMEM), pl.BlockSpec(memory_space=pltpu.VMEM)),
            scratch_shapes=scratch,
            compiler_params=pltpu.CompilerParams(collective_id=0, has_side_effects=True, vmem_limit_bytes=55168 << 10),
        )(phase_label, concentration, potential, source, phase_factor)

    return jax.shard_map(
        local,
        mesh=mesh,
        in_specs=(P(*names), P(*names), P(), P(None, *names), P(None, *names)),
        out_specs=(P(None, *names), P(None, names[0], names[1], None)),
        check_vma=False,
    )
```

```python
import functools

import jax
import jax.numpy as jnp
from jax import lax
from jax.experimental import pallas as pl
from jax.experimental.pallas import tpu as pltpu
from jax.sharding import PartitionSpec as P

MESH = pl.DeviceIdType.MESH
FIELDS = 3
MASS = 0.05
DAMPING = 0.7
DECAY = 0.3
XREACH = 4
YREACH = 3
WIDE = 256
HALVES = (-3, -2, 2, 3)
XROW = 4


def rs(x, k):
    k %= x.shape[-2]
    return pltpu.roll(x, k, x.ndim - 2) if k else x


def rl(x, k):
    k %= x.shape[-1]
    return pltpu.roll(x, k, x.ndim - 1) if k else x


def harmonic(a, b):
    return 2.0 * a * b / (a + b)


def safe(d):
    return jnp.where(d > 0.0, d, 1.0)


def kernel(names, sizes, phase, conc, pot, src, factors, lev_out, coarse_out, *scratch):
    (ph, co, po, so, in_sem, ys1, yr1, zs1, zr1, xs1, xr1, xk1, xs2, xr2, xk2, ys3, yr3, zs3, zr3, ys4, yr4, zs4, zr4,
     qb, ys6, yr6, zs6, zr6, ys7, yr7, zs7, zr7, gb, gh, hs, factor, row_sem, ssem, rsem) = scratch
    ax, ay, az = names
    nx, ny, nz = sizes
    gx, gy, gz = (lax.axis_index(a) for a in names)
    here = {ax: gx, ay: gy, az: gz}
    count = {ax: nx, ay: ny, az: nz}

    def has(axis, step):
        at = here[axis] + step
        return (at >= 0) & (at < count[axis])

    barrier = pltpu.get_barrier_semaphore()
    place = lax.rem(gx, XROW)
    met = jnp.int32(nz - 1)
    for d in (1, -1, 2, -2, 3, -3):
        known = has(ax, d) & (place + d >= 0) & (place + d < XROW)
        if abs(d) == 1:
            known = has(ax, d)
        met = met + known.astype(jnp.int32)

        @pl.when(known)
        def _(d=d):
            pl.semaphore_signal(barrier, inc=1, device_id={ax: gx + d}, device_id_type=MESH)

    for d in range(-YREACH, YREACH + 1):
        if d:
            met = met + nz * has(ay, d).astype(jnp.int32)

            @pl.when(has(ay, d))
            def _(d=d):
                for rel in range(nz):
                    to = {ay: gy + d, az: lax.rem(gz + rel, nz)}
                    pl.semaphore_signal(barrier, inc=1, device_id=to, device_id_type=MESH)

    for rel in range(1, nz):
        pl.semaphore_signal(barrier, inc=1, device_id={az: lax.rem(gz + rel, nz)}, device_id_type=MESH)

    loads = [pltpu.make_async_copy(a, b, in_sem.at[i]) for i, (a, b) in enumerate(((phase, ph), (conc, co), (factors, factor), (pot, po), (src, so)))]
    for load in loads:
        load.start()

    for axis, bufs in ((ax, (xr1, xr2)), (ay, (yr1, yr3, yr4, yr6, yr7)), (az, (zr1, zr3, zr4, zr6, zr7))):
        for side, d in ((0, -1), (1, 1)):

            @pl.when(jnp.logical_not(has(axis, d)))
            def _(bufs=bufs, side=side):
                for buf in bufs:
                    buf[side] = jnp.zeros(buf.shape[1:], jnp.float32)

    blocks = [(ax, d, qb, XREACH + d) for d in range(-XREACH, XREACH + 1) if d]
    blocks += [(ay, d, gb, YREACH + d) for d in (-1, 1)] + [(ay, d, gh, i) for i, d in enumerate(HALVES)]
    for axis, d, buf, slot in blocks:

        @pl.when(jnp.logical_not(has(axis, d)))
        def _(buf=buf, slot=slot):
            buf[slot] = jnp.zeros(buf.shape[1:], jnp.float32)

    pending = []
    used = [0]

    def fresh(n=1):
        used[0] += n
        return used[0] - n

    def copy(k, a, b, target):
        return pltpu.make_async_remote_copy(
            src_ref=a, dst_ref=b, send_sem=ssem.at[k], recv_sem=rsem.at[k], device_id=target, device_id_type=MESH
        )

    def start(k, a, b, target, when):
        pending.append((k, a, b, target, when))

        @pl.when(when)
        def _():
            copy(k, a, b, target).start()

    def arrived(k, b, when):
        @pl.when(when)
        def _():
            copy(k, b, b, {}).wait_recv()

    def drain(n):
        for k, a, b, target, when in pending[:n]:

            @pl.when(when)
            def _(k=k, a=a, b=b, target=target):
                copy(k, a, b, target).wait_send()

        del pending[:n]

    def push(k, a, b, axis, d):
        start(k, a, b, {axis: here[axis] + d}, has(axis, d))

    def take(k, b, axis, d):
        arrived(k, b, has(axis, d))

    def exchange(axis, sent, got):
        k = fresh(2)
        push(k, sent.at[0], got.at[1], axis, -1)
        push(k + 1, sent.at[1], got.at[0], axis, 1)

        def wait():
            take(k, got.at[1], axis, 1)
            take(k + 1, got.at[0], axis, -1)

        return wait

    class Crossing:
        def __init__(self, sent, got, kept, pieces, lines):
            self.sent, self.got, self.kept, self.pieces, self.lines = sent, got, kept, pieces, lines
            self.whole = fresh(2)
            self.part = fresh(2 * len(pieces))
            self.hop = fresh(2 * len(pieces))
            for side, d in ((0, -1), (1, 1)):
                edge = 0 if side == 0 else XROW - 1
                inside = has(ax, d) & (place != edge)
                leaves = has(ax, d) & (place == edge)
                start(self.whole + side, sent.at[side], got.at[1 - side], {ax: gx + d}, inside)
                for i, piece in enumerate(pieces):
                    line = lines[side][i]
                    if line == edge:
                        start(self.sem(side, i), sent.at[side, piece], got.at[1 - side, piece], {ax: gx + d}, leaves)
                    else:
                        peer = {ax: gx + line - edge}
                        k = self.hop + side * len(pieces) + i
                        start(k, sent.at[side, piece], kept.at[side], peer, leaves)

        def sem(self, side, i):
            return self.part + side * len(self.pieces) + i

        def forward(self):
            for side, d in ((0, -1), (1, 1)):
                edge = 0 if side == 0 else XROW - 1
                to = gx - place + edge + d
                exists = (to >= 0) & (to < nx)
                for i, piece in enumerate(self.pieces):
                    line = self.lines[side][i]
                    if line != edge:
                        mine = exists & (place == line)
                        arrived(self.hop + side * len(self.pieces) + i, self.kept.at[side], mine)
                        start(self.sem(side, i), self.kept.at[side], self.got.at[1 - side, piece], {ax: to}, mine)

        def finish(self):
            for side, d in ((0, -1), (1, 1)):
                edge = 0 if side == 0 else XROW - 1
                arrived(self.whole + 1 - side, self.got.at[side], has(ax, d) & (place != edge))
                for i, piece in enumerate(self.pieces):
                    arrived(self.sem(1 - side, i), self.got.at[side, piece], has(ax, d) & (place == edge))

    sub = lax.broadcasted_iota(jnp.int32, (8, WIDE), 0)
    lane = lax.broadcasted_iota(jnp.int32, (8, WIDE), 1)
    lane1 = lax.broadcasted_iota(jnp.int32, (8, 128), 1)

    def zpack(sent, slabs, stride, unit):
        low = high = jnp.zeros((8, 128), jnp.float32)
        for k, s in enumerate(slabs):
            mine = (lane1 >= unit * k) & (lane1 < unit * (k + 1))
            low = jnp.where(mine, rl(s[:, :128], unit * k), low)
            high = jnp.where(mine, rl(s[:, 128:], unit * k - (128 - stride)), high)
        sent[0] = low
        sent[1] = high

    def zhalo(low, high, k, stride, unit):
        return jnp.concatenate([rl(low, -unit * k), rl(high, 128 - stride - unit * k)], axis=1)

    def ypack_rows(sent, slabs, stride):
        for g in range(sent.shape[1]):
            low = high = jnp.zeros((8, WIDE), jnp.float32)
            for j, s in enumerate(slabs[8 * g : 8 * g + 8]):
                low = jnp.where(sub == j, rs(s, j), low)
                high = jnp.where(sub == j, rs(s, j - (8 - stride)), high)
            sent[0, g] = low
            sent[1, g] = high

    def row(got, side, k):
        return jnp.broadcast_to(got[side, k // 8, k % 8 : k % 8 + 1, :], (8, WIDE))

    loads[0].wait()
    loads[1].wait()
    loads[2].wait()
    loads[3].wait()
    phase_v = ph[...]
    conc_v = co[...]
    lookup = jnp.zeros(phase_v.shape, jnp.float32)
    for i in range(3):
        lookup = lookup + jnp.where(phase_v == i, factor[i], 0.0)
    conduct = lookup * conc_v * jnp.exp(-DECAY * conc_v)
    fine = [jnp.stack([conduct[x]] + [po[f, x] for f in range(FIELDS)]) for x in range(8)]
    ypack_rows(ys1, [fine[x][a] for a in range(4) for x in range(8)], 1)
    zpack(zs1, [fine[x][a] for a in range(4) for x in range(8)], 1, 1)
    xs1[0] = fine[0]
    xs1[1] = fine[7]
    loads[4].wait()

    pl.semaphore_wait(barrier, met)

    wait_y1 = exchange(ay, ys1, yr1)
    wait_z1 = exchange(az, zs1, zr1)
    slabs = [pl.ds(i, 1) for i in range(4)]
    early = Crossing(xs1, xr1, xk1, slabs, ([0, 1, 2, 3], [0, 1, 2, 3]))

    def rest(c):
        return c[0], c[1:]

    def flux(c, v, other):
        face = harmonic(c, other[0])
        return face, face * (v - other[1:])

    inner = []
    for i in range(3):
        a, b = fine[2 * i + 1], fine[2 * i + 2]
        inner.append(flux(a[0], a[1:], b))

    wait_y1()
    wait_z1()
    zlow, zhigh = zr1[0], zr1[1]
    part, ypart, zpart = [], [], []
    for x in range(8):
        c, v = rest(fine[x])
        near = jnp.where(sub % 2 == 0, rs(fine[x], 1), rs(fine[x], -1))
        edge = jnp.stack([jnp.where(sub == 0, row(yr1, 0, a * 8 + x), row(yr1, 1, a * 8 + x)) for a in range(4)])
        near = jnp.where((sub == 0) | (sub == 7), edge, near)
        sy, fy = flux(c, v, near)
        near = jnp.where(lane % 2 == 0, rl(fine[x], 1), rl(fine[x], -1))
        edge = jnp.stack([zhalo(zlow, zhigh, a * 8 + x, 1, 1) for a in range(4)])
        near = jnp.where((lane == 0) | (lane == WIDE - 1), edge, near)
        sz, fz = flux(c, v, near)
        source = jnp.stack([so[f, x] for f in range(FIELDS)])
        part.append(source - MASS * v - fy - fz)
        ypart.append(sy)
        zpart.append(sz)

    def fold(t, stride):
        t = t + rl(t, -stride)
        return t + rs(t, -stride)

    mass1 = MASS * 8.0
    r1, ylo, yhi, zlo, zhi, diag, sx = {}, {}, {}, {}, {}, {}, {}
    for i in range(3):
        sx[i] = fold(inner[i][0], 1)
    for i in range(4):
        t = part[2 * i] + part[2 * i + 1]
        if i < 3:
            t = t - inner[i][1]
        if i > 0:
            t = t + inner[i - 1][1]
        r1[i] = fold(t, 1)
        a = ypart[2 * i] + ypart[2 * i + 1]
        a = a + rl(a, -1)
        ylo[i], yhi[i] = a, rs(a, -1)
        b = zpart[2 * i] + zpart[2 * i + 1]
        b = b + rs(b, -1)
        zlo[i], zhi[i] = b, rl(b, -1)
        d = mass1 + ylo[i] + yhi[i] + zlo[i] + zhi[i]
        if i < 3:
            d = d + sx[i]
        if i > 0:
            d = d + sx[i - 1]
        diag[i] = d

    e0, weight = {}, {}
    for i in (1, 2):
        weight[i] = DAMPING / safe(diag[i])
        e0[i] = weight[i] * r1[i]

    q0 = sub % 2 == 0
    p0 = lane % 2 == 0

    def merge4(a, b, c, d):
        return jnp.where(q0, jnp.where(p0, a, rl(b, 1)), jnp.where(p0, rs(c, 1), rs(rl(d, 1), 1)))

    def split4(m):
        low = rs(m, -1)
        return m, rl(m, -1), low, rl(low, -1)

    for side, (edge, next_to, face) in enumerate(((0, 1, 0), (3, 2, 2))):
        xs2[side, 0] = merge4(e0[next_to][0], e0[next_to][1], e0[next_to][2], diag[edge])
        xs2[side, 1] = merge4(r1[edge][0], r1[edge][1], r1[edge][2], sx[face])
        xs2[side, 2] = merge4(ylo[edge], yhi[edge], zlo[edge], zhi[edge])
    late = Crossing(xs2, xr2, xk2, [pl.ds(0, 2), pl.ds(2, 1)], ([0, 1], [XROW - 1, XROW - 2]))
    early.forward()
    late.forward()
    early.finish()
    for side, edge in ((0, 0), (1, XROW - 1)):
        step = 1 if side == 0 else -1

        @pl.when((place == edge) & has(ax, -step))
        def _(side=side, step=step):
            for i in range(1, XROW):
                pl.semaphore_signal(row_sem.at[side], inc=1, device_id={ax: gx + step * i}, device_id_type=MESH)

    border = {}
    for side, x in ((0, 0), (1, 7)):
        face, out = flux(fine[x][0], fine[x][1:], xr1[side])
        border[side] = (fold(face, 1), fold(out, 1))
    late.finish()
    for side, edge, out, far, own_face, far_face in ((0, 0, -1, -2, -1, -2), (1, 3, 4, 5, 3, 4)):
        face, through = border[side]
        a = split4(xr2[side, 0])
        b = split4(xr2[side, 1])
        c = split4(xr2[side, 2])
        e0[far] = jnp.stack(a[:3])
        r1[out] = jnp.stack(b[:3]) + through
        r1[edge] = r1[edge] - through
        sx[far_face] = b[3]
        sx[own_face] = face
        ylo[out], yhi[out], zlo[out], zhi[out] = c
        diag[out] = a[3] + face
        diag[edge] = diag[edge] + face
        for i in (out, edge):
            weight[i] = DAMPING / safe(diag[i])
            e0[i] = weight[i] * r1[i]

    def halos(got_y, got_z, layers, low, high, i):
        base = layers.index(i) * FIELDS
        ylow = jnp.stack([rl(row(got_y, 0, k // 2), -(k % 2)) for k in range(base, base + FIELDS)])
        yhigh = jnp.stack([rl(row(got_y, 1, k // 2), -(k % 2)) for k in range(base, base + FIELDS)])
        zedge = jnp.stack([zhalo(low, high, base + f, 2, 1) for f in range(FIELDS)])
        return ylow, yhigh, zedge

    def two_by_two(slabs):
        return [jnp.where(p0, a, rl(b, 1)) for a, b in zip(slabs[::2], slabs[1::2])]

    six = [-1, 0, 1, 2, 3, 4]
    slabs = [e0[i][f] for i in six for f in range(FIELDS)]
    ypack_rows(ys3, two_by_two(slabs), 2)
    wait_y = exchange(ay, ys3, yr3)
    zpack(zs3, slabs, 2, 1)
    wait_z = exchange(az, zs3, zr3)
    wait_y()
    wait_z()
    low, high = zr3[0], zr3[1]
    e1 = {}
    for i in six:
        e = e0[i]
        ylow, yhigh, zedge = halos(yr3, zr3, six, low, high, i)
        total = mass1 * e + sx[i - 1] * (e - e0[i - 1]) + sx[i] * (e - e0[i + 1])
        total = total + ylo[i] * (e - jnp.where(sub < 2, ylow, rs(e, 2)))
        total = total + yhi[i] * (e - jnp.where(sub >= 6, yhigh, rs(e, -2)))
        total = total + zlo[i] * (e - jnp.where(lane < 2, zedge, rl(e, 2)))
        total = total + zhi[i] * (e - jnp.where(lane >= WIDE - 2, zedge, rl(e, -2)))
        e1[i] = e + weight[i] * (r1[i] - total)

    four = [0, 1, 2, 3]
    slabs = [e1[i][f] for i in four for f in range(FIELDS)]
    ypack_rows(ys4, two_by_two(slabs), 2)
    wait_y = exchange(ay, ys4, yr4)
    zpack(zs4, slabs, 2, 1)
    wait_z = exchange(az, zs4, zr4)

    mass2 = mass1 * 8.0
    yfirst = sub % 4 < 2
    zfirst = lane % 4 < 2
    yout = {i: jnp.where(yfirst, ylo[i], yhi[i]) for i in four}
    zout = {i: jnp.where(zfirst, zlo[i], zhi[i]) for i in four}
    sx2 = {-1: fold(sx[-1], 2), 0: fold(sx[1], 2), 1: fold(sx[3], 2)}
    ylo2, yhi2, zlo2, zhi2, diag2 = {}, {}, {}, {}, {}
    for i in range(2):
        a = yout[2 * i] + yout[2 * i + 1]
        a = a + rl(a, -2)
        ylo2[i], yhi2[i] = a, rs(a, -2)
        b = zout[2 * i] + zout[2 * i + 1]
        b = b + rs(b, -2)
        zlo2[i], zhi2[i] = b, rl(b, -2)
        diag2[i] = mass2 + sx2[i - 1] + sx2[i] + ylo2[i] + yhi2[i] + zlo2[i] + zhi2[i]

    wait_y()
    wait_z()
    low, high = zr4[0], zr4[1]
    left = {}
    for i in four:
        e = e1[i]
        ylow, yhigh, zedge = halos(yr4, zr4, four, low, high, i)
        across = i - 1 if i % 2 == 0 else i + 1
        near_y = jnp.where(yfirst, jnp.where(sub < 2, ylow, rs(e, 2)), jnp.where(sub >= 6, yhigh, rs(e, -2)))
        near_z = jnp.where(zfirst, rl(e, 2), rl(e, -2))
        near_z = jnp.where((lane < 2) | (lane >= WIDE - 2), zedge, near_z)
        total = mass1 * e + sx[min(i, across)] * (e - e1[across])
        total = total + yout[i] * (e - near_y) + zout[i] * (e - near_z)
        left[i] = r1[i] - total
    r2 = {i: fold(left[2 * i] + left[2 * i + 1], 2) for i in range(2)}

    q4 = sub % 4
    p4 = lane % 4

    def by(which, a, b, c, d):
        return jnp.where(which < 2, jnp.where(which == 0, a, b), jnp.where(which == 2, c, d))

    def rows4(a, b, c, d):
        return by(q4, a, rs(b, 1), rs(c, 2), rs(d, 3))

    block = by(
        p4,
        rows4(r2[0][0], r2[0][1], r2[0][2], diag2[0]),
        rl(rows4(r2[1][0], r2[1][1], r2[1][2], diag2[1]), 1),
        rl(rows4(sx2[0], yhi2[0], zhi2[0], zlo2[0]), 2),
        rl(rows4(sx2[1], yhi2[1], zhi2[1], zlo2[1]), 3),
    )
    qb[XREACH] = block
    old = len(pending)
    direct = fresh(2 * XREACH + 1)
    for side, edge in ((0, 0), (1, XROW - 1)):

        @pl.when((place != edge) & has(ax, XREACH * (2 * side - 1)))
        def _(side=side):
            pl.semaphore_wait(row_sem.at[side], 1)

    for d in (-XREACH, XREACH, 1, -1, 2, -2, 3, -3):
        inside = has(ax, d) if abs(d) == XREACH else has(ax, d) & (place + d >= 0) & (place + d < XROW)
        start(direct + XREACH - d, qb.at[XREACH], qb.at[XREACH - d], {ax: gx + d}, inside)

    drain(old)
    packed = jnp.concatenate([merge4(*(e1[i][f] for i in four)) for f in range(FIELDS)], axis=0)
    r = lax.broadcasted_iota(jnp.int32, (WIDE, WIDE), 0)
    c = lax.broadcasted_iota(jnp.int32, (WIDE, WIDE), 1)
    order = jnp.where(c == (r % 2) * 128 + r // 2, 1.0, 0.0)
    dense = jnp.dot(packed, order, precision=lax.Precision.HIGHEST, preferred_element_type=jnp.float32)
    for f in range(FIELDS):
        for y in range(4):
            for q in range(2):
                for p in range(2):
                    k = f * 8 + 2 * y + q
                    lev_out[f, 2 * q + p, y : y + 1, :] = dense[k : k + 1, 128 * p : 128 * p + 128]

    handed = fresh(2 * XREACH + 1)
    for side in (-1, 1):
        far = XREACH + side * XREACH
        take(direct + far, qb.at[far], ax, side * XREACH)
        for step in range(1, XROW):
            slot = far - side * step
            inside = has(ax, side * XREACH) & (place + side * step >= 0) & (place + side * step < XROW)
            start(handed + slot, qb.at[far], qb.at[slot], {ax: gx + side * step}, inside)
    for side in (-1, 1):
        for step in range(1, XROW):
            slot = XREACH + side * step
            inside = (place + side * step >= 0) & (place + side * step < XROW)
            arrived(direct + slot, qb.at[slot], has(ax, side * step) & inside)
            arrived(handed + slot, qb.at[slot], has(ax, side * step) & jnp.logical_not(inside))

    n2 = 2 * XREACH + 1
    q = qb[...]

    def spread(x, item):
        return jnp.where(q4 == 0, rs(x, -item), jnp.where(q4 == 1, rs(x, 1 - item), rs(x, 2 - item)))

    layer0 = p4 == 0
    weight2 = DAMPING / safe(spread(q, 3))
    coef = rl(q, -2)
    xhi, yhi_, zhi_, zlo_ = (spread(coef, item) for item in range(4))
    e = weight2 * q

    def below(x):
        return jnp.concatenate([x[:1], x[:-1]], axis=0)

    def above(x):
        return jnp.concatenate([x[1:], x[-1:]], axis=0)

    def next_x(x):
        return jnp.where(layer0, rl(x, -1), above(rl(x, 1)))

    def last_x(x):
        return jnp.where(layer0, below(rl(x, -1)), rl(x, 1))

    def ypack_halves(sent, x):
        low, high = [], []
        for m in range(0, x.shape[0], 2):
            a, b = x[m], x[min(m + 1, x.shape[0] - 1)]
            low.append(jnp.where(sub < 4, a, rs(b, 4)))
            high.append(jnp.where(sub < 4, rs(a, 4), b))
        for side, h in ((0, low), (1, high)):
            for g in range(sent.shape[1]):
                sent[side, g] = jnp.where(p4 < 2, h[2 * g], rl(h[min(2 * g + 1, len(h) - 1)], 2))

    def yedges(got, n):
        out = []
        for d in range(n):
            low, high = (rl(got[side, d // 4], -2 * (d // 2 % 2)) for side in (0, 1))
            if d % 2 == 0:
                out.append(jnp.where(sub < 4, low, rs(high, 4)))
            else:
                out.append(jnp.where(sub < 4, rs(low, 4), high))
        return jnp.stack(out)

    def zedges(got, n):
        low, high = got[0], got[1]
        return jnp.stack([zhalo(low, high, d, 4, 4) for d in range(n)])

    ypack_halves(ys6, jnp.where(q4 == 3, rs(coef, 2), e))
    wait_y = exchange(ay, ys6, yr6)
    zpack(zs6, [e[d] for d in range(n2)], 4, 4)
    wait_z = exchange(az, zs6, zr6)
    xlo = last_x(xhi)
    near = xlo * (e - last_x(e)) + xhi * (e - next_x(e)) + mass2 * e
    wait_y()
    wait_z()
    edge = yedges(yr6, n2)
    zedge = zedges(zr6, n2)
    ylo_ = jnp.where(sub < 4, spread(edge, 3), rs(yhi_, 4))
    other = rs(e, 4)
    total = near + ylo_ * (e - jnp.where(sub < 4, edge, other)) + yhi_ * (e - jnp.where(sub < 4, other, edge))
    total = total + zlo_ * (e - jnp.where(lane < 4, zedge, rl(e, 4)))
    total = total + zhi_ * (e - jnp.where(lane >= WIDE - 4, zedge, rl(e, -4)))
    e = e + weight2 * (q - total)

    n3 = n2 - 2
    ypack_halves(ys7, e[1:-1])
    wait_y = exchange(ay, ys7, yr7)
    zpack(zs7, [e[d] for d in range(1, n2 - 1)], 4, 4)
    wait_z = exchange(az, zs7, zr7)

    mass3 = mass2 * 8.0
    zfirst = lane % 8 < 4
    xout = jnp.where(layer0, xlo, xhi)[1:-1]
    yout = jnp.where(sub < 4, ylo_, yhi_)[1:-1]
    zout = jnp.where(zfirst, zlo_, zhi_)[1:-1]
    a = xout + rs(xout, 4)
    a = a + rl(a, -4)
    xlo3, xhi3 = a, rl(a, -1)
    a = yout + rl(yout, -1)
    a = a + rl(a, -4)
    ylo3, yhi3 = a, rs(a, 4)
    a = zout + rl(zout, -1)
    a = a + rs(a, 4)
    zlo3, zhi3 = a, rl(a, -4)
    diag3 = mass3 + xlo3 + xhi3 + ylo3 + yhi3 + zlo3 + zhi3
    near_x = jnp.where(layer0, last_x(e), next_x(e))[1:-1]
    e = e[1:-1]
    near_z = jnp.where(zfirst, rl(e, 4), rl(e, -4))
    partial = q[1:-1] - mass2 * e - xout * (e - near_x)
    coefs = jnp.where(sub == 3, rs(diag3, 3), jnp.where(sub == 4, rs(xhi3, 4), jnp.where(sub == 5, rs(yhi3, 5), rs(zhi3, 6))))
    wait_y()
    wait_z()
    edge = yedges(yr7, n3)
    zedge = zedges(zr7, n3)
    near_z = jnp.where((lane < 4) | (lane >= WIDE - 4), zedge, near_z)
    t = partial - yout * (e - edge) - zout * (e - near_z)
    t = t + rl(t, -1)
    t = t + rs(t, 4)
    t = t + rl(t, -4)
    t = jnp.where(sub < 3, t, coefs)
    block = jnp.zeros((8, WIDE), jnp.float32)
    for l in range(n3):
        block = jnp.where((lane % 8 == l) & (sub < 7), rl(t[l], l), block)

    def column(slot, at):
        return gb.at[slot, :, pl.ds(pl.multiple_of(at * WIDE, WIDE), WIDE)]

    def half(slot, at):
        return gh.at[slot, :, pl.ds(pl.multiple_of(at * 128, 128), 128)]

    gb[YREACH, :, pl.ds(pl.multiple_of(gz * WIDE, WIDE), WIDE)] = block
    third = lane1 % 8
    hs[...] = jnp.where(third < 3, rl(block[:, :128], -2), jnp.where(third < 6, rl(block[:, 128:], 1), 0.0))
    first = fresh((2 * YREACH + 1) * nz)
    old = len(pending)
    others = [(d, rel) for d in sorted(range(-YREACH, YREACH + 1), key=abs) for rel in range(nz) if d or rel]
    for d, rel in others:
        k = first + (YREACH - d) * nz + rel
        to = {ay: gy + d, az: lax.rem(gz + rel, nz)}
        if d in HALVES:
            start(k, hs, half(HALVES.index(-d), gz), to, has(ay, d))
        else:
            start(k, column(YREACH, gz), column(YREACH - d, gz), to, has(ay, d))
    drain(old)
    for d, rel in others:
        k = first + (YREACH - d) * nz + rel
        back = lax.rem(gz + nz - rel, nz)
        arrived(k, half(HALVES.index(-d), back) if d in HALVES else column(YREACH - d, back), has(ay, -d))
    middle = (third >= 2) & (third < 5)
    for i, d in enumerate(HALVES):
        for at in range(nz):
            m = gh[i, :, 128 * at : 128 * at + 128]
            gb[YREACH + d, :, WIDE * at : WIDE * at + 128] = jnp.where(middle, rl(m, 2), 0.0)
            gb[YREACH + d, :, WIDE * at + 128 : WIDE * at + 256] = jnp.where(middle, rl(m, -1), 0.0)

    full = (8, WIDE * nz)
    n = 2 * YREACH + 1

    def coefficient(j, item):
        return jnp.broadcast_to(gb[j, item : item + 1, :], full)

    r3 = [gb[j] for j in range(n)]
    w3 = [DAMPING / safe(coefficient(j, 3)) for j in range(n)]
    e = {j: w3[j] * r3[j] for j in range(n)}
    xhi = {j: coefficient(j, 4) for j in range(1, n - 1)}
    yhi = {j: coefficient(j, 5) for j in range(n - 1)}
    zhi = {j: coefficient(j, 6) for j in range(1, n - 1)}
    xlo = {j: rl(xhi[j], 1) for j in xhi}
    zlo = {j: rl(zhi[j], 8) for j in zhi}
    for sweep in range(1, YREACH + 1):
        new = {}
        for j in range(sweep, n - sweep):
            v = e[j]
            total = mass3 * v + xlo[j] * (v - rl(v, 1)) + xhi[j] * (v - rl(v, -1))
            total = total + yhi[j - 1] * (v - e[j - 1]) + yhi[j] * (v - e[j + 1])
            total = total + zlo[j] * (v - rl(v, 8)) + zhi[j] * (v - rl(v, -8))
            new[j] = v + w3[j] * (r3[j] - total)
        e = new
    own = e[YREACH]
    tile = jnp.zeros((8, 128), jnp.float32)
    for t in range(2 * nz):
        tile = jnp.where(lane1 % 8 == t, rl(own[:, 128 * t : 128 * t + 128], t - XREACH + 1), tile)
    r = lax.broadcasted_iota(jnp.int32, (128, 32 * nz), 0)
    c = lax.broadcasted_iota(jnp.int32, (128, 32 * nz), 1)
    order = jnp.where(c == (r % 8) * 16 + r // 8, 1.0, 0.0)
    dense = jnp.dot(tile, order, precision=lax.Precision.HIGHEST, preferred_element_type=jnp.float32)
    for f in range(FIELDS):
        coarse_out[f, 0, :, :] = dense[f : f + 1, :]

    drain(len(pending))


def solution(mesh):
    names = mesh.axis_names
    sizes = tuple(mesh.shape[a] for a in names)
    nz = sizes[2]
    f32 = jnp.float32

    def both(*shape):
        return [pltpu.VMEM((2, *shape), f32)] * 2

    scratch = [
        pltpu.VMEM((8, 8, WIDE), jnp.int32),
        pltpu.VMEM((8, 8, WIDE), f32),
        pltpu.VMEM((FIELDS, 8, 8, WIDE), f32),
        pltpu.VMEM((FIELDS, 8, 8, WIDE), f32),
        pltpu.SemaphoreType.DMA((5,)),
        *both(4, 8, WIDE), *both(8, 128),
        *both(4, 8, WIDE), pltpu.VMEM((2, 1, 8, WIDE), f32), *both(3, 8, WIDE), pltpu.VMEM((2, 1, 8, WIDE), f32),
        *both(2, 8, WIDE), *both(8, 128),
        *both(1, 8, WIDE), *both(8, 128),
        pltpu.VMEM((2 * XREACH + 1, 8, WIDE), f32),
        *both(3, 8, WIDE), *both(8, 128),
        *both(2, 8, WIDE), *both(8, 128),
        pltpu.VMEM((2 * YREACH + 1, 8, WIDE * nz), f32),
        pltpu.VMEM((len(HALVES), 8, 128 * nz), f32),
        pltpu.VMEM((8, 128), f32),
        pltpu.SMEM((3,), f32),
    ]
    sems = 2 * 2 * 5 + (2 + 16) + (2 + 8) + 2 * (2 * XREACH + 1) + (2 * YREACH + 1) * nz
    scratch += [pltpu.SemaphoreType.REGULAR((2,)), pltpu.SemaphoreType.DMA((sems,)), pltpu.SemaphoreType.DMA((sems,))]

    def local(phase_label, concentration, phase_factor, potential, source):
        return pl.pallas_call(
            functools.partial(kernel, names, sizes),
            out_shape=(
                jax.ShapeDtypeStruct((FIELDS, 4, 4, 128), f32),
                jax.ShapeDtypeStruct((FIELDS, 1, 1, 32 * nz), f32),
            ),
            in_specs=[pl.BlockSpec(memory_space=pltpu.HBM)] * 5,
            out_specs=(pl.BlockSpec(memory_space=pltpu.VMEM), pl.BlockSpec(memory_space=pltpu.VMEM)),
            scratch_shapes=scratch,
            compiler_params=pltpu.CompilerParams(collective_id=0, has_side_effects=True, vmem_limit_bytes=55168 << 10),
        )(phase_label, concentration, potential, source, phase_factor)

    return jax.shard_map(
        local,
        mesh=mesh,
        in_specs=(P(*names), P(*names), P(), P(None, *names), P(None, *names)),
        out_specs=(P(None, *names), P(None, names[0], names[1], None)),
        check_vma=False,
    )
```

```python
import functools

import jax
import jax.numpy as jnp
from jax import lax
from jax.experimental import pallas as pl
from jax.experimental.pallas import tpu as pltpu
from jax.sharding import PartitionSpec as P

MESH = pl.DeviceIdType.MESH
FIELDS = 3
MASS = 0.05
DAMPING = 0.7
DECAY = 0.3
XREACH = 4
YREACH = 3
WIDE = 256
HALVES = (-3, -2, 2, 3)
XROW = 4


def rs(x, k):
    k %= x.shape[-2]
    return pltpu.roll(x, k, x.ndim - 2) if k else x


def rl(x, k):
    k %= x.shape[-1]
    return pltpu.roll(x, k, x.ndim - 1) if k else x


def harmonic(a, b):
    return 2.0 * a * b / (a + b)


def safe(d):
    return jnp.where(d > 0.0, d, 1.0)


def kernel(names, sizes, phase, conc, pot, src, factors, lev_out, coarse_out, *scratch):
    (ph, co, po, so, in_sem, ys1, yr1, zs1, zr1, xs1, xr1, xk1, xs2, xr2, xk2, ys3, yr3, zs3, zr3, ys4, yr4, zs4, zr4,
     qb, ys6, yr6, zs6, zr6, ys7, yr7, zs7, zr7, gb, gh, hs, factor, row_sem, ssem, rsem) = scratch
    ax, ay, az = names
    nx, ny, nz = sizes
    gx, gy, gz = (lax.axis_index(a) for a in names)
    here = {ax: gx, ay: gy, az: gz}
    count = {ax: nx, ay: ny, az: nz}

    known_steps = {}

    def has(axis, step):
        if (axis, step) not in known_steps:
            at = here[axis] + step
            known_steps[axis, step] = (at >= 0) & (at < count[axis])
        return known_steps[axis, step]

    barrier = pltpu.get_barrier_semaphore()
    place = lax.rem(gx, XROW)
    met = jnp.int32(nz - 1)
    for d in (1, -1, 2, -2, 3, -3):
        known = has(ax, d) & (place + d >= 0) & (place + d < XROW)
        if abs(d) == 1:
            known = has(ax, d)
        met = met + known.astype(jnp.int32)

        @pl.when(known)
        def _(d=d):
            pl.semaphore_signal(barrier, inc=1, device_id={ax: gx + d}, device_id_type=MESH)

    for d in range(-YREACH, YREACH + 1):
        if d:
            met = met + nz * has(ay, d).astype(jnp.int32)

            @pl.when(has(ay, d))
            def _(d=d):
                for rel in range(nz):
                    to = {ay: gy + d, az: lax.rem(gz + rel, nz)}
                    pl.semaphore_signal(barrier, inc=1, device_id=to, device_id_type=MESH)

    for rel in range(1, nz):
        pl.semaphore_signal(barrier, inc=1, device_id={az: lax.rem(gz + rel, nz)}, device_id_type=MESH)

    loads = [pltpu.make_async_copy(a, b, in_sem.at[i]) for i, (a, b) in enumerate(((phase, ph), (conc, co), (factors, factor), (pot, po), (src, so)))]
    for load in loads:
        load.start()

    for axis, bufs in ((ax, (xr1, xr2)), (ay, (yr1, yr3, yr4, yr6, yr7)), (az, (zr1, zr3, zr4, zr6, zr7))):
        for side, d in ((0, -1), (1, 1)):

            @pl.when(jnp.logical_not(has(axis, d)))
            def _(bufs=bufs, side=side):
                for buf in bufs:
                    buf[side] = jnp.zeros(buf.shape[1:], jnp.float32)

    blocks = [(ax, d, qb, XREACH + d) for d in range(-XREACH, XREACH + 1) if d]
    blocks += [(ay, d, gb, YREACH + d) for d in (-1, 1)] + [(ay, d, gh, i) for i, d in enumerate(HALVES)]
    for axis, d, buf, slot in blocks:

        @pl.when(jnp.logical_not(has(axis, d)))
        def _(buf=buf, slot=slot):
            buf[slot] = jnp.zeros(buf.shape[1:], jnp.float32)

    pending = []
    used = [0]

    def fresh(n=1):
        used[0] += n
        return used[0] - n

    def copy(k, a, b, target):
        return pltpu.make_async_remote_copy(
            src_ref=a, dst_ref=b, send_sem=ssem.at[k], recv_sem=rsem.at[k], device_id=target, device_id_type=MESH
        )

    def start(copies, when):
        pending.append((copies, when))

        @pl.when(when)
        def _():
            for c in copies:
                copy(*c).start()

    def arrived(copies, when):
        @pl.when(when)
        def _():
            for k, b in copies:
                copy(k, b, b, {}).wait_recv()

    def drain(n):
        groups = {}
        for copies, when in pending[:n]:
            groups.setdefault(id(when), (when, []))[1].extend(copies)
        for when, copies in groups.values():

            @pl.when(when)
            def _(copies=copies):
                for c in copies:
                    copy(*c).wait_send()

        del pending[:n]

    def push(k, a, b, axis, d):
        start([(k, a, b, {axis: here[axis] + d})], has(axis, d))

    def take(k, b, axis, d):
        arrived([(k, b)], has(axis, d))

    def exchange(axis, sent, got):
        k = fresh(2)
        push(k, sent.at[0], got.at[1], axis, -1)
        push(k + 1, sent.at[1], got.at[0], axis, 1)

        def wait():
            take(k, got.at[1], axis, 1)
            take(k + 1, got.at[0], axis, -1)

        return wait

    class Crossing:
        def __init__(self, sent, got, kept, pieces, lines):
            self.sent, self.got, self.kept, self.pieces, self.lines = sent, got, kept, pieces, lines
            self.whole = fresh(2)
            self.part = fresh(2 * len(pieces))
            self.hop = fresh(2 * len(pieces))
            for side, d in ((0, -1), (1, 1)):
                edge = 0 if side == 0 else XROW - 1
                inside = has(ax, d) & (place != edge)
                leaves = has(ax, d) & (place == edge)
                start([(self.whole + side, sent.at[side], got.at[1 - side], {ax: gx + d})], inside)
                copies = []
                for i, piece in enumerate(pieces):
                    line = lines[side][i]
                    if line == edge:
                        copies.append((self.sem(side, i), sent.at[side, piece], got.at[1 - side, piece], {ax: gx + d}))
                    else:
                        k = self.hop + side * len(pieces) + i
                        copies.append((k, sent.at[side, piece], kept.at[side], {ax: gx + line - edge}))
                start(copies, leaves)

        def sem(self, side, i):
            return self.part + side * len(self.pieces) + i

        def forward(self):
            for side, d in ((0, -1), (1, 1)):
                edge = 0 if side == 0 else XROW - 1
                to = gx - place + edge + d
                exists = (to >= 0) & (to < nx)
                for i, piece in enumerate(self.pieces):
                    line = self.lines[side][i]
                    if line != edge:
                        mine = exists & (place == line)
                        arrived([(self.hop + side * len(self.pieces) + i, self.kept.at[side])], mine)
                        start([(self.sem(side, i), self.kept.at[side], self.got.at[1 - side, piece], {ax: to})], mine)

        def finish(self):
            for side, d in ((0, -1), (1, 1)):
                edge = 0 if side == 0 else XROW - 1
                arrived([(self.whole + 1 - side, self.got.at[side])], has(ax, d) & (place != edge))
                parts = [(self.sem(1 - side, i), self.got.at[side, piece]) for i, piece in enumerate(self.pieces)]
                arrived(parts, has(ax, d) & (place == edge))

    sub = lax.broadcasted_iota(jnp.int32, (8, WIDE), 0)
    lane = lax.broadcasted_iota(jnp.int32, (8, WIDE), 1)
    lane1 = lax.broadcasted_iota(jnp.int32, (8, 128), 1)

    def zpack(sent, slabs, stride, unit):
        low = high = jnp.zeros((8, 128), jnp.float32)
        for k, s in enumerate(slabs):
            mine = (lane1 >= unit * k) & (lane1 < unit * (k + 1))
            low = jnp.where(mine, rl(s[:, :128], unit * k), low)
            high = jnp.where(mine, rl(s[:, 128:], unit * k - (128 - stride)), high)
        sent[0] = low
        sent[1] = high

    def zhalo(low, high, k, stride, unit):
        return jnp.concatenate([rl(low, -unit * k), rl(high, 128 - stride - unit * k)], axis=1)

    def ypack_rows(sent, slabs, stride):
        for g in range(sent.shape[1]):
            low = high = jnp.zeros((8, WIDE), jnp.float32)
            for j, s in enumerate(slabs[8 * g : 8 * g + 8]):
                low = jnp.where(sub == j, rs(s, j), low)
                high = jnp.where(sub == j, rs(s, j - (8 - stride)), high)
            sent[0, g] = low
            sent[1, g] = high

    def row(got, side, k):
        return jnp.broadcast_to(got[side, k // 8, k % 8 : k % 8 + 1, :], (8, WIDE))

    loads[0].wait()
    loads[1].wait()
    loads[2].wait()
    loads[3].wait()
    phase_v = ph[...]
    conc_v = co[...]
    lookup = jnp.zeros(phase_v.shape, jnp.float32)
    for i in range(3):
        lookup = lookup + jnp.where(phase_v == i, factor[i], 0.0)
    conduct = lookup * conc_v * jnp.exp(-DECAY * conc_v)
    fine = [jnp.stack([conduct[x]] + [po[f, x] for f in range(FIELDS)]) for x in range(8)]
    ypack_rows(ys1, [fine[x][a] for a in range(4) for x in range(8)], 1)
    zpack(zs1, [fine[x][a] for a in range(4) for x in range(8)], 1, 1)
    xs1[0] = fine[0]
    xs1[1] = fine[7]
    loads[4].wait()

    pl.semaphore_wait(barrier, met)

    wait_y1 = exchange(ay, ys1, yr1)
    wait_z1 = exchange(az, zs1, zr1)
    slabs = [pl.ds(i, 1) for i in range(4)]
    early = Crossing(xs1, xr1, xk1, slabs, ([0, 1, 2, 3], [0, 1, 2, 3]))

    def rest(c):
        return c[0], c[1:]

    def flux(c, v, other):
        face = harmonic(c, other[0])
        return face, face * (v - other[1:])

    inner = []
    for i in range(3):
        a, b = fine[2 * i + 1], fine[2 * i + 2]
        inner.append(flux(a[0], a[1:], b))

    wait_y1()
    wait_z1()
    zlow, zhigh = zr1[0], zr1[1]
    part, ypart, zpart = [], [], []
    for x in range(8):
        c, v = rest(fine[x])
        near = jnp.where(sub % 2 == 0, rs(fine[x], 1), rs(fine[x], -1))
        edge = jnp.stack([jnp.where(sub == 0, row(yr1, 0, a * 8 + x), row(yr1, 1, a * 8 + x)) for a in range(4)])
        near = jnp.where((sub == 0) | (sub == 7), edge, near)
        sy, fy = flux(c, v, near)
        near = jnp.where(lane % 2 == 0, rl(fine[x], 1), rl(fine[x], -1))
        edge = jnp.stack([zhalo(zlow, zhigh, a * 8 + x, 1, 1) for a in range(4)])
        near = jnp.where((lane == 0) | (lane == WIDE - 1), edge, near)
        sz, fz = flux(c, v, near)
        source = jnp.stack([so[f, x] for f in range(FIELDS)])
        part.append(source - MASS * v - fy - fz)
        ypart.append(sy)
        zpart.append(sz)

    def fold(t, stride):
        t = t + rl(t, -stride)
        return t + rs(t, -stride)

    mass1 = MASS * 8.0
    r1, ylo, yhi, zlo, zhi, diag, sx = {}, {}, {}, {}, {}, {}, {}
    for i in range(3):
        sx[i] = fold(inner[i][0], 1)
    for i in range(4):
        t = part[2 * i] + part[2 * i + 1]
        if i < 3:
            t = t - inner[i][1]
        if i > 0:
            t = t + inner[i - 1][1]
        r1[i] = fold(t, 1)
        a = ypart[2 * i] + ypart[2 * i + 1]
        a = a + rl(a, -1)
        ylo[i], yhi[i] = a, rs(a, -1)
        b = zpart[2 * i] + zpart[2 * i + 1]
        b = b + rs(b, -1)
        zlo[i], zhi[i] = b, rl(b, -1)
        d = mass1 + ylo[i] + yhi[i] + zlo[i] + zhi[i]
        if i < 3:
            d = d + sx[i]
        if i > 0:
            d = d + sx[i - 1]
        diag[i] = d

    e0, weight = {}, {}
    for i in (1, 2):
        weight[i] = DAMPING / safe(diag[i])
        e0[i] = weight[i] * r1[i]

    q0 = sub % 2 == 0
    p0 = lane % 2 == 0

    def merge4(a, b, c, d):
        return jnp.where(q0, jnp.where(p0, a, rl(b, 1)), jnp.where(p0, rs(c, 1), rs(rl(d, 1), 1)))

    def split4(m):
        low = rs(m, -1)
        return m, rl(m, -1), low, rl(low, -1)

    for side, (edge, next_to, face) in enumerate(((0, 1, 0), (3, 2, 2))):
        xs2[side, 0] = merge4(e0[next_to][0], e0[next_to][1], e0[next_to][2], diag[edge])
        xs2[side, 1] = merge4(r1[edge][0], r1[edge][1], r1[edge][2], sx[face])
        xs2[side, 2] = merge4(ylo[edge], yhi[edge], zlo[edge], zhi[edge])
    late = Crossing(xs2, xr2, xk2, [pl.ds(0, 2), pl.ds(2, 1)], ([0, 1], [XROW - 1, XROW - 2]))
    early.forward()
    late.forward()
    early.finish()
    for side, edge in ((0, 0), (1, XROW - 1)):
        step = 1 if side == 0 else -1

        @pl.when((place == edge) & has(ax, -step))
        def _(side=side, step=step):
            for i in range(1, XROW):
                pl.semaphore_signal(row_sem.at[side], inc=1, device_id={ax: gx + step * i}, device_id_type=MESH)

    border = {}
    for side, x in ((0, 0), (1, 7)):
        face, out = flux(fine[x][0], fine[x][1:], xr1[side])
        border[side] = (fold(face, 1), fold(out, 1))
    late.finish()
    for side, edge, out, far, own_face, far_face in ((0, 0, -1, -2, -1, -2), (1, 3, 4, 5, 3, 4)):
        face, through = border[side]
        a = split4(xr2[side, 0])
        b = split4(xr2[side, 1])
        c = split4(xr2[side, 2])
        e0[far] = jnp.stack(a[:3])
        r1[out] = jnp.stack(b[:3]) + through
        r1[edge] = r1[edge] - through
        sx[far_face] = b[3]
        sx[own_face] = face
        ylo[out], yhi[out], zlo[out], zhi[out] = c
        diag[out] = a[3] + face
        diag[edge] = diag[edge] + face
        for i in (out, edge):
            weight[i] = DAMPING / safe(diag[i])
            e0[i] = weight[i] * r1[i]

    def halos(got_y, got_z, layers, low, high, i):
        base = layers.index(i) * FIELDS
        ylow = jnp.stack([rl(row(got_y, 0, k // 2), -(k % 2)) for k in range(base, base + FIELDS)])
        yhigh = jnp.stack([rl(row(got_y, 1, k // 2), -(k % 2)) for k in range(base, base + FIELDS)])
        zedge = jnp.stack([zhalo(low, high, base + f, 2, 1) for f in range(FIELDS)])
        return ylow, yhigh, zedge

    def two_by_two(slabs):
        return [jnp.where(p0, a, rl(b, 1)) for a, b in zip(slabs[::2], slabs[1::2])]

    six = [-1, 0, 1, 2, 3, 4]
    slabs = [e0[i][f] for i in six for f in range(FIELDS)]
    ypack_rows(ys3, two_by_two(slabs), 2)
    wait_y = exchange(ay, ys3, yr3)
    zpack(zs3, slabs, 2, 1)
    wait_z = exchange(az, zs3, zr3)
    wait_y()
    wait_z()
    low, high = zr3[0], zr3[1]
    e1 = {}
    for i in six:
        e = e0[i]
        ylow, yhigh, zedge = halos(yr3, zr3, six, low, high, i)
        total = mass1 * e + sx[i - 1] * (e - e0[i - 1]) + sx[i] * (e - e0[i + 1])
        total = total + ylo[i] * (e - jnp.where(sub < 2, ylow, rs(e, 2)))
        total = total + yhi[i] * (e - jnp.where(sub >= 6, yhigh, rs(e, -2)))
        total = total + zlo[i] * (e - jnp.where(lane < 2, zedge, rl(e, 2)))
        total = total + zhi[i] * (e - jnp.where(lane >= WIDE - 2, zedge, rl(e, -2)))
        e1[i] = e + weight[i] * (r1[i] - total)

    four = [0, 1, 2, 3]
    slabs = [e1[i][f] for i in four for f in range(FIELDS)]
    ypack_rows(ys4, two_by_two(slabs), 2)
    wait_y = exchange(ay, ys4, yr4)
    zpack(zs4, slabs, 2, 1)
    wait_z = exchange(az, zs4, zr4)

    mass2 = mass1 * 8.0
    yfirst = sub % 4 < 2
    zfirst = lane % 4 < 2
    yout = {i: jnp.where(yfirst, ylo[i], yhi[i]) for i in four}
    zout = {i: jnp.where(zfirst, zlo[i], zhi[i]) for i in four}
    sx2 = {-1: fold(sx[-1], 2), 0: fold(sx[1], 2), 1: fold(sx[3], 2)}
    ylo2, yhi2, zlo2, zhi2, diag2 = {}, {}, {}, {}, {}
    for i in range(2):
        a = yout[2 * i] + yout[2 * i + 1]
        a = a + rl(a, -2)
        ylo2[i], yhi2[i] = a, rs(a, -2)
        b = zout[2 * i] + zout[2 * i + 1]
        b = b + rs(b, -2)
        zlo2[i], zhi2[i] = b, rl(b, -2)
        diag2[i] = mass2 + sx2[i - 1] + sx2[i] + ylo2[i] + yhi2[i] + zlo2[i] + zhi2[i]

    wait_y()
    wait_z()
    low, high = zr4[0], zr4[1]
    left = {}
    for i in four:
        e = e1[i]
        ylow, yhigh, zedge = halos(yr4, zr4, four, low, high, i)
        across = i - 1 if i % 2 == 0 else i + 1
        near_y = jnp.where(yfirst, jnp.where(sub < 2, ylow, rs(e, 2)), jnp.where(sub >= 6, yhigh, rs(e, -2)))
        near_z = jnp.where(zfirst, rl(e, 2), rl(e, -2))
        near_z = jnp.where((lane < 2) | (lane >= WIDE - 2), zedge, near_z)
        total = mass1 * e + sx[min(i, across)] * (e - e1[across])
        total = total + yout[i] * (e - near_y) + zout[i] * (e - near_z)
        left[i] = r1[i] - total
    r2 = {i: fold(left[2 * i] + left[2 * i + 1], 2) for i in range(2)}

    q4 = sub % 4
    p4 = lane % 4

    def by(which, a, b, c, d):
        return jnp.where(which < 2, jnp.where(which == 0, a, b), jnp.where(which == 2, c, d))

    def rows4(a, b, c, d):
        return by(q4, a, rs(b, 1), rs(c, 2), rs(d, 3))

    block = by(
        p4,
        rows4(r2[0][0], r2[0][1], r2[0][2], diag2[0]),
        rl(rows4(r2[1][0], r2[1][1], r2[1][2], diag2[1]), 1),
        rl(rows4(sx2[0], yhi2[0], zhi2[0], zlo2[0]), 2),
        rl(rows4(sx2[1], yhi2[1], zhi2[1], zlo2[1]), 3),
    )
    qb[XREACH] = block
    old = len(pending)
    direct = fresh(2 * XREACH + 1)
    for side, edge in ((0, 0), (1, XROW - 1)):

        @pl.when((place != edge) & has(ax, XREACH * (2 * side - 1)))
        def _(side=side):
            pl.semaphore_wait(row_sem.at[side], 1)

    for d in (-XREACH, XREACH, 1, -1, 2, -2, 3, -3):
        inside = has(ax, d) if abs(d) == XREACH else has(ax, d) & (place + d >= 0) & (place + d < XROW)
        start([(direct + XREACH - d, qb.at[XREACH], qb.at[XREACH - d], {ax: gx + d})], inside)

    drain(old)
    packed = jnp.concatenate([merge4(*(e1[i][f] for i in four)) for f in range(FIELDS)], axis=0)
    r = lax.broadcasted_iota(jnp.int32, (WIDE, WIDE), 0)
    c = lax.broadcasted_iota(jnp.int32, (WIDE, WIDE), 1)
    order = jnp.where(c == (r % 2) * 128 + r // 2, 1.0, 0.0)
    dense = jnp.dot(packed, order, precision=lax.Precision.HIGHEST, preferred_element_type=jnp.float32)
    for f in range(FIELDS):
        for y in range(4):
            for q in range(2):
                for p in range(2):
                    k = f * 8 + 2 * y + q
                    lev_out[f, 2 * q + p, y : y + 1, :] = dense[k : k + 1, 128 * p : 128 * p + 128]

    handed = fresh(2 * XREACH + 1)
    for side in (-1, 1):
        far = XREACH + side * XREACH
        take(direct + far, qb.at[far], ax, side * XREACH)
        for step in range(1, XROW):
            slot = far - side * step
            inside = has(ax, side * XREACH) & (place + side * step >= 0) & (place + side * step < XROW)
            start([(handed + slot, qb.at[far], qb.at[slot], {ax: gx + side * step})], inside)
    for side in (-1, 1):
        for step in range(1, XROW):
            slot = XREACH + side * step
            inside = (place + side * step >= 0) & (place + side * step < XROW)
            arrived([(direct + slot, qb.at[slot])], has(ax, side * step) & inside)
            arrived([(handed + slot, qb.at[slot])], has(ax, side * step) & jnp.logical_not(inside))

    n2 = 2 * XREACH + 1
    q = qb[...]

    def spread(x, item):
        return jnp.where(q4 == 0, rs(x, -item), jnp.where(q4 == 1, rs(x, 1 - item), rs(x, 2 - item)))

    layer0 = p4 == 0
    weight2 = DAMPING / safe(spread(q, 3))
    coef = rl(q, -2)
    xhi, yhi_, zhi_, zlo_ = (spread(coef, item) for item in range(4))
    e = weight2 * q

    def below(x):
        return jnp.concatenate([x[:1], x[:-1]], axis=0)

    def above(x):
        return jnp.concatenate([x[1:], x[-1:]], axis=0)

    def next_x(x):
        return jnp.where(layer0, rl(x, -1), above(rl(x, 1)))

    def last_x(x):
        return jnp.where(layer0, below(rl(x, -1)), rl(x, 1))

    def ypack_halves(sent, x):
        low, high = [], []
        for m in range(0, x.shape[0], 2):
            a, b = x[m], x[min(m + 1, x.shape[0] - 1)]
            low.append(jnp.where(sub < 4, a, rs(b, 4)))
            high.append(jnp.where(sub < 4, rs(a, 4), b))
        for side, h in ((0, low), (1, high)):
            for g in range(sent.shape[1]):
                sent[side, g] = jnp.where(p4 < 2, h[2 * g], rl(h[min(2 * g + 1, len(h) - 1)], 2))

    def yedges(got, n):
        out = []
        for d in range(n):
            low, high = (rl(got[side, d // 4], -2 * (d // 2 % 2)) for side in (0, 1))
            if d % 2 == 0:
                out.append(jnp.where(sub < 4, low, rs(high, 4)))
            else:
                out.append(jnp.where(sub < 4, rs(low, 4), high))
        return jnp.stack(out)

    def zedges(got, n):
        low, high = got[0], got[1]
        return jnp.stack([zhalo(low, high, d, 4, 4) for d in range(n)])

    ypack_halves(ys6, jnp.where(q4 == 3, rs(coef, 2), e))
    wait_y = exchange(ay, ys6, yr6)
    zpack(zs6, [e[d] for d in range(n2)], 4, 4)
    wait_z = exchange(az, zs6, zr6)
    xlo = last_x(xhi)
    near = xlo * (e - last_x(e)) + xhi * (e - next_x(e)) + mass2 * e
    wait_y()
    wait_z()
    edge = yedges(yr6, n2)
    zedge = zedges(zr6, n2)
    ylo_ = jnp.where(sub < 4, spread(edge, 3), rs(yhi_, 4))
    other = rs(e, 4)
    total = near + ylo_ * (e - jnp.where(sub < 4, edge, other)) + yhi_ * (e - jnp.where(sub < 4, other, edge))
    total = total + zlo_ * (e - jnp.where(lane < 4, zedge, rl(e, 4)))
    total = total + zhi_ * (e - jnp.where(lane >= WIDE - 4, zedge, rl(e, -4)))
    e = e + weight2 * (q - total)

    n3 = n2 - 2
    ypack_halves(ys7, e[1:-1])
    wait_y = exchange(ay, ys7, yr7)
    zpack(zs7, [e[d] for d in range(1, n2 - 1)], 4, 4)
    wait_z = exchange(az, zs7, zr7)

    mass3 = mass2 * 8.0
    zfirst = lane % 8 < 4
    xout = jnp.where(layer0, xlo, xhi)[1:-1]
    yout = jnp.where(sub < 4, ylo_, yhi_)[1:-1]
    zout = jnp.where(zfirst, zlo_, zhi_)[1:-1]
    a = xout + rs(xout, 4)
    a = a + rl(a, -4)
    xlo3, xhi3 = a, rl(a, -1)
    a = yout + rl(yout, -1)
    a = a + rl(a, -4)
    ylo3, yhi3 = a, rs(a, 4)
    a = zout + rl(zout, -1)
    a = a + rs(a, 4)
    zlo3, zhi3 = a, rl(a, -4)
    diag3 = mass3 + xlo3 + xhi3 + ylo3 + yhi3 + zlo3 + zhi3
    near_x = jnp.where(layer0, last_x(e), next_x(e))[1:-1]
    e = e[1:-1]
    near_z = jnp.where(zfirst, rl(e, 4), rl(e, -4))
    partial = q[1:-1] - mass2 * e - xout * (e - near_x)
    coefs = jnp.where(sub == 3, rs(diag3, 3), jnp.where(sub == 4, rs(xhi3, 4), jnp.where(sub == 5, rs(yhi3, 5), rs(zhi3, 6))))
    wait_y()
    wait_z()
    edge = yedges(yr7, n3)
    zedge = zedges(zr7, n3)
    near_z = jnp.where((lane < 4) | (lane >= WIDE - 4), zedge, near_z)
    t = partial - yout * (e - edge) - zout * (e - near_z)
    t = t + rl(t, -1)
    t = t + rs(t, 4)
    t = t + rl(t, -4)
    t = jnp.where(sub < 3, t, coefs)
    block = jnp.zeros((8, WIDE), jnp.float32)
    for l in range(n3):
        block = jnp.where((lane % 8 == l) & (sub < 7), rl(t[l], l), block)

    def column(slot, at):
        return gb.at[slot, :, pl.ds(pl.multiple_of(at * WIDE, WIDE), WIDE)]

    def half(slot, at):
        return gh.at[slot, :, pl.ds(pl.multiple_of(at * 128, 128), 128)]

    gb[YREACH, :, pl.ds(pl.multiple_of(gz * WIDE, WIDE), WIDE)] = block
    third = lane1 % 8
    hs[...] = jnp.where(third < 3, rl(block[:, :128], -2), jnp.where(third < 6, rl(block[:, 128:], 1), 0.0))
    first = fresh((2 * YREACH + 1) * nz)
    old = len(pending)
    order3 = [(d, [rel for rel in (2, 1, 3, 0) if rel < nz and (d or rel)]) for d in (3, -3, 2, -2, 1, -1, 0)]
    order3 = [(d, rels) for d, rels in order3 if rels]

    def place3(d, at):
        return half(HALVES.index(d), at) if d in HALVES else column(YREACH + d, at)

    def sem3(d, rel):
        return first + (YREACH - d) * nz + rel

    for d, rels in order3:
        source = hs if d in HALVES else column(YREACH, gz)
        to = [{ay: gy + d, az: lax.rem(gz + rel, nz)} for rel in rels]
        start([(sem3(d, rel), source, place3(-d, gz), t) for rel, t in zip(rels, to)], has(ay, d))
    drain(old)
    for d, rels in reversed(order3):
        arrived([(sem3(d, rel), place3(-d, lax.rem(gz + nz - rel, nz))) for rel in rels], has(ay, -d))
    middle = (third >= 2) & (third < 5)
    for i, d in enumerate(HALVES):
        for at in range(nz):
            m = gh[i, :, 128 * at : 128 * at + 128]
            gb[YREACH + d, :, WIDE * at : WIDE * at + 128] = jnp.where(middle, rl(m, 2), 0.0)
            gb[YREACH + d, :, WIDE * at + 128 : WIDE * at + 256] = jnp.where(middle, rl(m, -1), 0.0)

    full = (8, WIDE * nz)
    n = 2 * YREACH + 1

    def coefficient(j, item):
        return jnp.broadcast_to(gb[j, item : item + 1, :], full)

    r3 = [gb[j] for j in range(n)]
    w3 = [DAMPING / safe(coefficient(j, 3)) for j in range(n)]
    e = {j: w3[j] * r3[j] for j in range(n)}
    xhi = {j: coefficient(j, 4) for j in range(1, n - 1)}
    yhi = {j: coefficient(j, 5) for j in range(n - 1)}
    zhi = {j: coefficient(j, 6) for j in range(1, n - 1)}
    xlo = {j: rl(xhi[j], 1) for j in xhi}
    zlo = {j: rl(zhi[j], 8) for j in zhi}
    for sweep in range(1, YREACH + 1):
        new = {}
        for j in range(sweep, n - sweep):
            v = e[j]
            total = mass3 * v + xlo[j] * (v - rl(v, 1)) + xhi[j] * (v - rl(v, -1))
            total = total + yhi[j - 1] * (v - e[j - 1]) + yhi[j] * (v - e[j + 1])
            total = total + zlo[j] * (v - rl(v, 8)) + zhi[j] * (v - rl(v, -8))
            new[j] = v + w3[j] * (r3[j] - total)
        e = new
    own = e[YREACH]
    tile = jnp.zeros((8, 128), jnp.float32)
    for t in range(2 * nz):
        tile = jnp.where(lane1 % 8 == t, rl(own[:, 128 * t : 128 * t + 128], t - XREACH + 1), tile)
    r = lax.broadcasted_iota(jnp.int32, (128, 32 * nz), 0)
    c = lax.broadcasted_iota(jnp.int32, (128, 32 * nz), 1)
    order = jnp.where(c == (r % 8) * 16 + r // 8, 1.0, 0.0)
    dense = jnp.dot(tile, order, precision=lax.Precision.HIGHEST, preferred_element_type=jnp.float32)
    for f in range(FIELDS):
        coarse_out[f, 0, :, :] = dense[f : f + 1, :]

    drain(len(pending))


def solution(mesh):
    names = mesh.axis_names
    sizes = tuple(mesh.shape[a] for a in names)
    nz = sizes[2]
    f32 = jnp.float32

    def both(*shape):
        return [pltpu.VMEM((2, *shape), f32)] * 2

    scratch = [
        pltpu.VMEM((8, 8, WIDE), jnp.int32),
        pltpu.VMEM((8, 8, WIDE), f32),
        pltpu.VMEM((FIELDS, 8, 8, WIDE), f32),
        pltpu.VMEM((FIELDS, 8, 8, WIDE), f32),
        pltpu.SemaphoreType.DMA((5,)),
        *both(4, 8, WIDE), *both(8, 128),
        *both(4, 8, WIDE), pltpu.VMEM((2, 1, 8, WIDE), f32), *both(3, 8, WIDE), pltpu.VMEM((2, 1, 8, WIDE), f32),
        *both(2, 8, WIDE), *both(8, 128),
        *both(1, 8, WIDE), *both(8, 128),
        pltpu.VMEM((2 * XREACH + 1, 8, WIDE), f32),
        *both(3, 8, WIDE), *both(8, 128),
        *both(2, 8, WIDE), *both(8, 128),
        pltpu.VMEM((2 * YREACH + 1, 8, WIDE * nz), f32),
        pltpu.VMEM((len(HALVES), 8, 128 * nz), f32),
        pltpu.VMEM((8, 128), f32),
        pltpu.SMEM((3,), f32),
    ]
    sems = 2 * 2 * 5 + (2 + 16) + (2 + 8) + 2 * (2 * XREACH + 1) + (2 * YREACH + 1) * nz
    scratch += [pltpu.SemaphoreType.REGULAR((2,)), pltpu.SemaphoreType.DMA((sems,)), pltpu.SemaphoreType.DMA((sems,))]

    def local(phase_label, concentration, phase_factor, potential, source):
        return pl.pallas_call(
            functools.partial(kernel, names, sizes),
            out_shape=(
                jax.ShapeDtypeStruct((FIELDS, 4, 4, 128), f32),
                jax.ShapeDtypeStruct((FIELDS, 1, 1, 32 * nz), f32),
            ),
            in_specs=[pl.BlockSpec(memory_space=pltpu.HBM)] * 5,
            out_specs=(pl.BlockSpec(memory_space=pltpu.VMEM), pl.BlockSpec(memory_space=pltpu.VMEM)),
            scratch_shapes=scratch,
            compiler_params=pltpu.CompilerParams(collective_id=0, has_side_effects=True, vmem_limit_bytes=55168 << 10),
        )(phase_label, concentration, potential, source, phase_factor)

    return jax.shard_map(
        local,
        mesh=mesh,
        in_specs=(P(*names), P(*names), P(), P(None, *names), P(None, *names)),
        out_specs=(P(None, *names), P(None, names[0], names[1], None)),
        check_vma=False,
    )
```

```python
import functools

import jax
import jax.numpy as jnp
from jax import lax
from jax.experimental import pallas as pl
from jax.experimental.pallas import tpu as pltpu
from jax.sharding import PartitionSpec as P

MESH = pl.DeviceIdType.MESH
FIELDS = 3
MASS = 0.05
DAMPING = 0.7
DECAY = 0.3
XREACH = 4
YREACH = 3
WIDE = 256
HALVES = (-3, -2, 2, 3)
XROW = 4


def rs(x, k):
    k %= x.shape[-2]
    return pltpu.roll(x, k, x.ndim - 2) if k else x


def rl(x, k):
    k %= x.shape[-1]
    return pltpu.roll(x, k, x.ndim - 1) if k else x


def harmonic(a, b):
    return 2.0 * a * b / (a + b)


def safe(d):
    return jnp.where(d > 0.0, d, 1.0)


def kernel(names, sizes, phase, conc, pot, src, factors, lev_out, coarse_out, *scratch):
    (ph, co, po, so, in_sem, ys1, yr1, zs1, zr1, xs1, xr1, xk1, xs2, xr2, xk2, ys3, yr3, zs3, zr3, ys4, yr4, zs4, zr4,
     qb, ys6, yr6, zs6, zr6, ys7, yr7, zs7, zr7, gb, gh, hs, factor, row_sem, ssem, rsem) = scratch
    ax, ay, az = names
    nx, ny, nz = sizes
    gx, gy, gz = (lax.axis_index(a) for a in names)
    here = {ax: gx, ay: gy, az: gz}
    count = {ax: nx, ay: ny, az: nz}

    known_steps = {}

    def has(axis, step):
        if (axis, step) not in known_steps:
            at = here[axis] + step
            known_steps[axis, step] = (at >= 0) & (at < count[axis])
        return known_steps[axis, step]

    barrier = pltpu.get_barrier_semaphore()
    place = lax.rem(gx, XROW)
    met = jnp.int32(nz - 1)
    for d in (1, -1, 2, -2, 3, -3):
        known = has(ax, d) & (place + d >= 0) & (place + d < XROW)
        if abs(d) == 1:
            known = has(ax, d)
        met = met + known.astype(jnp.int32)

        @pl.when(known)
        def _(d=d):
            pl.semaphore_signal(barrier, inc=1, device_id={ax: gx + d}, device_id_type=MESH)

    loads = [pltpu.make_async_copy(a, b, in_sem.at[i]) for i, (a, b) in enumerate(((phase, ph), (conc, co), (factors, factor), (pot, po), (src, so)))]
    for load in loads:
        load.start()

    for d in range(-YREACH, YREACH + 1):
        if d:
            met = met + nz * has(ay, d).astype(jnp.int32)

            @pl.when(has(ay, d))
            def _(d=d):
                for rel in range(nz):
                    to = {ay: gy + d, az: lax.rem(gz + rel, nz)}
                    pl.semaphore_signal(barrier, inc=1, device_id=to, device_id_type=MESH)

    for rel in range(1, nz):
        pl.semaphore_signal(barrier, inc=1, device_id={az: lax.rem(gz + rel, nz)}, device_id_type=MESH)

    for axis, bufs in ((ax, (xr1, xr2)), (ay, (yr1, yr3, yr4, yr6, yr7)), (az, (zr1, zr3, zr4, zr6, zr7))):
        for side, d in ((0, -1), (1, 1)):

            @pl.when(jnp.logical_not(has(axis, d)))
            def _(bufs=bufs, side=side):
                for buf in bufs:
                    buf[side] = jnp.zeros(buf.shape[1:], jnp.float32)

    pending = []
    used = [0]

    def fresh(n=1):
        used[0] += n
        return used[0] - n

    def copy(k, a, b, target):
        return pltpu.make_async_remote_copy(
            src_ref=a, dst_ref=b, send_sem=ssem.at[k], recv_sem=rsem.at[k], device_id=target, device_id_type=MESH
        )

    def start(copies, when):
        pending.append((copies, when))

        @pl.when(when)
        def _():
            for c in copies:
                copy(*c).start()

    def arrived(copies, when):
        @pl.when(when)
        def _():
            for k, b in copies:
                copy(k, b, b, {}).wait_recv()

    def drain(n):
        groups = {}
        for copies, when in pending[:n]:
            groups.setdefault(id(when), (when, []))[1].extend(copies)
        for when, copies in groups.values():

            @pl.when(when)
            def _(copies=copies):
                for c in copies:
                    copy(*c).wait_send()

        del pending[:n]

    def push(k, a, b, axis, d):
        start([(k, a, b, {axis: here[axis] + d})], has(axis, d))

    def take(k, b, axis, d):
        arrived([(k, b)], has(axis, d))

    def exchange(axis, sent, got):
        k = fresh(2)
        push(k, sent.at[0], got.at[1], axis, -1)
        push(k + 1, sent.at[1], got.at[0], axis, 1)

        def wait():
            take(k, got.at[1], axis, 1)
            take(k + 1, got.at[0], axis, -1)

        return wait

    class Crossing:
        def __init__(self, sent, got, kept, pieces, lines):
            self.sent, self.got, self.kept, self.pieces, self.lines = sent, got, kept, pieces, lines
            self.whole = fresh(2)
            self.part = fresh(2 * len(pieces))
            self.hop = fresh(2 * len(pieces))
            for side, d in ((0, -1), (1, 1)):
                edge = 0 if side == 0 else XROW - 1
                inside = has(ax, d) & (place != edge)
                leaves = has(ax, d) & (place == edge)
                start([(self.whole + side, sent.at[side], got.at[1 - side], {ax: gx + d})], inside)
                copies = []
                for i, piece in enumerate(pieces):
                    line = lines[side][i]
                    if line == edge:
                        copies.append((self.sem(side, i), sent.at[side, piece], got.at[1 - side, piece], {ax: gx + d}))
                    else:
                        k = self.hop + side * len(pieces) + i
                        copies.append((k, sent.at[side, piece], kept.at[side], {ax: gx + line - edge}))
                start(copies, leaves)

        def sem(self, side, i):
            return self.part + side * len(self.pieces) + i

        def forward(self):
            for side, d in ((0, -1), (1, 1)):
                edge = 0 if side == 0 else XROW - 1
                to = gx - place + edge + d
                exists = (to >= 0) & (to < nx)
                for i, piece in enumerate(self.pieces):
                    line = self.lines[side][i]
                    if line != edge:
                        mine = exists & (place == line)
                        arrived([(self.hop + side * len(self.pieces) + i, self.kept.at[side])], mine)
                        start([(self.sem(side, i), self.kept.at[side], self.got.at[1 - side, piece], {ax: to})], mine)

        def finish(self):
            for side, d in ((0, -1), (1, 1)):
                edge = 0 if side == 0 else XROW - 1
                arrived([(self.whole + 1 - side, self.got.at[side])], has(ax, d) & (place != edge))
                parts = [(self.sem(1 - side, i), self.got.at[side, piece]) for i, piece in enumerate(self.pieces)]
                arrived(parts, has(ax, d) & (place == edge))

    sub = lax.broadcasted_iota(jnp.int32, (8, WIDE), 0)
    lane = lax.broadcasted_iota(jnp.int32, (8, WIDE), 1)
    lane1 = lax.broadcasted_iota(jnp.int32, (8, 128), 1)

    def zpack(sent, slabs, stride, unit):
        low = high = jnp.zeros((8, 128), jnp.float32)
        for k, s in enumerate(slabs):
            mine = (lane1 >= unit * k) & (lane1 < unit * (k + 1))
            low = jnp.where(mine, rl(s[:, :128], unit * k), low)
            high = jnp.where(mine, rl(s[:, 128:], unit * k - (128 - stride)), high)
        sent[0] = low
        sent[1] = high

    def zhalo(low, high, k, stride, unit):
        return jnp.concatenate([rl(low, -unit * k), rl(high, 128 - stride - unit * k)], axis=1)

    def ypack_rows(sent, slabs, stride):
        for g in range(sent.shape[1]):
            low = high = jnp.zeros((8, WIDE), jnp.float32)
            for j, s in enumerate(slabs[8 * g : 8 * g + 8]):
                low = jnp.where(sub == j, rs(s, j), low)
                high = jnp.where(sub == j, rs(s, j - (8 - stride)), high)
            sent[0, g] = low
            sent[1, g] = high

    def row(got, side, k):
        return jnp.broadcast_to(got[side, k // 8, k % 8 : k % 8 + 1, :], (8, WIDE))

    loads[0].wait()
    loads[1].wait()
    loads[2].wait()
    loads[3].wait()
    phase_v = ph[...]
    conc_v = co[...]
    lookup = jnp.zeros(phase_v.shape, jnp.float32)
    for i in range(3):
        lookup = lookup + jnp.where(phase_v == i, factor[i], 0.0)
    conduct = lookup * conc_v * jnp.exp(-DECAY * conc_v)
    fine = [jnp.stack([conduct[x]] + [po[f, x] for f in range(FIELDS)]) for x in range(8)]
    ypack_rows(ys1, [fine[x][a] for a in range(4) for x in range(8)], 1)
    zpack(zs1, [fine[x][a] for a in range(4) for x in range(8)], 1, 1)
    xs1[0] = fine[0]
    xs1[1] = fine[7]

    pl.semaphore_wait(barrier, met)

    wait_y1 = exchange(ay, ys1, yr1)
    wait_z1 = exchange(az, zs1, zr1)
    slabs = [pl.ds(i, 1) for i in range(4)]
    early = Crossing(xs1, xr1, xk1, slabs, ([0, 1, 2, 3], [0, 1, 2, 3]))

    def rest(c):
        return c[0], c[1:]

    def flux(c, v, other):
        face = harmonic(c, other[0])
        return face, face * (v - other[1:])

    inner = []
    for i in range(3):
        a, b = fine[2 * i + 1], fine[2 * i + 2]
        inner.append(flux(a[0], a[1:], b))

    loads[4].wait()
    wait_y1()
    wait_z1()
    zlow, zhigh = zr1[0], zr1[1]
    part, ypart, zpart = [], [], []
    for x in range(8):
        c, v = rest(fine[x])
        near = jnp.where(sub % 2 == 0, rs(fine[x], 1), rs(fine[x], -1))
        edge = jnp.stack([jnp.where(sub == 0, row(yr1, 0, a * 8 + x), row(yr1, 1, a * 8 + x)) for a in range(4)])
        near = jnp.where((sub == 0) | (sub == 7), edge, near)
        sy, fy = flux(c, v, near)
        near = jnp.where(lane % 2 == 0, rl(fine[x], 1), rl(fine[x], -1))
        edge = jnp.stack([zhalo(zlow, zhigh, a * 8 + x, 1, 1) for a in range(4)])
        near = jnp.where((lane == 0) | (lane == WIDE - 1), edge, near)
        sz, fz = flux(c, v, near)
        source = jnp.stack([so[f, x] for f in range(FIELDS)])
        part.append(source - MASS * v - fy - fz)
        ypart.append(sy)
        zpart.append(sz)

    def fold(t, stride):
        t = t + rl(t, -stride)
        return t + rs(t, -stride)

    mass1 = MASS * 8.0
    r1, ylo, yhi, zlo, zhi, diag, sx = {}, {}, {}, {}, {}, {}, {}
    for i in range(3):
        sx[i] = fold(inner[i][0], 1)
    for i in range(4):
        t = part[2 * i] + part[2 * i + 1]
        if i < 3:
            t = t - inner[i][1]
        if i > 0:
            t = t + inner[i - 1][1]
        r1[i] = fold(t, 1)
        a = ypart[2 * i] + ypart[2 * i + 1]
        a = a + rl(a, -1)
        ylo[i], yhi[i] = a, rs(a, -1)
        b = zpart[2 * i] + zpart[2 * i + 1]
        b = b + rs(b, -1)
        zlo[i], zhi[i] = b, rl(b, -1)
        d = mass1 + ylo[i] + yhi[i] + zlo[i] + zhi[i]
        if i < 3:
            d = d + sx[i]
        if i > 0:
            d = d + sx[i - 1]
        diag[i] = d

    e0, weight = {}, {}
    for i in (1, 2):
        weight[i] = DAMPING / safe(diag[i])
        e0[i] = weight[i] * r1[i]

    q0 = sub % 2 == 0
    p0 = lane % 2 == 0

    def merge4(a, b, c, d):
        return jnp.where(q0, jnp.where(p0, a, rl(b, 1)), jnp.where(p0, rs(c, 1), rs(rl(d, 1), 1)))

    def split4(m):
        low = rs(m, -1)
        return m, rl(m, -1), low, rl(low, -1)

    for side, (edge, next_to, face) in enumerate(((0, 1, 0), (3, 2, 2))):
        xs2[side, 0] = merge4(e0[next_to][0], e0[next_to][1], e0[next_to][2], diag[edge])
        xs2[side, 1] = merge4(r1[edge][0], r1[edge][1], r1[edge][2], sx[face])
        xs2[side, 2] = merge4(ylo[edge], yhi[edge], zlo[edge], zhi[edge])
    late = Crossing(xs2, xr2, xk2, [pl.ds(0, 2), pl.ds(2, 1)], ([0, 1], [XROW - 1, XROW - 2]))
    early.forward()
    late.forward()
    early.finish()
    for side, edge in ((0, 0), (1, XROW - 1)):
        step = 1 if side == 0 else -1

        @pl.when((place == edge) & has(ax, -step))
        def _(side=side, step=step):
            for i in range(1, XROW):
                pl.semaphore_signal(row_sem.at[side], inc=1, device_id={ax: gx + step * i}, device_id_type=MESH)

    border = {}
    for side, x in ((0, 0), (1, 7)):
        face, out = flux(fine[x][0], fine[x][1:], xr1[side])
        border[side] = (fold(face, 1), fold(out, 1))
    late.finish()
    for side, edge, out, far, own_face, far_face in ((0, 0, -1, -2, -1, -2), (1, 3, 4, 5, 3, 4)):
        face, through = border[side]
        a = split4(xr2[side, 0])
        b = split4(xr2[side, 1])
        c = split4(xr2[side, 2])
        e0[far] = jnp.stack(a[:3])
        r1[out] = jnp.stack(b[:3]) + through
        r1[edge] = r1[edge] - through
        sx[far_face] = b[3]
        sx[own_face] = face
        ylo[out], yhi[out], zlo[out], zhi[out] = c
        diag[out] = a[3] + face
        diag[edge] = diag[edge] + face
        for i in (out, edge):
            weight[i] = DAMPING / safe(diag[i])
            e0[i] = weight[i] * r1[i]

    def halos(got_y, got_z, layers, low, high, i):
        base = layers.index(i) * FIELDS
        ylow = jnp.stack([rl(row(got_y, 0, k // 2), -(k % 2)) for k in range(base, base + FIELDS)])
        yhigh = jnp.stack([rl(row(got_y, 1, k // 2), -(k % 2)) for k in range(base, base + FIELDS)])
        zedge = jnp.stack([zhalo(low, high, base + f, 2, 1) for f in range(FIELDS)])
        return ylow, yhigh, zedge

    def two_by_two(slabs):
        return [jnp.where(p0, a, rl(b, 1)) for a, b in zip(slabs[::2], slabs[1::2])]

    six = [-1, 0, 1, 2, 3, 4]
    slabs = [e0[i][f] for i in six for f in range(FIELDS)]
    ypack_rows(ys3, two_by_two(slabs), 2)
    wait_y = exchange(ay, ys3, yr3)
    zpack(zs3, slabs, 2, 1)
    wait_z = exchange(az, zs3, zr3)
    wait_y()
    wait_z()
    low, high = zr3[0], zr3[1]
    e1 = {}
    for i in six:
        e = e0[i]
        ylow, yhigh, zedge = halos(yr3, zr3, six, low, high, i)
        total = mass1 * e + sx[i - 1] * (e - e0[i - 1]) + sx[i] * (e - e0[i + 1])
        total = total + ylo[i] * (e - jnp.where(sub < 2, ylow, rs(e, 2)))
        total = total + yhi[i] * (e - jnp.where(sub >= 6, yhigh, rs(e, -2)))
        total = total + zlo[i] * (e - jnp.where(lane < 2, zedge, rl(e, 2)))
        total = total + zhi[i] * (e - jnp.where(lane >= WIDE - 2, zedge, rl(e, -2)))
        e1[i] = e + weight[i] * (r1[i] - total)

    four = [0, 1, 2, 3]
    slabs = [e1[i][f] for i in four for f in range(FIELDS)]
    ypack_rows(ys4, two_by_two(slabs), 2)
    wait_y = exchange(ay, ys4, yr4)
    zpack(zs4, slabs, 2, 1)
    wait_z = exchange(az, zs4, zr4)

    mass2 = mass1 * 8.0
    yfirst = sub % 4 < 2
    zfirst = lane % 4 < 2
    yout = {i: jnp.where(yfirst, ylo[i], yhi[i]) for i in four}
    zout = {i: jnp.where(zfirst, zlo[i], zhi[i]) for i in four}
    sx2 = {-1: fold(sx[-1], 2), 0: fold(sx[1], 2), 1: fold(sx[3], 2)}
    ylo2, yhi2, zlo2, zhi2, diag2 = {}, {}, {}, {}, {}
    for i in range(2):
        a = yout[2 * i] + yout[2 * i + 1]
        a = a + rl(a, -2)
        ylo2[i], yhi2[i] = a, rs(a, -2)
        b = zout[2 * i] + zout[2 * i + 1]
        b = b + rs(b, -2)
        zlo2[i], zhi2[i] = b, rl(b, -2)
        diag2[i] = mass2 + sx2[i - 1] + sx2[i] + ylo2[i] + yhi2[i] + zlo2[i] + zhi2[i]

    wait_y()
    wait_z()
    low, high = zr4[0], zr4[1]
    left = {}
    for i in four:
        e = e1[i]
        ylow, yhigh, zedge = halos(yr4, zr4, four, low, high, i)
        across = i - 1 if i % 2 == 0 else i + 1
        near_y = jnp.where(yfirst, jnp.where(sub < 2, ylow, rs(e, 2)), jnp.where(sub >= 6, yhigh, rs(e, -2)))
        near_z = jnp.where(zfirst, rl(e, 2), rl(e, -2))
        near_z = jnp.where((lane < 2) | (lane >= WIDE - 2), zedge, near_z)
        total = mass1 * e + sx[min(i, across)] * (e - e1[across])
        total = total + yout[i] * (e - near_y) + zout[i] * (e - near_z)
        left[i] = r1[i] - total
    r2 = {i: fold(left[2 * i] + left[2 * i + 1], 2) for i in range(2)}

    q4 = sub % 4
    p4 = lane % 4

    def by(which, a, b, c, d):
        return jnp.where(which < 2, jnp.where(which == 0, a, b), jnp.where(which == 2, c, d))

    def rows4(a, b, c, d):
        return by(q4, a, rs(b, 1), rs(c, 2), rs(d, 3))

    block = by(
        p4,
        rows4(r2[0][0], r2[0][1], r2[0][2], diag2[0]),
        rl(rows4(r2[1][0], r2[1][1], r2[1][2], diag2[1]), 1),
        rl(rows4(sx2[0], yhi2[0], zhi2[0], zlo2[0]), 2),
        rl(rows4(sx2[1], yhi2[1], zhi2[1], zlo2[1]), 3),
    )
    qb[XREACH] = block
    old = len(pending)
    direct = fresh(2 * XREACH + 1)
    for side, edge in ((0, 0), (1, XROW - 1)):

        @pl.when((place != edge) & has(ax, XREACH * (2 * side - 1)))
        def _(side=side):
            pl.semaphore_wait(row_sem.at[side], 1)

    for d in (-XREACH, XREACH, 1, -1, 2, -2, 3, -3):
        inside = has(ax, d) if abs(d) == XREACH else has(ax, d) & (place + d >= 0) & (place + d < XROW)
        start([(direct + XREACH - d, qb.at[XREACH], qb.at[XREACH - d], {ax: gx + d})], inside)

    drain(old)
    blocks = [(ax, d, qb, XREACH + d) for d in range(-XREACH, XREACH + 1) if d]
    blocks += [(ay, d, gb, YREACH + d) for d in (-1, 1)] + [(ay, d, gh, i) for i, d in enumerate(HALVES)]
    for axis, d, buf, slot in blocks:

        @pl.when(jnp.logical_not(has(axis, d)))
        def _(buf=buf, slot=slot):
            buf[slot] = jnp.zeros(buf.shape[1:], jnp.float32)

    packed = jnp.concatenate([merge4(*(e1[i][f] for i in four)) for f in range(FIELDS)], axis=0)
    r = lax.broadcasted_iota(jnp.int32, (WIDE, WIDE), 0)
    c = lax.broadcasted_iota(jnp.int32, (WIDE, WIDE), 1)
    order = jnp.where(c == (r % 2) * 128 + r // 2, 1.0, 0.0)
    dense = jnp.dot(packed, order, precision=lax.Precision.HIGHEST, preferred_element_type=jnp.float32)
    for f in range(FIELDS):
        for y in range(4):
            for q in range(2):
                for p in range(2):
                    k = f * 8 + 2 * y + q
                    lev_out[f, 2 * q + p, y : y + 1, :] = dense[k : k + 1, 128 * p : 128 * p + 128]

    handed = fresh(2 * XREACH + 1)
    for side in (-1, 1):
        far = XREACH + side * XREACH
        take(direct + far, qb.at[far], ax, side * XREACH)
        for step in range(1, XROW):
            slot = far - side * step
            inside = has(ax, side * XREACH) & (place + side * step >= 0) & (place + side * step < XROW)
            start([(handed + slot, qb.at[far], qb.at[slot], {ax: gx + side * step})], inside)
    for side in (-1, 1):
        for step in range(1, XROW):
            slot = XREACH + side * step
            inside = (place + side * step >= 0) & (place + side * step < XROW)
            arrived([(direct + slot, qb.at[slot])], has(ax, side * step) & inside)
            arrived([(handed + slot, qb.at[slot])], has(ax, side * step) & jnp.logical_not(inside))

    n2 = 2 * XREACH + 1
    q = qb[...]

    def spread(x, item):
        return jnp.where(q4 == 0, rs(x, -item), jnp.where(q4 == 1, rs(x, 1 - item), rs(x, 2 - item)))

    layer0 = p4 == 0
    weight2 = DAMPING / safe(spread(q, 3))
    coef = rl(q, -2)
    xhi, yhi_, zhi_, zlo_ = (spread(coef, item) for item in range(4))
    e = weight2 * q

    def below(x):
        return jnp.concatenate([x[:1], x[:-1]], axis=0)

    def above(x):
        return jnp.concatenate([x[1:], x[-1:]], axis=0)

    def next_x(x):
        return jnp.where(layer0, rl(x, -1), above(rl(x, 1)))

    def last_x(x):
        return jnp.where(layer0, below(rl(x, -1)), rl(x, 1))

    def ypack_halves(sent, x):
        low, high = [], []
        for m in range(0, x.shape[0], 2):
            a, b = x[m], x[min(m + 1, x.shape[0] - 1)]
            low.append(jnp.where(sub < 4, a, rs(b, 4)))
            high.append(jnp.where(sub < 4, rs(a, 4), b))
        for side, h in ((0, low), (1, high)):
            for g in range(sent.shape[1]):
                sent[side, g] = jnp.where(p4 < 2, h[2 * g], rl(h[min(2 * g + 1, len(h) - 1)], 2))

    def yedges(got, n):
        out = []
        for d in range(n):
            low, high = (rl(got[side, d // 4], -2 * (d // 2 % 2)) for side in (0, 1))
            if d % 2 == 0:
                out.append(jnp.where(sub < 4, low, rs(high, 4)))
            else:
                out.append(jnp.where(sub < 4, rs(low, 4), high))
        return jnp.stack(out)

    def zedges(got, n):
        low, high = got[0], got[1]
        return jnp.stack([zhalo(low, high, d, 4, 4) for d in range(n)])

    ypack_halves(ys6, jnp.where(q4 == 3, rs(coef, 2), e))
    wait_y = exchange(ay, ys6, yr6)
    zpack(zs6, [e[d] for d in range(n2)], 4, 4)
    wait_z = exchange(az, zs6, zr6)
    xlo = last_x(xhi)
    near = xlo * (e - last_x(e)) + xhi * (e - next_x(e)) + mass2 * e
    wait_y()
    wait_z()
    edge = yedges(yr6, n2)
    zedge = zedges(zr6, n2)
    ylo_ = jnp.where(sub < 4, spread(edge, 3), rs(yhi_, 4))
    other = rs(e, 4)
    total = near + ylo_ * (e - jnp.where(sub < 4, edge, other)) + yhi_ * (e - jnp.where(sub < 4, other, edge))
    total = total + zlo_ * (e - jnp.where(lane < 4, zedge, rl(e, 4)))
    total = total + zhi_ * (e - jnp.where(lane >= WIDE - 4, zedge, rl(e, -4)))
    e = e + weight2 * (q - total)

    n3 = n2 - 2
    ypack_halves(ys7, e[1:-1])
    wait_y = exchange(ay, ys7, yr7)
    zpack(zs7, [e[d] for d in range(1, n2 - 1)], 4, 4)
    wait_z = exchange(az, zs7, zr7)

    mass3 = mass2 * 8.0
    zfirst = lane % 8 < 4
    xout = jnp.where(layer0, xlo, xhi)[1:-1]
    yout = jnp.where(sub < 4, ylo_, yhi_)[1:-1]
    zout = jnp.where(zfirst, zlo_, zhi_)[1:-1]
    a = xout + rs(xout, 4)
    a = a + rl(a, -4)
    xlo3, xhi3 = a, rl(a, -1)
    a = yout + rl(yout, -1)
    a = a + rl(a, -4)
    ylo3, yhi3 = a, rs(a, 4)
    a = zout + rl(zout, -1)
    a = a + rs(a, 4)
    zlo3, zhi3 = a, rl(a, -4)
    diag3 = mass3 + xlo3 + xhi3 + ylo3 + yhi3 + zlo3 + zhi3
    near_x = jnp.where(layer0, last_x(e), next_x(e))[1:-1]
    e = e[1:-1]
    near_z = jnp.where(zfirst, rl(e, 4), rl(e, -4))
    partial = q[1:-1] - mass2 * e - xout * (e - near_x)
    coefs = jnp.where(sub == 3, rs(diag3, 3), jnp.where(sub == 4, rs(xhi3, 4), jnp.where(sub == 5, rs(yhi3, 5), rs(zhi3, 6))))
    wait_y()
    wait_z()
    edge = yedges(yr7, n3)
    zedge = zedges(zr7, n3)
    near_z = jnp.where((lane < 4) | (lane >= WIDE - 4), zedge, near_z)
    t = partial - yout * (e - edge) - zout * (e - near_z)
    t = t + rl(t, -1)
    t = t + rs(t, 4)
    t = t + rl(t, -4)
    t = jnp.where(sub < 3, t, coefs)
    block = jnp.zeros((8, WIDE), jnp.float32)
    for l in range(n3):
        block = jnp.where((lane % 8 == l) & (sub < 7), rl(t[l], l), block)

    def column(slot, at):
        return gb.at[slot, :, pl.ds(pl.multiple_of(at * WIDE, WIDE), WIDE)]

    def half(slot, at):
        return gh.at[slot, :, pl.ds(pl.multiple_of(at * 128, 128), 128)]

    gb[YREACH, :, pl.ds(pl.multiple_of(gz * WIDE, WIDE), WIDE)] = block
    third = lane1 % 8
    hs[...] = jnp.where(third < 3, rl(block[:, :128], -2), jnp.where(third < 6, rl(block[:, 128:], 1), 0.0))
    first = fresh((2 * YREACH + 1) * nz)
    old = len(pending)
    order3 = [(d, [rel for rel in (2, 1, 3, 0) if rel < nz and (d or rel)]) for d in (3, -3, 2, -2, 1, -1, 0)]
    order3 = [(d, rels) for d, rels in order3 if rels]

    def place3(d, at):
        return half(HALVES.index(d), at) if d in HALVES else column(YREACH + d, at)

    def sem3(d, rel):
        return first + (YREACH - d) * nz + rel

    for d, rels in order3:
        source = hs if d in HALVES else column(YREACH, gz)
        to = [{ay: gy + d, az: lax.rem(gz + rel, nz)} for rel in rels]
        start([(sem3(d, rel), source, place3(-d, gz), t) for rel, t in zip(rels, to)], has(ay, d))
    drain(old)
    for d, rels in reversed(order3):
        arrived([(sem3(d, rel), place3(-d, lax.rem(gz + nz - rel, nz))) for rel in rels], has(ay, -d))
    middle = (third >= 2) & (third < 5)
    for i, d in enumerate(HALVES):
        for at in range(nz):
            m = gh[i, :, 128 * at : 128 * at + 128]
            gb[YREACH + d, :, WIDE * at : WIDE * at + 128] = jnp.where(middle, rl(m, 2), 0.0)
            gb[YREACH + d, :, WIDE * at + 128 : WIDE * at + 256] = jnp.where(middle, rl(m, -1), 0.0)

    full = (8, WIDE * nz)
    n = 2 * YREACH + 1

    def coefficient(j, item):
        return jnp.broadcast_to(gb[j, item : item + 1, :], full)

    r3 = [gb[j] for j in range(n)]
    w3 = [DAMPING / safe(coefficient(j, 3)) for j in range(n)]
    e = {j: w3[j] * r3[j] for j in range(n)}
    xhi = {j: coefficient(j, 4) for j in range(1, n - 1)}
    yhi = {j: coefficient(j, 5) for j in range(n - 1)}
    zhi = {j: coefficient(j, 6) for j in range(1, n - 1)}
    xlo = {j: rl(xhi[j], 1) for j in xhi}
    zlo = {j: rl(zhi[j], 8) for j in zhi}
    for sweep in range(1, YREACH + 1):
        new = {}
        for j in range(sweep, n - sweep):
            v = e[j]
            total = mass3 * v + xlo[j] * (v - rl(v, 1)) + xhi[j] * (v - rl(v, -1))
            total = total + yhi[j - 1] * (v - e[j - 1]) + yhi[j] * (v - e[j + 1])
            total = total + zlo[j] * (v - rl(v, 8)) + zhi[j] * (v - rl(v, -8))
            new[j] = v + w3[j] * (r3[j] - total)
        e = new
    own = e[YREACH]
    tile = jnp.zeros((8, 128), jnp.float32)
    for t in range(2 * nz):
        tile = jnp.where(lane1 % 8 == t, rl(own[:, 128 * t : 128 * t + 128], t - XREACH + 1), tile)
    r = lax.broadcasted_iota(jnp.int32, (128, 32 * nz), 0)
    c = lax.broadcasted_iota(jnp.int32, (128, 32 * nz), 1)
    order = jnp.where(c == (r % 8) * 16 + r // 8, 1.0, 0.0)
    dense = jnp.dot(tile, order, precision=lax.Precision.HIGHEST, preferred_element_type=jnp.float32)
    for f in range(FIELDS):
        coarse_out[f, 0, :, :] = dense[f : f + 1, :]

    drain(len(pending))


def solution(mesh):
    names = mesh.axis_names
    sizes = tuple(mesh.shape[a] for a in names)
    nz = sizes[2]
    f32 = jnp.float32

    def both(*shape):
        return [pltpu.VMEM((2, *shape), f32)] * 2

    scratch = [
        pltpu.VMEM((8, 8, WIDE), jnp.int32),
        pltpu.VMEM((8, 8, WIDE), f32),
        pltpu.VMEM((FIELDS, 8, 8, WIDE), f32),
        pltpu.VMEM((FIELDS, 8, 8, WIDE), f32),
        pltpu.SemaphoreType.DMA((5,)),
        *both(4, 8, WIDE), *both(8, 128),
        *both(4, 8, WIDE), pltpu.VMEM((2, 1, 8, WIDE), f32), *both(3, 8, WIDE), pltpu.VMEM((2, 1, 8, WIDE), f32),
        *both(2, 8, WIDE), *both(8, 128),
        *both(1, 8, WIDE), *both(8, 128),
        pltpu.VMEM((2 * XREACH + 1, 8, WIDE), f32),
        *both(3, 8, WIDE), *both(8, 128),
        *both(2, 8, WIDE), *both(8, 128),
        pltpu.VMEM((2 * YREACH + 1, 8, WIDE * nz), f32),
        pltpu.VMEM((len(HALVES), 8, 128 * nz), f32),
        pltpu.VMEM((8, 128), f32),
        pltpu.SMEM((3,), f32),
    ]
    sems = 2 * 2 * 5 + (2 + 16) + (2 + 8) + 2 * (2 * XREACH + 1) + (2 * YREACH + 1) * nz
    scratch += [pltpu.SemaphoreType.REGULAR((2,)), pltpu.SemaphoreType.DMA((sems,)), pltpu.SemaphoreType.DMA((sems,))]

    def local(phase_label, concentration, phase_factor, potential, source):
        return pl.pallas_call(
            functools.partial(kernel, names, sizes),
            out_shape=(
                jax.ShapeDtypeStruct((FIELDS, 4, 4, 128), f32),
                jax.ShapeDtypeStruct((FIELDS, 1, 1, 32 * nz), f32),
            ),
            in_specs=[pl.BlockSpec(memory_space=pltpu.HBM)] * 5,
            out_specs=(pl.BlockSpec(memory_space=pltpu.VMEM), pl.BlockSpec(memory_space=pltpu.VMEM)),
            scratch_shapes=scratch,
            compiler_params=pltpu.CompilerParams(collective_id=0, has_side_effects=True, vmem_limit_bytes=55168 << 10),
        )(phase_label, concentration, potential, source, phase_factor)

    return jax.shard_map(
        local,
        mesh=mesh,
        in_specs=(P(*names), P(*names), P(), P(None, *names), P(None, *names)),
        out_specs=(P(None, *names), P(None, names[0], names[1], None)),
        check_vma=False,
    )
```

```python
import functools

import jax
import jax.numpy as jnp
from jax import lax
from jax.experimental import pallas as pl
from jax.experimental.pallas import tpu as pltpu
from jax.sharding import PartitionSpec as P

MESH = pl.DeviceIdType.MESH
FIELDS = 3
MASS = 0.05
DAMPING = 0.7
DECAY = 0.3
XREACH = 4
YREACH = 3
WIDE = 256
HALVES = (-3, -2, 2, 3)
XROW = 4


def rs(x, k):
    k %= x.shape[-2]
    return pltpu.roll(x, k, x.ndim - 2) if k else x


def rl(x, k):
    k %= x.shape[-1]
    return pltpu.roll(x, k, x.ndim - 1) if k else x


def harmonic(a, b):
    return 2.0 * a * b / (a + b)


def safe(d):
    return jnp.where(d > 0.0, d, 1.0)


def kernel(names, sizes, phase, conc, pot, src, factors, lev_out, coarse_out, *scratch):
    (ph, co, po, so, in_sem, ys1, yr1, zs1, zr1, xs1, xr1, xk1, xs2, xr2, xk2, ys3, yr3, zs3, zr3, ys4, yr4, zs4, zr4,
     qb, ys6, yr6, zs6, zr6, ys7, yr7, zs7, zr7, gb, gh, hs, factor, row_sem, ssem, rsem) = scratch
    ax, ay, az = names
    nx, ny, nz = sizes
    gx, gy, gz = (lax.axis_index(a) for a in names)
    here = {ax: gx, ay: gy, az: gz}
    count = {ax: nx, ay: ny, az: nz}

    known_steps = {}

    def has(axis, step):
        if (axis, step) not in known_steps:
            at = here[axis] + step
            known_steps[axis, step] = (at >= 0) & (at < count[axis])
        return known_steps[axis, step]

    barrier = pltpu.get_barrier_semaphore()
    place = lax.rem(gx, XROW)
    met = jnp.int32(nz - 1)
    for d in (1, -1, 2, -2, 3, -3):
        known = has(ax, d) & (place + d >= 0) & (place + d < XROW)
        if abs(d) == 1:
            known = has(ax, d)
        met = met + known.astype(jnp.int32)

        @pl.when(known)
        def _(d=d):
            pl.semaphore_signal(barrier, inc=1, device_id={ax: gx + d}, device_id_type=MESH)

    for d in range(-YREACH, YREACH + 1):
        if d:
            met = met + nz * has(ay, d).astype(jnp.int32)

            @pl.when(has(ay, d))
            def _(d=d):
                for rel in range(nz):
                    to = {ay: gy + d, az: lax.rem(gz + rel, nz)}
                    pl.semaphore_signal(barrier, inc=1, device_id=to, device_id_type=MESH)

    for rel in range(1, nz):
        pl.semaphore_signal(barrier, inc=1, device_id={az: lax.rem(gz + rel, nz)}, device_id_type=MESH)

    loads = [pltpu.make_async_copy(a, b, in_sem.at[i]) for i, (a, b) in enumerate(((phase, ph), (conc, co), (factors, factor), (pot, po), (src, so)))]
    for load in loads:
        load.start()

    for axis, bufs in ((ax, (xr1, xr2)), (ay, (yr1, yr3, yr4, yr6, yr7)), (az, (zr1, zr3, zr4, zr6, zr7))):
        for side, d in ((0, -1), (1, 1)):

            @pl.when(jnp.logical_not(has(axis, d)))
            def _(bufs=bufs, side=side):
                for buf in bufs:
                    buf[side] = jnp.zeros(buf.shape[1:], jnp.float32)

    blocks = [(ax, d, qb, XREACH + d) for d in range(-XREACH, XREACH + 1) if d]
    blocks += [(ay, d, gb, YREACH + d) for d in (-1, 1)] + [(ay, d, gh, i) for i, d in enumerate(HALVES)]
    for axis, d, buf, slot in blocks:

        @pl.when(jnp.logical_not(has(axis, d)))
        def _(buf=buf, slot=slot):
            buf[slot] = jnp.zeros(buf.shape[1:], jnp.float32)

    pending = []
    used = [0]

    def fresh(n=1):
        used[0] += n
        return used[0] - n

    def copy(k, a, b, target):
        return pltpu.make_async_remote_copy(
            src_ref=a, dst_ref=b, send_sem=ssem.at[k], recv_sem=rsem.at[k], device_id=target, device_id_type=MESH
        )

    def start(copies, when):
        pending.append((copies, when))

        @pl.when(when)
        def _():
            for c in copies:
                copy(*c).start()

    def arrived(copies, when):
        @pl.when(when)
        def _():
            for k, b in copies:
                copy(k, b, b, {}).wait_recv()

    def drain(n):
        groups = {}
        for copies, when in pending[:n]:
            groups.setdefault(id(when), (when, []))[1].extend(copies)
        for when, copies in groups.values():

            @pl.when(when)
            def _(copies=copies):
                for c in copies:
                    copy(*c).wait_send()

        del pending[:n]

    def push(k, a, b, axis, d):
        start([(k, a, b, {axis: here[axis] + d})], has(axis, d))

    def take(k, b, axis, d):
        arrived([(k, b)], has(axis, d))

    def exchange(axis, sent, got):
        k = fresh(2)
        push(k, sent.at[0], got.at[1], axis, -1)
        push(k + 1, sent.at[1], got.at[0], axis, 1)

        def wait():
            take(k, got.at[1], axis, 1)
            take(k + 1, got.at[0], axis, -1)

        return wait

    class Crossing:
        def __init__(self, sent, got, kept, pieces, lines):
            self.sent, self.got, self.kept, self.pieces, self.lines = sent, got, kept, pieces, lines
            self.whole = fresh(2)
            self.part = fresh(2 * len(pieces))
            self.hop = fresh(2 * len(pieces))
            for side, d in ((0, -1), (1, 1)):
                edge = 0 if side == 0 else XROW - 1
                inside = has(ax, d) & (place != edge)
                leaves = has(ax, d) & (place == edge)
                start([(self.whole + side, sent.at[side], got.at[1 - side], {ax: gx + d})], inside)
                copies = []
                for i, piece in enumerate(pieces):
                    line = lines[side][i]
                    if line == edge:
                        copies.append((self.sem(side, i), sent.at[side, piece], got.at[1 - side, piece], {ax: gx + d}))
                    else:
                        k = self.hop + side * len(pieces) + i
                        copies.append((k, sent.at[side, piece], kept.at[side], {ax: gx + line - edge}))
                start(copies, leaves)

        def sem(self, side, i):
            return self.part + side * len(self.pieces) + i

        def forward(self):
            for side, d in ((0, -1), (1, 1)):
                edge = 0 if side == 0 else XROW - 1
                to = gx - place + edge + d
                exists = (to >= 0) & (to < nx)
                for i, piece in enumerate(self.pieces):
                    line = self.lines[side][i]
                    if line != edge:
                        mine = exists & (place == line)
                        arrived([(self.hop + side * len(self.pieces) + i, self.kept.at[side])], mine)
                        start([(self.sem(side, i), self.kept.at[side], self.got.at[1 - side, piece], {ax: to})], mine)

        def finish(self):
            for side, d in ((0, -1), (1, 1)):
                edge = 0 if side == 0 else XROW - 1
                arrived([(self.whole + 1 - side, self.got.at[side])], has(ax, d) & (place != edge))
                parts = [(self.sem(1 - side, i), self.got.at[side, piece]) for i, piece in enumerate(self.pieces)]
                arrived(parts, has(ax, d) & (place == edge))

    sub = lax.broadcasted_iota(jnp.int32, (8, WIDE), 0)
    lane = lax.broadcasted_iota(jnp.int32, (8, WIDE), 1)
    lane1 = lax.broadcasted_iota(jnp.int32, (8, 128), 1)

    def zpack(sent, slabs, stride, unit):
        low = high = jnp.zeros((8, 128), jnp.float32)
        for k, s in enumerate(slabs):
            mine = (lane1 >= unit * k) & (lane1 < unit * (k + 1))
            low = jnp.where(mine, rl(s[:, :128], unit * k), low)
            high = jnp.where(mine, rl(s[:, 128:], unit * k - (128 - stride)), high)
        sent[0] = low
        sent[1] = high

    def zhalo(low, high, k, stride, unit):
        return jnp.concatenate([rl(low, -unit * k), rl(high, 128 - stride - unit * k)], axis=1)

    def ypack_rows(sent, slabs, stride):
        for g in range(sent.shape[1]):
            low = high = jnp.zeros((8, WIDE), jnp.float32)
            for j, s in enumerate(slabs[8 * g : 8 * g + 8]):
                low = jnp.where(sub == j, rs(s, j), low)
                high = jnp.where(sub == j, rs(s, j - (8 - stride)), high)
            sent[0, g] = low
            sent[1, g] = high

    def row(got, side, k):
        return jnp.broadcast_to(got[side, k // 8, k % 8 : k % 8 + 1, :], (8, WIDE))

    loads[0].wait()
    loads[1].wait()
    loads[2].wait()
    loads[3].wait()
    phase_v = ph[...]
    conc_v = co[...]
    lookup = jnp.zeros(phase_v.shape, jnp.float32)
    for i in range(3):
        lookup = lookup + jnp.where(phase_v == i, factor[i], 0.0)
    conduct = lookup * conc_v * jnp.exp(-DECAY * conc_v)
    fine = [jnp.stack([conduct[x]] + [po[f, x] for f in range(FIELDS)]) for x in range(8)]
    ypack_rows(ys1, [fine[x][a] for a in range(4) for x in range(8)], 1)
    zpack(zs1, [fine[x][a] for a in range(4) for x in range(8)], 1, 1)
    xs1[0] = fine[0]
    xs1[1] = fine[7]
    loads[4].wait()

    pl.semaphore_wait(barrier, met)

    wait_y1 = exchange(ay, ys1, yr1)
    wait_z1 = exchange(az, zs1, zr1)
    slabs = [pl.ds(i, 1) for i in range(4)]
    early = Crossing(xs1, xr1, xk1, slabs, ([0, 1, 2, 3], [0, 1, 2, 3]))

    def rest(c):
        return c[0], c[1:]

    def flux(c, v, other):
        face = harmonic(c, other[0])
        return face, face * (v - other[1:])

    inner = []
    for i in range(3):
        a, b = fine[2 * i + 1], fine[2 * i + 2]
        inner.append(flux(a[0], a[1:], b))

    wait_y1()
    wait_z1()
    early.forward()
    zlow, zhigh = zr1[0], zr1[1]
    part, ypart, zpart = [], [], []
    for x in range(8):
        c, v = rest(fine[x])
        near = jnp.where(sub % 2 == 0, rs(fine[x], 1), rs(fine[x], -1))
        edge = jnp.stack([jnp.where(sub == 0, row(yr1, 0, a * 8 + x), row(yr1, 1, a * 8 + x)) for a in range(4)])
        near = jnp.where((sub == 0) | (sub == 7), edge, near)
        sy, fy = flux(c, v, near)
        near = jnp.where(lane % 2 == 0, rl(fine[x], 1), rl(fine[x], -1))
        edge = jnp.stack([zhalo(zlow, zhigh, a * 8 + x, 1, 1) for a in range(4)])
        near = jnp.where((lane == 0) | (lane == WIDE - 1), edge, near)
        sz, fz = flux(c, v, near)
        source = jnp.stack([so[f, x] for f in range(FIELDS)])
        part.append(source - MASS * v - fy - fz)
        ypart.append(sy)
        zpart.append(sz)

    def fold(t, stride):
        t = t + rl(t, -stride)
        return t + rs(t, -stride)

    mass1 = MASS * 8.0
    r1, ylo, yhi, zlo, zhi, diag, sx = {}, {}, {}, {}, {}, {}, {}
    for i in range(3):
        sx[i] = fold(inner[i][0], 1)
    for i in range(4):
        t = part[2 * i] + part[2 * i + 1]
        if i < 3:
            t = t - inner[i][1]
        if i > 0:
            t = t + inner[i - 1][1]
        r1[i] = fold(t, 1)
        a = ypart[2 * i] + ypart[2 * i + 1]
        a = a + rl(a, -1)
        ylo[i], yhi[i] = a, rs(a, -1)
        b = zpart[2 * i] + zpart[2 * i + 1]
        b = b + rs(b, -1)
        zlo[i], zhi[i] = b, rl(b, -1)
        d = mass1 + ylo[i] + yhi[i] + zlo[i] + zhi[i]
        if i < 3:
            d = d + sx[i]
        if i > 0:
            d = d + sx[i - 1]
        diag[i] = d

    e0, weight = {}, {}
    for i in (1, 2):
        weight[i] = DAMPING / safe(diag[i])
        e0[i] = weight[i] * r1[i]

    q0 = sub % 2 == 0
    p0 = lane % 2 == 0

    def merge4(a, b, c, d):
        return jnp.where(q0, jnp.where(p0, a, rl(b, 1)), jnp.where(p0, rs(c, 1), rs(rl(d, 1), 1)))

    def split4(m):
        low = rs(m, -1)
        return m, rl(m, -1), low, rl(low, -1)

    for side, (edge, next_to, face) in enumerate(((0, 1, 0), (3, 2, 2))):
        xs2[side, 0] = merge4(e0[next_to][0], e0[next_to][1], e0[next_to][2], diag[edge])
        xs2[side, 1] = merge4(r1[edge][0], r1[edge][1], r1[edge][2], sx[face])
        xs2[side, 2] = merge4(ylo[edge], yhi[edge], zlo[edge], zhi[edge])
    late = Crossing(xs2, xr2, xk2, [pl.ds(0, 2), pl.ds(2, 1)], ([0, 1], [XROW - 1, XROW - 2]))
    late.forward()
    early.finish()
    for side, edge in ((0, 0), (1, XROW - 1)):
        step = 1 if side == 0 else -1

        @pl.when((place == edge) & has(ax, -step))
        def _(side=side, step=step):
            for i in range(1, XROW):
                pl.semaphore_signal(row_sem.at[side], inc=1, device_id={ax: gx + step * i}, device_id_type=MESH)

    border = {}
    for side, x in ((0, 0), (1, 7)):
        face, out = flux(fine[x][0], fine[x][1:], xr1[side])
        border[side] = (fold(face, 1), fold(out, 1))
    late.finish()
    for side, edge, out, far, own_face, far_face in ((0, 0, -1, -2, -1, -2), (1, 3, 4, 5, 3, 4)):
        face, through = border[side]
        a = split4(xr2[side, 0])
        b = split4(xr2[side, 1])
        c = split4(xr2[side, 2])
        e0[far] = jnp.stack(a[:3])
        r1[out] = jnp.stack(b[:3]) + through
        r1[edge] = r1[edge] - through
        sx[far_face] = b[3]
        sx[own_face] = face
        ylo[out], yhi[out], zlo[out], zhi[out] = c
        diag[out] = a[3] + face
        diag[edge] = diag[edge] + face
        for i in (out, edge):
            weight[i] = DAMPING / safe(diag[i])
            e0[i] = weight[i] * r1[i]

    def halos(got_y, got_z, layers, low, high, i):
        base = layers.index(i) * FIELDS
        ylow = jnp.stack([rl(row(got_y, 0, k // 2), -(k % 2)) for k in range(base, base + FIELDS)])
        yhigh = jnp.stack([rl(row(got_y, 1, k // 2), -(k % 2)) for k in range(base, base + FIELDS)])
        zedge = jnp.stack([zhalo(low, high, base + f, 2, 1) for f in range(FIELDS)])
        return ylow, yhigh, zedge

    def two_by_two(slabs):
        return [jnp.where(p0, a, rl(b, 1)) for a, b in zip(slabs[::2], slabs[1::2])]

    six = [-1, 0, 1, 2, 3, 4]
    slabs = [e0[i][f] for i in six for f in range(FIELDS)]
    ypack_rows(ys3, two_by_two(slabs), 2)
    wait_y = exchange(ay, ys3, yr3)
    zpack(zs3, slabs, 2, 1)
    wait_z = exchange(az, zs3, zr3)
    wait_y()
    wait_z()
    low, high = zr3[0], zr3[1]
    e1 = {}
    for i in six:
        e = e0[i]
        ylow, yhigh, zedge = halos(yr3, zr3, six, low, high, i)
        total = mass1 * e + sx[i - 1] * (e - e0[i - 1]) + sx[i] * (e - e0[i + 1])
        total = total + ylo[i] * (e - jnp.where(sub < 2, ylow, rs(e, 2)))
        total = total + yhi[i] * (e - jnp.where(sub >= 6, yhigh, rs(e, -2)))
        total = total + zlo[i] * (e - jnp.where(lane < 2, zedge, rl(e, 2)))
        total = total + zhi[i] * (e - jnp.where(lane >= WIDE - 2, zedge, rl(e, -2)))
        e1[i] = e + weight[i] * (r1[i] - total)

    four = [0, 1, 2, 3]
    slabs = [e1[i][f] for i in four for f in range(FIELDS)]
    ypack_rows(ys4, two_by_two(slabs), 2)
    wait_y = exchange(ay, ys4, yr4)
    zpack(zs4, slabs, 2, 1)
    wait_z = exchange(az, zs4, zr4)

    mass2 = mass1 * 8.0
    yfirst = sub % 4 < 2
    zfirst = lane % 4 < 2
    yout = {i: jnp.where(yfirst, ylo[i], yhi[i]) for i in four}
    zout = {i: jnp.where(zfirst, zlo[i], zhi[i]) for i in four}
    sx2 = {-1: fold(sx[-1], 2), 0: fold(sx[1], 2), 1: fold(sx[3], 2)}
    ylo2, yhi2, zlo2, zhi2, diag2 = {}, {}, {}, {}, {}
    for i in range(2):
        a = yout[2 * i] + yout[2 * i + 1]
        a = a + rl(a, -2)
        ylo2[i], yhi2[i] = a, rs(a, -2)
        b = zout[2 * i] + zout[2 * i + 1]
        b = b + rs(b, -2)
        zlo2[i], zhi2[i] = b, rl(b, -2)
        diag2[i] = mass2 + sx2[i - 1] + sx2[i] + ylo2[i] + yhi2[i] + zlo2[i] + zhi2[i]

    wait_y()
    wait_z()
    low, high = zr4[0], zr4[1]
    left = {}
    for i in four:
        e = e1[i]
        ylow, yhigh, zedge = halos(yr4, zr4, four, low, high, i)
        across = i - 1 if i % 2 == 0 else i + 1
        near_y = jnp.where(yfirst, jnp.where(sub < 2, ylow, rs(e, 2)), jnp.where(sub >= 6, yhigh, rs(e, -2)))
        near_z = jnp.where(zfirst, rl(e, 2), rl(e, -2))
        near_z = jnp.where((lane < 2) | (lane >= WIDE - 2), zedge, near_z)
        total = mass1 * e + sx[min(i, across)] * (e - e1[across])
        total = total + yout[i] * (e - near_y) + zout[i] * (e - near_z)
        left[i] = r1[i] - total
    r2 = {i: fold(left[2 * i] + left[2 * i + 1], 2) for i in range(2)}

    q4 = sub % 4
    p4 = lane % 4

    def by(which, a, b, c, d):
        return jnp.where(which < 2, jnp.where(which == 0, a, b), jnp.where(which == 2, c, d))

    def rows4(a, b, c, d):
        return by(q4, a, rs(b, 1), rs(c, 2), rs(d, 3))

    block = by(
        p4,
        rows4(r2[0][0], r2[0][1], r2[0][2], diag2[0]),
        rl(rows4(r2[1][0], r2[1][1], r2[1][2], diag2[1]), 1),
        rl(rows4(sx2[0], yhi2[0], zhi2[0], zlo2[0]), 2),
        rl(rows4(sx2[1], yhi2[1], zhi2[1], zlo2[1]), 3),
    )
    qb[XREACH] = block
    old = len(pending)
    direct = fresh(2 * XREACH + 1)
    for side, edge in ((0, 0), (1, XROW - 1)):

        @pl.when((place != edge) & has(ax, XREACH * (2 * side - 1)))
        def _(side=side):
            pl.semaphore_wait(row_sem.at[side], 1)

    for d in (-XREACH, XREACH, 1, -1, 2, -2, 3, -3):
        inside = has(ax, d) if abs(d) == XREACH else has(ax, d) & (place + d >= 0) & (place + d < XROW)
        start([(direct + XREACH - d, qb.at[XREACH], qb.at[XREACH - d], {ax: gx + d})], inside)

    drain(old)
    packed = jnp.concatenate([merge4(*(e1[i][f] for i in four)) for f in range(FIELDS)], axis=0)
    r = lax.broadcasted_iota(jnp.int32, (WIDE, WIDE), 0)
    c = lax.broadcasted_iota(jnp.int32, (WIDE, WIDE), 1)
    order = jnp.where(c == (r % 2) * 128 + r // 2, 1.0, 0.0)
    dense = jnp.dot(packed, order, precision=lax.Precision.HIGHEST, preferred_element_type=jnp.float32)
    for f in range(FIELDS):
        for y in range(4):
            for q in range(2):
                for p in range(2):
                    k = f * 8 + 2 * y + q
                    lev_out[f, 2 * q + p, y : y + 1, :] = dense[k : k + 1, 128 * p : 128 * p + 128]

    handed = fresh(2 * XREACH + 1)
    for side in (-1, 1):
        far = XREACH + side * XREACH
        take(direct + far, qb.at[far], ax, side * XREACH)
        for step in range(1, XROW):
            slot = far - side * step
            inside = has(ax, side * XREACH) & (place + side * step >= 0) & (place + side * step < XROW)
            start([(handed + slot, qb.at[far], qb.at[slot], {ax: gx + side * step})], inside)
    for side in (-1, 1):
        for step in range(1, XROW):
            slot = XREACH + side * step
            inside = (place + side * step >= 0) & (place + side * step < XROW)
            arrived([(direct + slot, qb.at[slot])], has(ax, side * step) & inside)
            arrived([(handed + slot, qb.at[slot])], has(ax, side * step) & jnp.logical_not(inside))

    n2 = 2 * XREACH + 1
    q = qb[...]

    def spread(x, item):
        return jnp.where(q4 == 0, rs(x, -item), jnp.where(q4 == 1, rs(x, 1 - item), rs(x, 2 - item)))

    layer0 = p4 == 0
    weight2 = DAMPING / safe(spread(q, 3))
    coef = rl(q, -2)
    xhi, yhi_, zhi_, zlo_ = (spread(coef, item) for item in range(4))
    e = weight2 * q

    def below(x):
        return jnp.concatenate([x[:1], x[:-1]], axis=0)

    def above(x):
        return jnp.concatenate([x[1:], x[-1:]], axis=0)

    def next_x(x):
        return jnp.where(layer0, rl(x, -1), above(rl(x, 1)))

    def last_x(x):
        return jnp.where(layer0, below(rl(x, -1)), rl(x, 1))

    def ypack_halves(sent, x):
        low, high = [], []
        for m in range(0, x.shape[0], 2):
            a, b = x[m], x[min(m + 1, x.shape[0] - 1)]
            low.append(jnp.where(sub < 4, a, rs(b, 4)))
            high.append(jnp.where(sub < 4, rs(a, 4), b))
        for side, h in ((0, low), (1, high)):
            for g in range(sent.shape[1]):
                sent[side, g] = jnp.where(p4 < 2, h[2 * g], rl(h[min(2 * g + 1, len(h) - 1)], 2))

    def yedges(got, n):
        out = []
        for d in range(n):
            low, high = (rl(got[side, d // 4], -2 * (d // 2 % 2)) for side in (0, 1))
            if d % 2 == 0:
                out.append(jnp.where(sub < 4, low, rs(high, 4)))
            else:
                out.append(jnp.where(sub < 4, rs(low, 4), high))
        return jnp.stack(out)

    def zedges(got, n):
        low, high = got[0], got[1]
        return jnp.stack([zhalo(low, high, d, 4, 4) for d in range(n)])

    ypack_halves(ys6, jnp.where(q4 == 3, rs(coef, 2), e))
    wait_y = exchange(ay, ys6, yr6)
    zpack(zs6, [e[d] for d in range(n2)], 4, 4)
    wait_z = exchange(az, zs6, zr6)
    xlo = last_x(xhi)
    near = xlo * (e - last_x(e)) + xhi * (e - next_x(e)) + mass2 * e
    wait_y()
    wait_z()
    edge = yedges(yr6, n2)
    zedge = zedges(zr6, n2)
    ylo_ = jnp.where(sub < 4, spread(edge, 3), rs(yhi_, 4))
    other = rs(e, 4)
    total = near + ylo_ * (e - jnp.where(sub < 4, edge, other)) + yhi_ * (e - jnp.where(sub < 4, other, edge))
    total = total + zlo_ * (e - jnp.where(lane < 4, zedge, rl(e, 4)))
    total = total + zhi_ * (e - jnp.where(lane >= WIDE - 4, zedge, rl(e, -4)))
    e = e + weight2 * (q - total)

    n3 = n2 - 2
    ypack_halves(ys7, e[1:-1])
    wait_y = exchange(ay, ys7, yr7)
    zpack(zs7, [e[d] for d in range(1, n2 - 1)], 4, 4)
    wait_z = exchange(az, zs7, zr7)

    mass3 = mass2 * 8.0
    zfirst = lane % 8 < 4
    xout = jnp.where(layer0, xlo, xhi)[1:-1]
    yout = jnp.where(sub < 4, ylo_, yhi_)[1:-1]
    zout = jnp.where(zfirst, zlo_, zhi_)[1:-1]
    a = xout + rs(xout, 4)
    a = a + rl(a, -4)
    xlo3, xhi3 = a, rl(a, -1)
    a = yout + rl(yout, -1)
    a = a + rl(a, -4)
    ylo3, yhi3 = a, rs(a, 4)
    a = zout + rl(zout, -1)
    a = a + rs(a, 4)
    zlo3, zhi3 = a, rl(a, -4)
    diag3 = mass3 + xlo3 + xhi3 + ylo3 + yhi3 + zlo3 + zhi3
    near_x = jnp.where(layer0, last_x(e), next_x(e))[1:-1]
    e = e[1:-1]
    near_z = jnp.where(zfirst, rl(e, 4), rl(e, -4))
    partial = q[1:-1] - mass2 * e - xout * (e - near_x)
    coefs = jnp.where(sub == 3, rs(diag3, 3), jnp.where(sub == 4, rs(xhi3, 4), jnp.where(sub == 5, rs(yhi3, 5), rs(zhi3, 6))))
    wait_y()
    wait_z()
    edge = yedges(yr7, n3)
    zedge = zedges(zr7, n3)
    near_z = jnp.where((lane < 4) | (lane >= WIDE - 4), zedge, near_z)
    t = partial - yout * (e - edge) - zout * (e - near_z)
    t = t + rl(t, -1)
    t = t + rs(t, 4)
    t = t + rl(t, -4)
    t = jnp.where(sub < 3, t, coefs)
    block = jnp.zeros((8, WIDE), jnp.float32)
    for l in range(n3):
        block = jnp.where((lane % 8 == l) & (sub < 7), rl(t[l], l), block)

    def column(slot, at):
        return gb.at[slot, :, pl.ds(pl.multiple_of(at * WIDE, WIDE), WIDE)]

    def half(slot, at):
        return gh.at[slot, :, pl.ds(pl.multiple_of(at * 128, 128), 128)]

    gb[YREACH, :, pl.ds(pl.multiple_of(gz * WIDE, WIDE), WIDE)] = block
    third = lane1 % 8
    hs[...] = jnp.where(third < 3, rl(block[:, :128], -2), jnp.where(third < 6, rl(block[:, 128:], 1), 0.0))
    first = fresh((2 * YREACH + 1) * nz)
    old = len(pending)
    order3 = [(d, [rel for rel in (2, 1, 3, 0) if rel < nz and (d or rel)]) for d in (3, -3, 2, -2, 1, -1, 0)]
    order3 = [(d, rels) for d, rels in order3 if rels]

    def place3(d, at):
        return half(HALVES.index(d), at) if d in HALVES else column(YREACH + d, at)

    def sem3(d, rel):
        return first + (YREACH - d) * nz + rel

    for d, rels in order3:
        source = hs if d in HALVES else column(YREACH, gz)
        to = [{ay: gy + d, az: lax.rem(gz + rel, nz)} for rel in rels]
        start([(sem3(d, rel), source, place3(-d, gz), t) for rel, t in zip(rels, to)], has(ay, d))
    drain(old)
    for d, rels in reversed(order3):
        arrived([(sem3(d, rel), place3(-d, lax.rem(gz + nz - rel, nz))) for rel in rels], has(ay, -d))
    middle = (third >= 2) & (third < 5)
    for i, d in enumerate(HALVES):
        for at in range(nz):
            m = gh[i, :, 128 * at : 128 * at + 128]
            gb[YREACH + d, :, WIDE * at : WIDE * at + 128] = jnp.where(middle, rl(m, 2), 0.0)
            gb[YREACH + d, :, WIDE * at + 128 : WIDE * at + 256] = jnp.where(middle, rl(m, -1), 0.0)

    full = (8, WIDE * nz)
    n = 2 * YREACH + 1

    def coefficient(j, item):
        return jnp.broadcast_to(gb[j, item : item + 1, :], full)

    r3 = [gb[j] for j in range(n)]
    w3 = [DAMPING / safe(coefficient(j, 3)) for j in range(n)]
    e = {j: w3[j] * r3[j] for j in range(n)}
    xhi = {j: coefficient(j, 4) for j in range(1, n - 1)}
    yhi = {j: coefficient(j, 5) for j in range(n - 1)}
    zhi = {j: coefficient(j, 6) for j in range(1, n - 1)}
    xlo = {j: rl(xhi[j], 1) for j in xhi}
    zlo = {j: rl(zhi[j], 8) for j in zhi}
    for sweep in range(1, YREACH + 1):
        new = {}
        for j in range(sweep, n - sweep):
            v = e[j]
            total = mass3 * v + xlo[j] * (v - rl(v, 1)) + xhi[j] * (v - rl(v, -1))
            total = total + yhi[j - 1] * (v - e[j - 1]) + yhi[j] * (v - e[j + 1])
            total = total + zlo[j] * (v - rl(v, 8)) + zhi[j] * (v - rl(v, -8))
            new[j] = v + w3[j] * (r3[j] - total)
        e = new
    own = e[YREACH]
    tile = jnp.zeros((8, 128), jnp.float32)
    for t in range(2 * nz):
        tile = jnp.where(lane1 % 8 == t, rl(own[:, 128 * t : 128 * t + 128], t - XREACH + 1), tile)
    r = lax.broadcasted_iota(jnp.int32, (128, 32 * nz), 0)
    c = lax.broadcasted_iota(jnp.int32, (128, 32 * nz), 1)
    order = jnp.where(c == (r % 8) * 16 + r // 8, 1.0, 0.0)
    dense = jnp.dot(tile, order, precision=lax.Precision.HIGHEST, preferred_element_type=jnp.float32)
    for f in range(FIELDS):
        coarse_out[f, 0, :, :] = dense[f : f + 1, :]

    drain(len(pending))


def solution(mesh):
    names = mesh.axis_names
    sizes = tuple(mesh.shape[a] for a in names)
    nz = sizes[2]
    f32 = jnp.float32

    def both(*shape):
        return [pltpu.VMEM((2, *shape), f32)] * 2

    scratch = [
        pltpu.VMEM((8, 8, WIDE), jnp.int32),
        pltpu.VMEM((8, 8, WIDE), f32),
        pltpu.VMEM((FIELDS, 8, 8, WIDE), f32),
        pltpu.VMEM((FIELDS, 8, 8, WIDE), f32),
        pltpu.SemaphoreType.DMA((5,)),
        *both(4, 8, WIDE), *both(8, 128),
        *both(4, 8, WIDE), pltpu.VMEM((2, 1, 8, WIDE), f32), *both(3, 8, WIDE), pltpu.VMEM((2, 1, 8, WIDE), f32),
        *both(2, 8, WIDE), *both(8, 128),
        *both(1, 8, WIDE), *both(8, 128),
        pltpu.VMEM((2 * XREACH + 1, 8, WIDE), f32),
        *both(3, 8, WIDE), *both(8, 128),
        *both(2, 8, WIDE), *both(8, 128),
        pltpu.VMEM((2 * YREACH + 1, 8, WIDE * nz), f32),
        pltpu.VMEM((len(HALVES), 8, 128 * nz), f32),
        pltpu.VMEM((8, 128), f32),
        pltpu.SMEM((3,), f32),
    ]
    sems = 2 * 2 * 5 + (2 + 16) + (2 + 8) + 2 * (2 * XREACH + 1) + (2 * YREACH + 1) * nz
    scratch += [pltpu.SemaphoreType.REGULAR((2,)), pltpu.SemaphoreType.DMA((sems,)), pltpu.SemaphoreType.DMA((sems,))]

    def local(phase_label, concentration, phase_factor, potential, source):
        return pl.pallas_call(
            functools.partial(kernel, names, sizes),
            out_shape=(
                jax.ShapeDtypeStruct((FIELDS, 4, 4, 128), f32),
                jax.ShapeDtypeStruct((FIELDS, 1, 1, 32 * nz), f32),
            ),
            in_specs=[pl.BlockSpec(memory_space=pltpu.HBM)] * 5,
            out_specs=(pl.BlockSpec(memory_space=pltpu.VMEM), pl.BlockSpec(memory_space=pltpu.VMEM)),
            scratch_shapes=scratch,
            compiler_params=pltpu.CompilerParams(collective_id=0, has_side_effects=True, vmem_limit_bytes=55168 << 10),
        )(phase_label, concentration, potential, source, phase_factor)

    return jax.shard_map(
        local,
        mesh=mesh,
        in_specs=(P(*names), P(*names), P(), P(None, *names), P(None, *names)),
        out_specs=(P(None, *names), P(None, names[0], names[1], None)),
        check_vma=False,
    )
```
